32 devices in a mesh: replica: 2 (over x), shard: 16 (over z, y, core).
Axes of the slice: x: 2, y: 2, z: 4, core: 2. Of those that a mesh axis runs over, the one named last changes fastest.
Arguments:
- tokens: bfloat16 [5120, 1024], P(('replica', 'shard')), may hold values from -6 to 6
- segments: int32 [5120], P(('replica', 'shard')), may hold values from 0 to 9, as said below
- counts: int32 [32], P(('replica', 'shard')), may hold values from 80 to 160, as said below
- ln1_gain: bfloat16 [1024], P('shard'), may hold values from 0.5 to 1.5
- ln1_bias: bfloat16 [1024], P('shard'), may hold values from -3 to 3
- w_qkv: bfloat16 [1024, 3072], P('shard'), may hold values from -0.1875 to 0.1875
- bias_query: bfloat16 [1024], P('shard'), may hold values from -3 to 3
- bias_value: bfloat16 [1024], P('shard'), may hold values from -3 to 3
- w_proj: bfloat16 [1024, 1024], P('shard'), may hold values from -0.75 to 0.75
- bias_proj: bfloat16 [1024], P('shard'), may hold values from -3 to 3
- ln2_gain: bfloat16 [1024], P('shard'), may hold values from 0.5 to 1.5
- ln2_bias: bfloat16 [1024], P('shard'), may hold values from -3 to 3
- w_fc: bfloat16 [1024, 4096], P('shard'), may hold values from -0.1875 to 0.1875
- bias_fc: bfloat16 [4096], P('shard'), may hold values from -3 to 3
- w_out: bfloat16 [4096, 1024], P('shard'), may hold values from -0.09375 to 0.09375
- bias_out: bfloat16 [1024], P('shard'), may hold values from -3 to 3
- cotangent: bfloat16 [5120, 1024], P(('replica', 'shard')), may hold values from -6 to 6
Outputs:
- mixed: bfloat16 [5120, 1024], P(('replica', 'shard'))
- grad_tokens: float32 [5120, 1024], P(('replica', 'shard'))
- grad_ln1_gain: float32 [1024], P('shard')
- grad_ln1_bias: float32 [1024], P('shard')
- grad_w_qkv: float32 [1024, 3072], P('shard')
- grad_bias_query: float32 [1024], P('shard')
- grad_bias_value: float32 [1024], P('shard')
- grad_w_proj: float32 [1024, 1024], P('shard')
- grad_bias_proj: float32 [1024], P('shard')
- grad_ln2_gain: float32 [1024], P('shard')
- grad_ln2_bias: float32 [1024], P('shard')
- grad_w_fc: float32 [1024, 4096], P('shard')
- grad_bias_fc: float32 [4096], P('shard')
- grad_w_out: float32 [4096, 1024], P('shard')
- grad_bias_out: float32 [1024], P('shard')
The draws below stay inside these ranges and needn't reach their ends.
Inputs may be any that keep to these rules, and one draw needn't show every extreme that they name: `counts`: in every draw one device has all 160 slots in use. `segments`: on each device the ids start at 0 on its first row, never fall and rise by at most one a row; slots at or beyond the device's count repeat the id of its last slot in use.
All inputs are finite; a program needn't handle non-finite values.
Results may differ from the reference program's by a relative error of at most 0.019.
Values may be sent and summed in bfloat16 or wider, within the bound.
No kernel may reach another device: no remote copies, remote signals or barrier semaphores. Data moves between devices by JAX's collectives and lax.ppermute only.
A program may use at most 128 MiB of HBM per device.

```python
import jax
import jax.numpy as jnp
from jax import lax

D = 1024
HEADS = 16
HEAD_DIM = 64
FF = 4096
TOK_DEV = 160
TOKENS = 5120
N_REPLICA = 2
N_SHARD = 16


def layout(key):
    device_count = N_REPLICA * N_SHARD
    most_id = max(1, TOK_DEV // 16 - 1)
    spacing = TOK_DEV // (most_id + 1)
    key_count, key_full, key_break = jax.random.split(key, 3)
    used = jax.random.randint(key_count, (device_count,), TOK_DEV // 2, TOK_DEV + 1)
    fullest = jax.random.randint(key_full, (), 0, device_count)
    is_full = jnp.arange(device_count) == fullest
    used = jnp.where(is_full, TOK_DEV, used).astype(jnp.int32)
    position = jnp.arange(TOK_DEV, dtype=jnp.int32)[None, :]
    starts = (jax.random.randint(key_break, (device_count, TOK_DEV), 0, max(4, TOK_DEV // 4)) == 0) & (position > 0)
    regular = (position % spacing == 0) & (position > 0)
    starts = jnp.where(is_full[:, None], regular, starts)
    segment_ids = jnp.minimum(jnp.cumsum(starts.astype(jnp.int32), axis=1), most_id)
    last_id = jnp.take_along_axis(segment_ids, (used - 1)[:, None], axis=1)
    segment_ids = jnp.where(position < used[:, None], segment_ids, last_id)
    return (used, segment_ids.reshape(-1).astype(jnp.int32))


def draw_counts(key, part):
    return layout(key)[0]


def draw_segments(key, part):
    return layout(key)[1]


def levels(own_key, extent, shards, least, largest):
    gain = 1.0
    for dim, blocks in shards:
        heights = jax.random.uniform(jax.random.fold_in(jax.random.fold_in(own_key, 6), dim), (blocks,), jnp.float32, least / len(shards), largest / len(shards))
        gain = gain * jnp.repeat(jnp.exp(heights), extent[dim] // blocks).reshape((-1,) + (1,) * (len(extent) - 1 - dim))
    return gain


def scatter_about(stream_key, extent, scale, most, shards=(), held_as=jnp.bfloat16):
    gain = levels(stream_key, extent, shards, -0.22, 0.18) if shards else 1.0
    entries = jax.random.normal(stream_key, extent, jnp.float32) * scale * gain
    return jnp.minimum(jnp.maximum(entries, -most), most).astype(held_as)


def setup_inputs(seed: int = 0) -> dict:
    key_list = jax.random.split(jax.random.key(seed), 18)
    return {
        "tokens": scatter_about(key_list[0], (TOKENS, D), 1.0, 6.0, ((0, 32),)),
        "segments": draw_segments(jax.random.fold_in(key_list[17], 71), 0),
        "counts": draw_counts(jax.random.fold_in(key_list[17], 71), 0),
        "ln1_gain": jnp.clip(1.0 + 0.1 * jax.random.normal(key_list[3], (D,), jnp.float32), 0.5, 1.5).astype(jnp.bfloat16),
        "ln1_bias": scatter_about(key_list[4], (D,), 0.5, 3.0, ((0, 16),)),
        "w_qkv": scatter_about(key_list[5], (D, 3 * D), D ** -0.5, 0.1875, ((0, 16),)),
        "bias_query": scatter_about(key_list[6], (D,), 0.5, 3.0, ((0, 16),)),
        "bias_value": scatter_about(key_list[7], (D,), 0.5, 3.0, ((0, 16),)),
        "w_proj": scatter_about(key_list[8], (D, D), (D // 16) ** -0.5, 0.75, ((0, 16),)),
        "bias_proj": scatter_about(key_list[9], (D,), 0.5, 3.0, ((0, 16),)),
        "ln2_gain": jnp.clip(1.0 + 0.1 * jax.random.normal(key_list[10], (D,), jnp.float32), 0.5, 1.5).astype(jnp.bfloat16),
        "ln2_bias": scatter_about(key_list[11], (D,), 0.5, 3.0, ((0, 16),)),
        "w_fc": scatter_about(key_list[12], (D, FF), D ** -0.5, 0.1875, ((0, 16),)),
        "bias_fc": scatter_about(key_list[13], (FF,), 0.5, 3.0, ((0, 16),)),
        "w_out": scatter_about(key_list[14], (FF, D), FF ** -0.5, 0.09375, ((0, 16),)),
        "bias_out": scatter_about(key_list[15], (D,), 0.5, 3.0, ((0, 16),)),
        "cotangent": scatter_about(key_list[16], (TOKENS, D), 1.0, 6.0, ((0, 32),)),
    }


@jax.custom_vjp
def low(v):
    return lax.optimization_barrier(v.astype(jnp.bfloat16)).astype(jnp.float32)

@jax.custom_vjp
def low_back(v):
    return v

def low_keep(v):
    return (low(v), None)

def low_pass(kept, grad):
    return (grad,)

def back_keep(v):
    return (v, None)

def back_low(kept, grad):
    return (low(grad),)
low.defvjp(low_keep, low_pass)
low_back.defvjp(back_keep, back_low)
HIGHEST = lax.Precision.HIGHEST

def layer_norm(values, gain_full, shift_full):
    center = values - lax.optimization_barrier(jnp.mean(values, axis=-1, keepdims=True))
    spread = lax.optimization_barrier(jnp.mean(center * center, axis=-1, keepdims=True))
    return center * lax.rsqrt(spread + 1e-05) * gain_full + shift_full

def layer(params, stream, seg_block, count_block):
    gain_one, shift_one, qkv_weight, query_shift, value_shift, proj_weight, proj_shift, gain_two, shift_two, fc_weight, fc_shift, out_weight, out_shift = params
    row_count = stream.shape[1]
    position = jnp.arange(row_count, dtype=jnp.int32)
    in_use = (position[None, :] < count_block[:, None]).astype(jnp.float32)
    visible = (seg_block[:, :, None] == seg_block[:, None, :]) & (position[None, None, :] <= position[None, :, None]) & (position[None, None, :] < count_block[:, None, None])
    normed_one = low(layer_norm(stream, gain_one, shift_one))
    qkv_shift = jnp.concatenate([query_shift, jnp.zeros_like(query_shift), value_shift])
    raw_qkv = jnp.einsum('gtd,de->gte', normed_one, qkv_weight, precision=HIGHEST) + qkv_shift
    qkv_rows = low(low_back(raw_qkv))
    split_shape = stream.shape[:2] + (HEADS, HEAD_DIM)
    queries = qkv_rows[..., :D].reshape(split_shape)
    keys_rows = qkv_rows[..., D:2 * D].reshape(split_shape)
    values_rows = qkv_rows[..., 2 * D:].reshape(split_shape)
    scores = low_back(HEAD_DIM ** (-0.5) * jnp.einsum('gqhd,gkhd->ghqk', queries, keys_rows, precision=HIGHEST))
    scores = jnp.where(visible[:, None], scores, -1e+30)
    weights = low(jax.nn.softmax(scores, axis=-1))
    context = jnp.einsum('ghqk,gkhd->gqhd', weights, values_rows, precision=HIGHEST).reshape(stream.shape)
    context = low(low_back(context))
    branch_one = low_back(jnp.einsum('gtd,de->gte', context, proj_weight, precision=HIGHEST) + proj_shift)
    middle = stream + branch_one
    normed_two = low(layer_norm(middle, gain_two, shift_two))
    pre_act = low_back(jnp.einsum('gtd,df->gtf', normed_two, fc_weight, precision=HIGHEST) + fc_shift)
    hidden = low(jax.nn.gelu(pre_act, approximate=True))
    branch_two = low_back(jnp.einsum('gtf,fd->gtd', hidden, out_weight, precision=HIGHEST) + out_shift)
    return in_use[..., None] * (middle + branch_two)

def reference(tokens, segments, counts, ln1_gain, ln1_bias, w_qkv, bias_query, bias_value, w_proj, bias_proj, ln2_gain, ln2_bias, w_fc, bias_fc, w_out, bias_out, cotangent):
    params = tuple((item.astype(jnp.float32) for item in (ln1_gain, ln1_bias, w_qkv, bias_query, bias_value, w_proj, bias_proj, ln2_gain, ln2_bias, w_fc, bias_fc, w_out, bias_out)))
    device_count = N_REPLICA * N_SHARD
    stream = tokens.astype(jnp.float32).reshape(device_count, 1, TOK_DEV, D)
    seg_all = segments.reshape(device_count, 1, TOK_DEV)
    count_all = counts.reshape(device_count, 1)

    def forward(params_in, stream_in):

        def one_device(item):
            device_params = tuple((low_back(entry) for entry in params_in))
            return layer(device_params, item[0], item[1], item[2])
        return lax.map(jax.checkpoint(one_device), (stream_in, seg_all, count_all))
    output, pullback = jax.vjp(forward, params, stream)
    grads, grad_stream = pullback(cotangent.astype(jnp.float32).reshape(stream.shape))
    mixed = output.reshape(TOKENS, D).astype(jnp.bfloat16)
    return (mixed, grad_stream.reshape(TOKENS, D), grads[0], grads[1], grads[2], grads[3], grads[4], grads[5], grads[6], grads[7], grads[8], grads[9], grads[10], grads[11], grads[12])
```

```python
import jax
import jax.numpy as jnp
from jax import lax
from jax.sharding import PartitionSpec as P

HEADS = 16
RANKS = 4
MESH_AXES = ("replica", "shard")
BF16 = jnp.bfloat16
F32 = jnp.float32
SMALL_ROWS = 16


def layer_norm(values, gain, shift):
    center = values - jnp.mean(values, axis=-1, keepdims=True)
    spread = jnp.mean(center * center, axis=-1, keepdims=True)
    return center * lax.rsqrt(spread + 1e-05) * gain + shift


def unit_norm(values):
    center = values - jnp.mean(values, axis=-1, keepdims=True)
    spread = jnp.mean(center * center, axis=-1, keepdims=True)
    return center * lax.rsqrt(spread + 1e-05)


def smooth_gate(values):
    return jax.nn.gelu(values, approximate=True)


def dot_rows(left, right):
    return lax.dot_general(left, right, (((0,), (0,)), ((), ())), preferred_element_type=F32)


def dot_cols(left, right):
    return lax.dot_general(left, right, (((1,), (1,)), ((), ())), preferred_element_type=F32)


def dot(left, right):
    return jnp.dot(left, right, preferred_element_type=F32)


def make_local(n_replica, n_shard):
    n_pos = n_shard // 2
    half = n_pos // 2
    head_a_shard = n_shard == HEADS
    n_pairs = n_replica // 2
    pair_groups = [[2 * i + j for i in range(n_pairs)] for j in range(2)]

    def every(move):
        pairs = []
        for r in range(n_replica):
            for p in range(n_pos):
                for c in range(2):
                    to = move(r, p, c)
                    if to is not None:
                        pairs.append((r * n_shard + p * 2 + c, to[0] * n_shard + to[1] * 2 + to[2]))
        return pairs

    ring = list(range(0, n_pos, 2)) + list(range(n_pos - 1, 0, -2))
    after = {p: ring[(i + 1) % n_pos] for i, p in enumerate(ring)}
    before = {p: ring[i - 1] for i, p in enumerate(ring)}
    core_pairs = every(lambda r, p, c: (r, p, 1 - c))
    copy_pairs = every(lambda r, p, c: (r ^ 1, p, c))
    next_pairs = every(lambda r, p, c: (r, after[p], c))
    back_pairs = every(lambda r, p, c: (r, before[p], c))
    lend_pairs = every(lambda r, p, c: (r, p ^ 1, c) if p % 2 == r % 2 else None)
    give_pairs = every(lambda r, p, c: (r, p ^ 1, c) if p % 2 != r % 2 else None)
    share_pairs = every(lambda r, p, c: (r ^ 1, p, c) if p % 2 == r % 2 else None)

    def to_core(v):
        return lax.ppermute(v, MESH_AXES, core_pairs)

    def to_copy(v):
        return lax.ppermute(v, MESH_AXES, copy_pairs)

    def to_next(v):
        return lax.ppermute(v, MESH_AXES, next_pairs)

    def to_back(v):
        return lax.ppermute(v, MESH_AXES, back_pairs)

    def cut(rows):
        return max(16, rows // 32 * 16)

    def ring_gather(chunk, place, origin):
        low = cut(chunk.shape[0])
        full = jnp.zeros((n_pos,) + chunk.shape, chunk.dtype)

        def put(full, value, offset, row=0):
            return lax.dynamic_update_slice(full, value[None], (origin(place + offset), row, 0))

        full = put(full, chunk, 0)
        forth = back = chunk
        for step in range(1, half):
            forth = to_next(forth)
            back = to_back(back)
            full = put(full, forth, -step)
            full = put(full, back, step)
        forth = to_next(forth[:low])
        back = to_back(back[low:])
        full = put(full, forth, half)
        full = put(full, back, half, low)
        return full

    def ring_scatter(full, place, origin):
        low = cut(full.shape[1])

        def term(offset):
            return lax.dynamic_index_in_dim(full, origin(place + offset), 0, keepdims=False)

        def add(left, right):
            return (left.astype(F32) + right.astype(F32)).astype(BF16)

        far = term(half)
        forth = to_next(far[:low])
        back = to_back(far[low:])
        ahead = term(half - 1)
        behind = term(1 - half)
        forth = to_next(jnp.concatenate([add(forth, ahead[:low]), ahead[low:]]))
        back = to_back(jnp.concatenate([behind[:low], add(back, behind[low:])]))
        for step in range(half - 2, 0, -1):
            forth = to_next(add(forth, term(step)))
            back = to_back(add(back, term(-step)))
        return term(0).astype(F32) + forth.astype(F32) + back.astype(F32)

    def group_gather(block):
        other = to_copy(block)
        return jnp.stack([block, to_core(block), other, to_core(other)])

    def group_scatter(parts):
        near = to_core(jnp.stack([parts[1], parts[3]]).astype(BF16)).astype(F32)
        away = to_copy((parts[2] + near[1]).astype(BF16)).astype(F32)
        return parts[0] + near[0] + away

    def local(
        tokens,
        segments,
        counts,
        ln1_gain,
        ln1_bias,
        w_qkv,
        bias_query,
        bias_value,
        w_proj,
        bias_proj,
        ln2_gain,
        ln2_bias,
        w_fc,
        bias_fc,
        w_out,
        bias_out,
        cotangent,
    ):
        row_count, width = tokens.shape
        head_width = width // HEADS
        own_rows = width // n_shard
        chip_rows = 2 * own_rows
        own_hidden = w_out.shape[0]
        piece = own_hidden // 2
        groups = HEADS // RANKS
        scale = head_width ** (-0.5)
        replica_at = lax.axis_index("replica")
        shard_at = lax.axis_index("shard")
        x = replica_at % 2
        c = shard_at % 2
        p = shard_at // 2
        rank = 2 * x + c
        place = jnp.where(p % 2 == 0, p // 2, n_pos - 1 - p // 2)

        def origin(index):
            index = index % n_pos
            return jnp.where(index < half, 2 * index, 2 * (n_pos - 1 - index) + 1)

        def by_core(mine, other):
            return jnp.where(c == 0, jnp.stack([mine, other]), jnp.stack([other, mine]))

        position = jnp.arange(row_count, dtype=jnp.int32)
        in_use = (position < counts[0]).astype(F32)
        notes = jnp.stack([segments.astype(BF16), in_use.astype(BF16)])
        notes = jnp.pad(notes, ((0, SMALL_ROWS - 2), (0, width - row_count)))
        seen = group_gather(jnp.concatenate([tokens, notes]))
        tokens_all = seen[:, :row_count].reshape(RANKS * row_count, width)
        seg_all = seen[:, row_count, :row_count]
        use_all = seen[:, row_count + 1, :row_count]

        def qkv_part(which):
            view = w_qkv.reshape(own_rows, 3, groups, RANKS, head_width)
            return lax.dynamic_index_in_dim(view, which, 3, keepdims=False).reshape(own_rows, -1)

        def fc_part(core):
            view = w_fc.reshape(own_rows, n_pos, 4, piece)
            part = lax.dynamic_index_in_dim(view, 2 * core + x, 2, keepdims=False)
            return part.reshape(own_rows, -1)

        vectors = [ln1_gain, ln1_bias, bias_query, bias_value, bias_proj, ln2_gain, ln2_bias, bias_out, bias_fc]
        starts = [0]
        for vector in vectors:
            starts.append(starts[-1] + vector.shape[0])
        n_small = starts[-1]
        qkv_width = 3 * groups * head_width
        small = jnp.concatenate(vectors)[None]
        small = jnp.pad(small, ((0, SMALL_ROWS - 1), (0, 0)))
        both_small = by_core(small[0], to_core(small)[0])
        qkv_chunk = by_core(qkv_part(rank), to_core(qkv_part(rank ^ 1))).reshape(chip_rows, qkv_width)
        if head_a_shard:
            lent = lax.ppermute(w_proj[:, width // 2 :], MESH_AXES, lend_pairs)
            proj_half = jnp.where(p % 2 == x, w_proj[:, : width // 2], lent)
            proj_chunk = jnp.concatenate([proj_half[:, : width // 4], proj_half[:, width // 4 :]])
        else:
            proj_chunk = jnp.zeros((chip_rows, width // 4), BF16)
        small_chunk = jnp.pad(both_small, ((0, SMALL_ROWS - 2), (0, width - n_small)))
        first_chunk = jnp.concatenate(
            [jnp.concatenate([qkv_chunk, proj_chunk], axis=1), small_chunk]
        )
        fc_chunk = by_core(fc_part(c), to_core(fc_part(1 - c))).reshape(chip_rows, n_pos * piece)
        out_chunk = lax.dynamic_slice_in_dim(w_out, x * piece, piece, 0)

        first_full = ring_gather(first_chunk, place, origin)
        fc_weight = ring_gather(fc_chunk, place, origin).reshape(width, n_pos * piece)
        out_weight = ring_gather(out_chunk, place, origin).reshape(n_pos * piece, width)

        qkv_weight = first_full[:, :chip_rows, :qkv_width].reshape(width, qkv_width)
        if head_a_shard:
            proj_full = first_full[:, :chip_rows, qkv_width:].reshape(
                n_pos // 2, 2, 2, own_rows, width // 4
            )
            proj_full = jnp.where(x == 0, proj_full, proj_full[:, ::-1])
            proj_weight = proj_full.transpose(0, 3, 1, 2, 4).reshape(groups * head_width, width)
        else:
            proj_full = lax.all_gather(w_proj, "shard", axis=0, tiled=True)
            proj_full = proj_full.reshape(groups, RANKS, head_width, width)
            proj_weight = lax.dynamic_index_in_dim(proj_full, rank, 1, keepdims=False)
            proj_weight = proj_weight.reshape(groups * head_width, width)
        smalls = first_full[:, chip_rows : chip_rows + 2, :n_small].reshape(n_shard, n_small)
        params = [
            smalls[:, starts[i] : starts[i + 1]].reshape(-1).astype(F32) for i in range(len(vectors))
        ]
        gain_one, shift_one, query_shift, value_shift, proj_shift, gain_two, shift_two, out_shift, fc_shift = params

        def rank_heads(vector):
            view = vector.reshape(groups, RANKS, head_width)
            return lax.dynamic_index_in_dim(view, rank, 1, keepdims=False).reshape(-1)

        fc_shift = lax.dynamic_index_in_dim(
            fc_shift.reshape(n_pos, 4, piece), 2 * c + x, 1, keepdims=False
        ).reshape(-1)
        qkv_shift = jnp.concatenate(
            [
                rank_heads(query_shift),
                jnp.zeros((groups * head_width,), F32),
                rank_heads(value_shift),
            ]
        )

        unit_one = unit_norm(tokens_all.astype(F32))
        input_one = (unit_one * gain_one + shift_one).astype(BF16)
        qkv_rows = (dot(input_one, qkv_weight) + qkv_shift).astype(BF16)
        qkv_view = qkv_rows.reshape(RANKS, row_count, 3, groups, head_width)
        queries, keys_rows, values_rows = qkv_view[:, :, 0], qkv_view[:, :, 1], qkv_view[:, :, 2]
        visible = (
            (seg_all[:, :, None] == seg_all[:, None, :])
            & (position[None, None, :] <= position[None, :, None])
            & (use_all[:, None, :] > 0)
        )[:, None]
        scores = scale * jnp.einsum("bqhd,bkhd->bhqk", queries, keys_rows, preferred_element_type=F32)
        scores = jnp.where(visible, scores, -1e30)
        top_score = jnp.max(scores, axis=-1, keepdims=True)
        expo = jnp.exp(scores - top_score)
        probs = expo / jnp.sum(expo, axis=-1, keepdims=True)
        probs_low = probs.astype(BF16)
        context = (
            jnp.einsum("bhqk,bkhd->bqhd", probs_low, values_rows, preferred_element_type=F32)
            .reshape(RANKS * row_count, groups * head_width)
            .astype(BF16)
        )
        block_shape = (RANKS, row_count, width)
        stream = tokens.astype(F32)
        middle = stream + proj_shift + group_scatter(dot(context, proj_weight).reshape(block_shape))

        normed_two, norm_two_back = jax.vjp(layer_norm, middle, gain_two, shift_two)
        input_two = group_gather(normed_two.astype(BF16)).reshape(RANKS * row_count, width)
        pre_act = dot(input_two, fc_weight) + fc_shift
        gate_value, gate_back = jax.vjp(smooth_gate, pre_act)
        hidden = gate_value.astype(BF16)
        branch_two = group_scatter(dot(hidden, out_weight).reshape(block_shape)) + out_shift
        mixed = (in_use[:, None] * (middle + branch_two)).astype(BF16)

        d_top = in_use[:, None] * cotangent.astype(F32)
        d_out = group_gather(d_top.astype(BF16)).reshape(RANKS * row_count, width)
        grad_w_out = dot_rows(hidden, d_out).astype(BF16).reshape(n_pos, piece, width)
        d_pre = gate_back(dot_cols(d_out, out_weight))[0].astype(BF16)
        grad_w_fc = dot_rows(input_two, d_pre).astype(BF16).reshape(n_pos, chip_rows, n_pos * piece)
        d_input_two = group_scatter(dot_cols(d_pre, fc_weight).reshape(block_shape))
        d_mid_norm, grad_gain_two, grad_shift_two = norm_two_back(d_input_two)
        d_middle = d_top + d_mid_norm
        own_w_out = ring_scatter(grad_w_out, place, origin)
        own_w_fc = ring_scatter(grad_w_fc, place, origin)

        d_branch = group_gather(d_middle.astype(BF16)).reshape(RANKS * row_count, width)
        grad_w_proj = dot_rows(context, d_branch)
        d_context = (
            dot_cols(d_branch, proj_weight)
            .astype(BF16)
            .reshape(RANKS, row_count, groups, head_width)
        )
        d_values = jnp.einsum("bhqk,bqhd->bkhd", probs_low, d_context, preferred_element_type=F32)
        d_probs = jnp.einsum("bqhd,bkhd->bhqk", d_context, values_rows, preferred_element_type=F32)
        d_scores = (
            probs * (d_probs - jnp.sum(probs * d_probs, axis=-1, keepdims=True))
        ).astype(BF16)
        d_queries = scale * jnp.einsum(
            "bhqk,bkhd->bqhd", d_scores, keys_rows, preferred_element_type=F32
        )
        d_keys = scale * jnp.einsum("bhqk,bqhd->bkhd", d_scores, queries, preferred_element_type=F32)
        d_qkv = (
            jnp.stack([d_queries, d_keys, d_values], axis=2)
            .reshape(RANKS * row_count, qkv_width)
            .astype(BF16)
        )
        grad_w_qkv = dot_rows(input_one, d_qkv).astype(BF16).reshape(n_pos, chip_rows, qkv_width)
        d_input_one = dot_cols(d_qkv, qkv_weight)
        grad_gain_one = jnp.sum(d_input_one * unit_one, axis=0)
        grad_shift_one = jnp.sum(d_input_one, axis=0)
        d_qkv_sums = jnp.sum(d_qkv.astype(F32), axis=0)

        def own_term(values):
            return jnp.sum(values.astype(BF16).astype(F32), axis=0)

        def at_rank(sums):
            view = sums.reshape(groups, 1, head_width)
            mine = jnp.arange(RANKS)[None, :, None] == rank
            return jnp.where(mine, view, 0.0).reshape(-1)

        fc_sums = jnp.sum(d_pre.astype(F32), axis=0).reshape(n_pos, 1, piece)
        fc_sums = jnp.where(jnp.arange(4)[None, :, None] == 2 * c + x, fc_sums, 0.0).reshape(-1)
        small_terms = [
            grad_gain_one,
            grad_shift_one,
            at_rank(d_qkv_sums[: groups * head_width]),
            at_rank(d_qkv_sums[2 * groups * head_width :]),
            own_term(d_middle),
            grad_gain_two,
            grad_shift_two,
            own_term(d_top),
            fc_sums,
        ]
        small_terms = jnp.concatenate(
            [term.reshape(n_shard, -1) for term in small_terms], axis=1
        ).astype(BF16)
        small_terms = jnp.pad(
            small_terms.reshape(n_pos, 2, n_small),
            ((0, 0), (0, SMALL_ROWS - 2), (0, width - n_small)),
        )
        if head_a_shard:
            proj_terms = grad_w_proj.astype(BF16).reshape(n_pos // 2, own_rows, 2, 2, width // 4)
            proj_terms = proj_terms.transpose(0, 2, 3, 1, 4)
            proj_terms = jnp.where(x == 0, proj_terms, proj_terms[:, ::-1])
            proj_terms = proj_terms.reshape(n_pos, chip_rows, width // 4)
        else:
            proj_terms = jnp.zeros((n_pos, chip_rows, width // 4), BF16)
        first_terms = jnp.concatenate(
            [jnp.concatenate([grad_w_qkv, proj_terms], axis=2), small_terms], axis=1
        )
        own_first = ring_scatter(first_terms, place, origin)
        d_in_norm = jax.vjp(unit_norm, stream)[1](
            group_scatter(d_input_one.reshape(block_shape)) * gain_one
        )[0]
        grad_tokens = d_middle + d_in_norm

        def rows_of(chunk, core):
            return lax.dynamic_slice_in_dim(chunk, core * own_rows, own_rows, 0)

        def by_copy(mine, other):
            return jnp.where(x == 0, jnp.stack([mine, other]), jnp.stack([other, mine]))

        own_w_out = own_w_out.astype(BF16)
        grad_w_out = by_copy(own_w_out, to_copy(own_w_out)).reshape(own_hidden, width)

        own_w_fc = own_w_fc.astype(BF16)
        fc_rows = by_core(rows_of(own_w_fc, c), to_core(rows_of(own_w_fc, 1 - c)))
        fc_rows = by_copy(fc_rows, to_copy(fc_rows))
        fc_rows = fc_rows.reshape(2, 2, own_rows, n_pos, piece)
        grad_w_fc = fc_rows.transpose(2, 3, 1, 0, 4).reshape(own_rows, -1)

        own_first = own_first.astype(BF16)
        own_qkv = own_first[:chip_rows, :qkv_width]
        qkv_grad = by_core(rows_of(own_qkv, c), to_core(rows_of(own_qkv, 1 - c)))
        qkv_grad = by_copy(qkv_grad, to_copy(qkv_grad))
        qkv_grad = qkv_grad.reshape(2, 2, own_rows, 3, groups, head_width)
        grad_w_qkv = qkv_grad.transpose(2, 3, 4, 0, 1, 5).reshape(own_rows, -1)

        own_small = own_first[chip_rows:, :n_small]
        near_small = to_core(own_small)
        small_sum = jnp.where(
            c == 0,
            own_small[0].astype(F32) + near_small[0].astype(F32),
            own_small[1].astype(F32) + near_small[1].astype(F32),
        )
        small_send = jnp.pad(small_sum[None].astype(BF16), ((0, SMALL_ROWS - 1), (0, 0)))
        small_sum = small_sum + to_copy(small_send)[0].astype(F32)

        if head_a_shard:
            own_proj = own_first[:chip_rows, qkv_width:]
            given = lax.ppermute(own_proj, MESH_AXES, give_pairs)
            proj_rows = jnp.stack([own_proj, given]).reshape(2, 2, own_rows, width // 4)
            proj_rows = proj_rows.transpose(2, 0, 1, 3).reshape(own_rows, width)
            shared = lax.ppermute(proj_rows, MESH_AXES, share_pairs)
            grad_w_proj = jnp.where(p % 2 == x, proj_rows, shared)
        else:
            proj_rows = grad_w_proj.astype(BF16).reshape(groups, 1, head_width, width)
            mine = jnp.arange(RANKS)[None, :, None, None] == rank
            proj_rows = jnp.where(mine, proj_rows, 0).reshape(width, width)
            proj_rows = lax.psum_scatter(proj_rows, "shard", scatter_dimension=0, tiled=True)
            grad_w_proj = proj_rows.astype(F32) + to_copy(proj_rows).astype(F32)

        if n_pairs > 1:
            grad_w_out, grad_w_fc, grad_w_qkv, grad_w_proj, small_sum = lax.psum(
                tuple(
                    value.astype(BF16)
                    for value in (grad_w_out, grad_w_fc, grad_w_qkv, grad_w_proj, small_sum)
                ),
                "replica",
                axis_index_groups=pair_groups,
            )
        small_sum = small_sum.astype(F32)
        small_grads = [small_sum[starts[i] : starts[i + 1]] for i in range(len(vectors))]
        g_gain_one, g_shift_one, g_query, g_value, g_proj, g_gain_two, g_shift_two, g_out, g_fc = small_grads
        return (
            mixed,
            grad_tokens,
            g_gain_one,
            g_shift_one,
            grad_w_qkv.astype(F32),
            g_query,
            g_value,
            grad_w_proj.astype(F32),
            g_proj,
            g_gain_two,
            g_shift_two,
            grad_w_fc.astype(F32),
            g_fc,
            grad_w_out.astype(F32),
            g_out,
        )

    return local


def solution(mesh):
    tokens_spec = P(MESH_AXES, None)
    slots_spec = P(MESH_AXES)
    rows_spec = P("shard", None)
    vector_spec = P("shard")
    in_specs = (
        tokens_spec,
        slots_spec,
        slots_spec,
        vector_spec,
        vector_spec,
        rows_spec,
        vector_spec,
        vector_spec,
        rows_spec,
        vector_spec,
        vector_spec,
        vector_spec,
        rows_spec,
        vector_spec,
        rows_spec,
        vector_spec,
        tokens_spec,
    )
    out_specs = (
        tokens_spec,
        tokens_spec,
        vector_spec,
        vector_spec,
        rows_spec,
        vector_spec,
        vector_spec,
        rows_spec,
        vector_spec,
        vector_spec,
        vector_spec,
        rows_spec,
        vector_spec,
        rows_spec,
        vector_spec,
    )
    local = make_local(mesh.shape["replica"], mesh.shape["shard"])
    return jax.shard_map(local, mesh=mesh, in_specs=in_specs, out_specs=out_specs, check_vma=False)
```

```python
import functools

import jax
import jax.numpy as jnp
from jax import lax
from jax.experimental import pallas as pl
from jax.experimental.pallas import tpu as pltpu
from jax.sharding import PartitionSpec as P

HEADS = 16
RANKS = 4
MESH_AXES = ("replica", "shard")
BF16 = jnp.bfloat16
F32 = jnp.float32
SMALL_ROWS = 16


def layer_norm(values, gain, shift):
    center = values - jnp.mean(values, axis=-1, keepdims=True)
    spread = jnp.mean(center * center, axis=-1, keepdims=True)
    return center * lax.rsqrt(spread + 1e-05) * gain + shift


def unit_norm(values):
    center = values - jnp.mean(values, axis=-1, keepdims=True)
    spread = jnp.mean(center * center, axis=-1, keepdims=True)
    return center * lax.rsqrt(spread + 1e-05)


def smooth_gate(values):
    return jax.nn.gelu(values, approximate=True)


def dot_rows(left, right):
    return lax.dot_general(left, right, (((0,), (0,)), ((), ())), preferred_element_type=F32)


def dot_cols(left, right):
    return lax.dot_general(left, right, (((1,), (1,)), ((), ())), preferred_element_type=F32)


def dot(left, right):
    return jnp.dot(left, right, preferred_element_type=F32)


def make_local(n_replica, n_shard):
    n_pos = n_shard // 2
    half = n_pos // 2
    head_a_shard = n_shard == HEADS
    n_pairs = n_replica // 2
    pair_groups = [[2 * i + j for i in range(n_pairs)] for j in range(2)]

    def every(move):
        pairs = []
        for r in range(n_replica):
            for p in range(n_pos):
                for c in range(2):
                    to = move(r, p, c)
                    if to is not None:
                        pairs.append((r * n_shard + p * 2 + c, to[0] * n_shard + to[1] * 2 + to[2]))
        return pairs

    ring = list(range(0, n_pos, 2)) + list(range(n_pos - 1, 0, -2))
    after = {p: ring[(i + 1) % n_pos] for i, p in enumerate(ring)}
    before = {p: ring[i - 1] for i, p in enumerate(ring)}
    core_pairs = every(lambda r, p, c: (r, p, 1 - c))
    copy_pairs = every(lambda r, p, c: (r ^ 1, p, c))
    next_pairs = every(lambda r, p, c: (r, after[p], c))
    back_pairs = every(lambda r, p, c: (r, before[p], c))
    lend_pairs = every(lambda r, p, c: (r, p ^ 1, c) if p % 2 == r % 2 else None)
    give_pairs = every(lambda r, p, c: (r, p ^ 1, c) if p % 2 != r % 2 else None)
    share_pairs = every(lambda r, p, c: (r ^ 1, p, c) if p % 2 == r % 2 else None)

    def to_core(v):
        return lax.ppermute(v, MESH_AXES, core_pairs)

    def to_copy(v):
        return lax.ppermute(v, MESH_AXES, copy_pairs)

    def to_next(v):
        return lax.ppermute(v, MESH_AXES, next_pairs)

    def to_back(v):
        return lax.ppermute(v, MESH_AXES, back_pairs)

    def cut(rows):
        return max(16, rows // 32 * 16)

    def ring_gather(chunk, place, origin):
        low = cut(chunk.shape[0])
        full = jnp.zeros((n_pos,) + chunk.shape, chunk.dtype)

        def put(full, value, offset, row=0):
            return lax.dynamic_update_slice(full, value[None], (origin(place + offset), row, 0))

        full = put(full, chunk, 0)
        forth = back = chunk
        for step in range(1, half):
            forth = to_next(forth)
            back = to_back(back)
            full = put(full, forth, -step)
            full = put(full, back, step)
        forth = to_next(forth[:low])
        back = to_back(back[low:])
        full = put(full, forth, half)
        full = put(full, back, half, low)
        return full

    def ring_scatter(full, place, origin):
        low = cut(full.shape[1])

        def term(offset):
            return lax.dynamic_index_in_dim(full, origin(place + offset), 0, keepdims=False)

        def add(left, right):
            return (left.astype(F32) + right.astype(F32)).astype(BF16)

        far = term(half)
        forth = to_next(far[:low])
        back = to_back(far[low:])
        ahead = term(half - 1)
        behind = term(1 - half)
        forth = to_next(jnp.concatenate([add(forth, ahead[:low]), ahead[low:]]))
        back = to_back(jnp.concatenate([behind[:low], add(back, behind[low:])]))
        for step in range(half - 2, 0, -1):
            forth = to_next(add(forth, term(step)))
            back = to_back(add(back, term(-step)))
        return term(0).astype(F32) + forth.astype(F32) + back.astype(F32)

    def group_gather(block):
        other = to_copy(block)
        return jnp.stack([block, to_core(block), other, to_core(other)])

    def group_scatter(parts):
        near = to_core(jnp.stack([parts[1], parts[3]]).astype(BF16)).astype(F32)
        away = to_copy((parts[2] + near[1]).astype(BF16)).astype(F32)
        return parts[0] + near[0] + away

    def local(
        tokens,
        segments,
        counts,
        ln1_gain,
        ln1_bias,
        w_qkv,
        bias_query,
        bias_value,
        w_proj,
        bias_proj,
        ln2_gain,
        ln2_bias,
        w_fc,
        bias_fc,
        w_out,
        bias_out,
        cotangent,
    ):
        row_count, width = tokens.shape
        head_width = width // HEADS
        own_rows = width // n_shard
        chip_rows = 2 * own_rows
        own_hidden = w_out.shape[0]
        piece = own_hidden // 2
        groups = HEADS // RANKS
        scale = head_width ** (-0.5)
        replica_at = lax.axis_index("replica")
        shard_at = lax.axis_index("shard")
        x = replica_at % 2
        c = shard_at % 2
        p = shard_at // 2
        rank = 2 * x + c
        place = jnp.where(p % 2 == 0, p // 2, n_pos - 1 - p // 2)

        def origin(index):
            index = index % n_pos
            return jnp.where(index < half, 2 * index, 2 * (n_pos - 1 - index) + 1)

        def by_core(mine, other):
            return jnp.where(c == 0, jnp.stack([mine, other]), jnp.stack([other, mine]))

        position = jnp.arange(row_count, dtype=jnp.int32)
        in_use = (position < counts[0]).astype(F32)
        notes = jnp.stack([segments.astype(BF16), in_use.astype(BF16)])
        notes = jnp.pad(notes, ((0, SMALL_ROWS - 2), (0, width - row_count)))
        seen = group_gather(jnp.concatenate([tokens, notes]))
        tokens_all = seen[:, :row_count].reshape(RANKS * row_count, width)
        seg_all = seen[:, row_count, :row_count]
        use_all = seen[:, row_count + 1, :row_count]

        def qkv_part(which):
            view = w_qkv.reshape(own_rows, 3, groups, RANKS, head_width)
            return lax.dynamic_index_in_dim(view, which, 3, keepdims=False).reshape(own_rows, -1)

        def fc_part(core):
            view = w_fc.reshape(own_rows, n_pos, 4, piece)
            part = lax.dynamic_index_in_dim(view, 2 * core + x, 2, keepdims=False)
            return part.reshape(own_rows, -1)

        vectors = [ln1_gain, ln1_bias, bias_query, bias_value, bias_proj, ln2_gain, ln2_bias, bias_out, bias_fc]
        starts = [0]
        for vector in vectors:
            starts.append(starts[-1] + vector.shape[0])
        n_small = starts[-1]
        qkv_width = 3 * groups * head_width
        small = jnp.concatenate(vectors)[None]
        small = jnp.pad(small, ((0, SMALL_ROWS - 1), (0, 0)))
        both_small = by_core(small[0], to_core(small)[0])
        qkv_chunk = by_core(qkv_part(rank), to_core(qkv_part(rank ^ 1))).reshape(chip_rows, qkv_width)
        if head_a_shard:
            lent = lax.ppermute(w_proj[:, width // 2 :], MESH_AXES, lend_pairs)
            proj_half = jnp.where(p % 2 == x, w_proj[:, : width // 2], lent)
            proj_chunk = jnp.concatenate([proj_half[:, : width // 4], proj_half[:, width // 4 :]])
        else:
            proj_chunk = jnp.zeros((chip_rows, width // 4), BF16)
        small_chunk = jnp.pad(both_small, ((0, SMALL_ROWS - 2), (0, width - n_small)))
        first_chunk = jnp.concatenate(
            [jnp.concatenate([qkv_chunk, proj_chunk], axis=1), small_chunk]
        )
        fc_chunk = by_core(fc_part(c), to_core(fc_part(1 - c))).reshape(chip_rows, n_pos * piece)
        out_chunk = lax.dynamic_slice_in_dim(w_out, x * piece, piece, 0)

        first_full = ring_gather(first_chunk, place, origin)
        fc_weight = ring_gather(fc_chunk, place, origin).reshape(width, n_pos * piece)
        out_weight = ring_gather(out_chunk, place, origin).reshape(n_pos * piece, width)

        qkv_weight = first_full[:, :chip_rows, :qkv_width].reshape(width, qkv_width)
        if head_a_shard:
            proj_full = first_full[:, :chip_rows, qkv_width:].reshape(
                n_pos // 2, 2, 2, own_rows, width // 4
            )
            proj_full = jnp.where(x == 0, proj_full, proj_full[:, ::-1])
            proj_weight = proj_full.transpose(0, 3, 1, 2, 4).reshape(groups * head_width, width)
        else:
            proj_full = lax.all_gather(w_proj, "shard", axis=0, tiled=True)
            proj_full = proj_full.reshape(groups, RANKS, head_width, width)
            proj_weight = lax.dynamic_index_in_dim(proj_full, rank, 1, keepdims=False)
            proj_weight = proj_weight.reshape(groups * head_width, width)
        smalls = first_full[:, chip_rows : chip_rows + 2, :n_small].reshape(n_shard, n_small)
        params = [
            smalls[:, starts[i] : starts[i + 1]].reshape(-1).astype(F32) for i in range(len(vectors))
        ]
        gain_one, shift_one, query_shift, value_shift, proj_shift, gain_two, shift_two, out_shift, fc_shift = params

        def rank_heads(vector):
            view = vector.reshape(groups, RANKS, head_width)
            return lax.dynamic_index_in_dim(view, rank, 1, keepdims=False).reshape(-1)

        fc_shift = lax.dynamic_index_in_dim(
            fc_shift.reshape(n_pos, 4, piece), 2 * c + x, 1, keepdims=False
        ).reshape(-1)
        qkv_shift = jnp.concatenate(
            [
                rank_heads(query_shift),
                jnp.zeros((groups * head_width,), F32),
                rank_heads(value_shift),
            ]
        )

        unit_one = unit_norm(tokens_all.astype(F32))
        input_one = (unit_one * gain_one + shift_one).astype(BF16)
        qkv_rows = (dot(input_one, qkv_weight) + qkv_shift).astype(BF16)
        qkv_view = qkv_rows.reshape(RANKS, row_count, 3, groups, head_width)
        queries, keys_rows, values_rows = qkv_view[:, :, 0], qkv_view[:, :, 1], qkv_view[:, :, 2]
        visible = (
            (seg_all[:, :, None] == seg_all[:, None, :])
            & (position[None, None, :] <= position[None, :, None])
            & (use_all[:, None, :] > 0)
        )[:, None]
        scores = scale * jnp.einsum("bqhd,bkhd->bhqk", queries, keys_rows, preferred_element_type=F32)
        scores = jnp.where(visible, scores, -1e30)
        top_score = jnp.max(scores, axis=-1, keepdims=True)
        expo = jnp.exp(scores - top_score)
        probs = expo / jnp.sum(expo, axis=-1, keepdims=True)
        probs_low = probs.astype(BF16)
        context = (
            jnp.einsum("bhqk,bkhd->bqhd", probs_low, values_rows, preferred_element_type=F32)
            .reshape(RANKS * row_count, groups * head_width)
            .astype(BF16)
        )
        block_shape = (RANKS, row_count, width)
        stream = tokens.astype(F32)
        middle = stream + proj_shift + group_scatter(dot(context, proj_weight).reshape(block_shape))

        normed_two, norm_two_back = jax.vjp(layer_norm, middle, gain_two, shift_two)
        input_two = group_gather(normed_two.astype(BF16)).reshape(RANKS * row_count, width)
        pre_act = dot(input_two, fc_weight) + fc_shift
        gate_value, gate_back = jax.vjp(smooth_gate, pre_act)
        hidden = gate_value.astype(BF16)
        branch_two = group_scatter(dot(hidden, out_weight).reshape(block_shape)) + out_shift
        mixed = (in_use[:, None] * (middle + branch_two)).astype(BF16)

        d_top = in_use[:, None] * cotangent.astype(F32)
        d_out = group_gather(d_top.astype(BF16)).reshape(RANKS * row_count, width)
        grad_w_out = dot_rows(hidden, d_out).astype(BF16).reshape(n_pos, piece, width)
        d_pre = gate_back(dot_cols(d_out, out_weight))[0].astype(BF16)
        grad_w_fc = dot_rows(input_two, d_pre).astype(BF16).reshape(n_pos, chip_rows, n_pos * piece)
        d_input_two = group_scatter(dot_cols(d_pre, fc_weight).reshape(block_shape))
        d_mid_norm, grad_gain_two, grad_shift_two = norm_two_back(d_input_two)
        d_middle = d_top + d_mid_norm
        own_w_out = ring_scatter(grad_w_out, place, origin)
        own_w_fc = ring_scatter(grad_w_fc, place, origin)

        d_branch = group_gather(d_middle.astype(BF16)).reshape(RANKS * row_count, width)
        grad_w_proj = dot_rows(context, d_branch)
        d_context = (
            dot_cols(d_branch, proj_weight)
            .astype(BF16)
            .reshape(RANKS, row_count, groups, head_width)
        )
        d_values = jnp.einsum("bhqk,bqhd->bkhd", probs_low, d_context, preferred_element_type=F32)
        d_probs = jnp.einsum("bqhd,bkhd->bhqk", d_context, values_rows, preferred_element_type=F32)
        d_scores = (
            probs * (d_probs - jnp.sum(probs * d_probs, axis=-1, keepdims=True))
        ).astype(BF16)
        d_queries = scale * jnp.einsum(
            "bhqk,bkhd->bqhd", d_scores, keys_rows, preferred_element_type=F32
        )
        d_keys = scale * jnp.einsum("bhqk,bqhd->bkhd", d_scores, queries, preferred_element_type=F32)
        d_qkv = (
            jnp.stack([d_queries, d_keys, d_values], axis=2)
            .reshape(RANKS * row_count, qkv_width)
            .astype(BF16)
        )
        grad_w_qkv = dot_rows(input_one, d_qkv).astype(BF16).reshape(n_pos, chip_rows, qkv_width)
        d_input_one = dot_cols(d_qkv, qkv_weight)
        grad_gain_one = jnp.sum(d_input_one * unit_one, axis=0)
        grad_shift_one = jnp.sum(d_input_one, axis=0)
        d_qkv_sums = jnp.sum(d_qkv.astype(F32), axis=0)

        def own_term(values):
            return jnp.sum(values.astype(BF16).astype(F32), axis=0)

        def at_rank(sums):
            view = sums.reshape(groups, 1, head_width)
            mine = jnp.arange(RANKS)[None, :, None] == rank
            return jnp.where(mine, view, 0.0).reshape(-1)

        fc_sums = jnp.sum(d_pre.astype(F32), axis=0).reshape(n_pos, 1, piece)
        fc_sums = jnp.where(jnp.arange(4)[None, :, None] == 2 * c + x, fc_sums, 0.0).reshape(-1)
        small_terms = [
            grad_gain_one,
            grad_shift_one,
            at_rank(d_qkv_sums[: groups * head_width]),
            at_rank(d_qkv_sums[2 * groups * head_width :]),
            own_term(d_middle),
            grad_gain_two,
            grad_shift_two,
            own_term(d_top),
            fc_sums,
        ]
        small_terms = jnp.concatenate(
            [term.reshape(n_shard, -1) for term in small_terms], axis=1
        ).astype(BF16)
        small_terms = jnp.pad(
            small_terms.reshape(n_pos, 2, n_small),
            ((0, 0), (0, SMALL_ROWS - 2), (0, width - n_small)),
        )
        if head_a_shard:
            proj_terms = grad_w_proj.astype(BF16).reshape(n_pos // 2, own_rows, 2, 2, width // 4)
            proj_terms = proj_terms.transpose(0, 2, 3, 1, 4)
            proj_terms = jnp.where(x == 0, proj_terms, proj_terms[:, ::-1])
            proj_terms = proj_terms.reshape(n_pos, chip_rows, width // 4)
        else:
            proj_terms = jnp.zeros((n_pos, chip_rows, width // 4), BF16)
        first_terms = jnp.concatenate(
            [jnp.concatenate([grad_w_qkv, proj_terms], axis=2), small_terms], axis=1
        )
        own_first = ring_scatter(first_terms, place, origin)
        d_in_norm = jax.vjp(unit_norm, stream)[1](
            group_scatter(d_input_one.reshape(block_shape)) * gain_one
        )[0]
        grad_tokens = d_middle + d_in_norm

        def rows_of(chunk, core):
            return lax.dynamic_slice_in_dim(chunk, core * own_rows, own_rows, 0)

        def by_copy(mine, other):
            return jnp.where(x == 0, jnp.stack([mine, other]), jnp.stack([other, mine]))

        own_w_out = own_w_out.astype(BF16)
        grad_w_out = by_copy(own_w_out, to_copy(own_w_out)).reshape(own_hidden, width)

        own_w_fc = own_w_fc.astype(BF16)
        fc_rows = by_core(rows_of(own_w_fc, c), to_core(rows_of(own_w_fc, 1 - c)))
        fc_rows = by_copy(fc_rows, to_copy(fc_rows))
        fc_rows = fc_rows.reshape(2, 2, own_rows, n_pos, piece)
        grad_w_fc = fc_rows.transpose(2, 3, 1, 0, 4).reshape(own_rows, -1)

        own_first = own_first.astype(BF16)
        own_qkv = own_first[:chip_rows, :qkv_width]
        qkv_grad = by_core(rows_of(own_qkv, c), to_core(rows_of(own_qkv, 1 - c)))
        qkv_grad = by_copy(qkv_grad, to_copy(qkv_grad))
        qkv_grad = qkv_grad.reshape(2, 2, own_rows, 3, groups, head_width)
        grad_w_qkv = qkv_grad.transpose(2, 3, 4, 0, 1, 5).reshape(own_rows, -1)

        own_small = own_first[chip_rows:, :n_small]
        near_small = to_core(own_small)
        small_sum = jnp.where(
            c == 0,
            own_small[0].astype(F32) + near_small[0].astype(F32),
            own_small[1].astype(F32) + near_small[1].astype(F32),
        )
        small_send = jnp.pad(small_sum[None].astype(BF16), ((0, SMALL_ROWS - 1), (0, 0)))
        small_sum = small_sum + to_copy(small_send)[0].astype(F32)

        if head_a_shard:
            own_proj = own_first[:chip_rows, qkv_width:]
            given = lax.ppermute(own_proj, MESH_AXES, give_pairs)
            proj_rows = jnp.stack([own_proj, given]).reshape(2, 2, own_rows, width // 4)
            proj_rows = proj_rows.transpose(2, 0, 1, 3).reshape(own_rows, width)
            shared = lax.ppermute(proj_rows, MESH_AXES, share_pairs)
            grad_w_proj = jnp.where(p % 2 == x, proj_rows, shared)
        else:
            proj_rows = grad_w_proj.astype(BF16).reshape(groups, 1, head_width, width)
            mine = jnp.arange(RANKS)[None, :, None, None] == rank
            proj_rows = jnp.where(mine, proj_rows, 0).reshape(width, width)
            proj_rows = lax.psum_scatter(proj_rows, "shard", scatter_dimension=0, tiled=True)
            grad_w_proj = proj_rows.astype(F32) + to_copy(proj_rows).astype(F32)

        if n_pairs > 1:
            grad_w_out, grad_w_fc, grad_w_qkv, grad_w_proj, small_sum = lax.psum(
                tuple(
                    value.astype(BF16)
                    for value in (grad_w_out, grad_w_fc, grad_w_qkv, grad_w_proj, small_sum)
                ),
                "replica",
                axis_index_groups=pair_groups,
            )
        small_sum = small_sum.astype(F32)
        small_grads = [small_sum[starts[i] : starts[i + 1]] for i in range(len(vectors))]
        g_gain_one, g_shift_one, g_query, g_value, g_proj, g_gain_two, g_shift_two, g_out, g_fc = small_grads
        return (
            mixed,
            grad_tokens,
            g_gain_one,
            g_shift_one,
            grad_w_qkv.astype(F32),
            g_query,
            g_value,
            grad_w_proj.astype(F32),
            g_proj,
            g_gain_two,
            g_shift_two,
            grad_w_fc.astype(F32),
            g_fc,
            grad_w_out.astype(F32),
            g_out,
        )

    return local

LANES = 128
HALF = 64
VMEM_BYTES = 56 * 1024 * 1024
ORIGINS = 9
AT_X, AT_C, AT_Y, AT_COUNT = 9, 10, 11, 12
VMEM_SPEC = pl.BlockSpec(memory_space=pltpu.VMEM)
SMEM_SPEC = pl.BlockSpec(memory_space=pltpu.SMEM)
ANY_SPEC = pl.BlockSpec(memory_space=pl.ANY)


def kernel_call(body, in_specs, outs, scratch=(), flops=0, moved=4 << 20):
    return pl.pallas_call(
        body,
        out_shape=tuple(jax.ShapeDtypeStruct(shape, dtype) for shape, dtype in outs),
        in_specs=list(in_specs),
        out_specs=tuple(VMEM_SPEC for _ in outs),
        scratch_shapes=list(scratch),
        compiler_params=pltpu.CompilerParams(vmem_limit_bytes=VMEM_BYTES),
        cost_estimate=pl.CostEstimate(flops=flops, bytes_accessed=moved, transcendentals=0),
    )


def low_half(shape):
    return lax.broadcasted_iota(jnp.int32, shape, len(shape) - 1) < HALF


def turn(values):
    return jnp.concatenate([values[:, HALF:], values[:, :HALF]], axis=1)


def join(c, first, second, low):
    even = jnp.where(low, first, turn(second))
    odd = jnp.where(low, turn(first), second)
    return jnp.where(c == 0, even, odd)


def statistics(values):
    center = values - jnp.mean(values, axis=-1, keepdims=True)
    spread = jnp.mean(center * center, axis=-1, keepdims=True)
    return center, lax.rsqrt(spread + 1e-05)


def norm_back(unit, inverse, d_unit):
    along = jnp.mean(d_unit * unit, axis=-1, keepdims=True)
    return inverse * (d_unit - jnp.mean(d_unit, axis=-1, keepdims=True) - unit * along)


def used_rows(info, rows):
    return (lax.broadcasted_iota(jnp.int32, (rows, 1), 0) < info[AT_COUNT]).astype(F32)


def prepare_body(info, tokens, notes, cotangent, w_qkv, w_fc, vectors, fc_shift, seen, d_out, sent, own):
    rows, width = tokens.shape
    own_rows = w_qkv.shape[0]
    x, c = info[AT_X], info[AT_C]
    seen[:rows, :] = tokens[...]
    seen[rows:, :] = notes[...]
    d_out[...] = (used_rows(info, rows) * cotangent[...].astype(F32)).astype(BF16)
    low = low_half((own_rows, LANES))
    for out in (sent, own):
        core = c if out is own else 1 - c
        for pair in range(w_qkv.shape[1] // (8 * HALF)):
            at = pair * 8 * HALF + x * LANES
            first = w_qkv[:, pl.ds(pl.multiple_of(at, LANES), LANES)].astype(F32)
            second = w_qkv[:, pl.ds(pl.multiple_of(at + 4 * HALF, LANES), LANES)].astype(F32)
            out[:own_rows, pair * LANES : (pair + 1) * LANES] = join(core, first, second, low).astype(BF16)
        for p in range(w_fc.shape[1] // (4 * LANES)):
            at = pl.multiple_of(p * 4 * LANES + (2 * core + x) * LANES, LANES)
            out[own_rows : 2 * own_rows, p * LANES : (p + 1) * LANES] = w_fc[:, pl.ds(at, LANES)]
        out[:own_rows, 3 * width // 4 :] = jnp.zeros((own_rows, width // 4), BF16)
        out[2 * own_rows :, :] = jnp.zeros((SMALL_ROWS, width), BF16)
        shifts = fc_shift[...].astype(F32)
        shift = jnp.broadcast_to(jnp.where(x == 0, shifts[0:1], shifts[1:2]), (8, LANES))
        rest = vectors[...].astype(F32)
        rest = jnp.where(lax.broadcasted_iota(jnp.int32, rest.shape, 0) == 6, shift, rest)
        out[2 * own_rows : 2 * own_rows + 8, :LANES] = rest.astype(BF16)


def chunks_body(info, own, got, w_proj, lent, w_out, first, second):
    own_rows, width = w_proj.shape
    x, c, y = info[AT_X], info[AT_C], info[AT_Y]
    qkv = 3 * width // 4
    for core in range(2):
        rows = slice(core * own_rows, (core + 1) * own_rows)
        mine = c == core
        first[rows, :qkv] = jnp.where(mine, own[:own_rows, :qkv], got[:own_rows, :qkv])
        second[rows, :] = jnp.where(
            mine, own[own_rows : 2 * own_rows, :], got[own_rows : 2 * own_rows, :]
        )
    half = jnp.where(x == y, w_proj[:, : width // 2], lent[...])
    first[:own_rows, qkv:] = half[:, : width // 4]
    first[own_rows : 2 * own_rows, qkv:] = half[:, width // 4 :]
    piece = w_out.shape[0] // 2
    second[2 * own_rows :, :] = w_out[pl.ds(pl.multiple_of(x * piece, piece), piece), :]
    mine = own[2 * own_rows :, :LANES].astype(F32)
    other = got[2 * own_rows :, :LANES].astype(F32)
    low = low_half(mine.shape)
    joined = jnp.where(
        c == 0, jnp.where(low, mine, turn(other)), jnp.where(low, other, turn(mine))
    )
    both = lax.broadcasted_iota(jnp.int32, mine.shape, 0) < 6
    first[2 * own_rows :, :] = jnp.zeros((SMALL_ROWS, width), BF16)
    first[2 * own_rows :, :LANES] = jnp.where(both, joined, mine).astype(BF16)


def run_copies(copies, sems):
    started = []
    for i, (source, target) in enumerate(copies):
        copy = pltpu.make_async_copy(source, target, sems.at[i])
        copy.start()
        started.append(copy)
    return started


def attention_body(info, *refs):
    blocks, chunks = refs[:RANKS], refs[RANKS : RANKS + ORIGINS]
    normed, qkv, probs, context, send, keep_own, keep_away, qkv_weight, proj_weight, smalls = refs[
        RANKS + ORIGINS : RANKS + ORIGINS + 10
    ]
    masks, sems = refs[RANKS + ORIGINS + 10 :]
    x = info[AT_X]
    width = normed.shape[1]
    rows = normed.shape[0] // RANKS
    chip_rows = chunks[0].shape[0] - SMALL_ROWS
    own_rows = chip_rows // 2
    cols = 3 * width // 4
    copies = []
    for i, chunk in enumerate(chunks):
        at = info[i]
        start = chunks[i - 1].shape[0] if i == ORIGINS - 1 else 0
        stop = start + chunk.shape[0]
        for part in range(2):
            top = part * own_rows
            if start <= top and top + own_rows <= stop:
                source = pl.ds(top - start, own_rows)
                copies.append(
                    (
                        chunk.at[source, pl.ds(0, cols)],
                        qkv_weight.at[pl.ds(pl.multiple_of(at * chip_rows + top, own_rows), own_rows), :],
                    )
                )
                side = lax.rem(at + x, 2) * (width // 2) + part * (width // 4)
                copies.append(
                    (
                        chunk.at[source, pl.ds(cols, width // 4)],
                        proj_weight.at[
                            pl.ds(pl.multiple_of(lax.div(at, 2) * own_rows, own_rows), own_rows),
                            pl.ds(pl.multiple_of(side, LANES), width // 4),
                        ],
                    )
                )
        if stop > chip_rows:
            copies.append(
                (
                    chunk.at[pl.ds(chip_rows - start, SMALL_ROWS), pl.ds(0, LANES)],
                    smalls.at[:, pl.ds(pl.multiple_of(at * LANES, LANES), LANES)],
                )
            )
    started = run_copies(copies, sems)

    down = lax.broadcasted_iota(jnp.int32, (rows, rows), 0)
    across = lax.broadcasted_iota(jnp.int32, (rows, rows), 1)
    for b, block in enumerate(blocks):
        notes = block[rows : rows + SMALL_ROWS, : 2 * LANES].astype(F32)
        seg_row, use_row = notes[0:1, :rows], notes[1:2, :rows]
        seg_column = jnp.sum(jnp.where(down == across, seg_row, 0.0), axis=1, keepdims=True)
        visible = (seg_column == seg_row) & (across <= down) & (use_row > 0)
        masks[b] = jnp.where(visible, 1.0, 0.0)
    for copy in started:
        copy.wait()
    gain = smalls[0:1, :].astype(F32)
    shift = smalls[1:2, :].astype(F32)
    for b, block in enumerate(blocks):
        center, inverse = statistics(block[:rows, :].astype(F32))
        normed[b * rows : (b + 1) * rows, :] = (center * inverse * gain + shift).astype(BF16)

    low_row = low_half((8, LANES))
    biases = jnp.broadcast_to(smalls[7:8, :].astype(F32), (8, width))
    query_shift, value_shift = [], []
    for pair in range(2):
        first, second = (
            jnp.where(
                x == 0,
                biases[:, z * 2 * LANES : z * 2 * LANES + LANES],
                biases[:, z * 2 * LANES + LANES : (z + 1) * 2 * LANES],
            )
            for z in (2 * pair, 2 * pair + 1)
        )
        query_shift.append(jnp.where(low_row, first, turn(second))[0:1])
        value_shift.append(jnp.where(low_row, turn(first), second)[0:1])
    third = width // 4
    for n in range(3):
        product = dot(normed[...], qkv_weight[:, n * third : (n + 1) * third])
        if n != 1:
            product = product + jnp.concatenate(value_shift if n else query_shift, axis=1)
        qkv[:, n * third : (n + 1) * third] = product.astype(BF16)

    scale = HALF ** (-0.5)
    low = low_half((1, LANES))
    keep_low = jnp.where(low, 1.0, 0.0).astype(BF16)
    keep_high = jnp.where(low, 0.0, 1.0).astype(BF16)

    def attend(b, carry):
        at = pl.ds(pl.multiple_of(b * rows, rows), rows)
        mask = masks[b] > 0.5
        for pair in range(2):
            lanes = pair * LANES
            queries = qkv[at, lanes : lanes + LANES]
            keys = qkv[at, third + lanes : third + lanes + LANES]
            values = qkv[at, 2 * third + lanes : 2 * third + lanes + LANES]
            outs = []
            for side, keep in enumerate((keep_low, keep_high)):
                scores = jnp.where(mask, scale * dot_cols(queries * keep, keys), -1e30)
                expo = jnp.exp(scores - jnp.max(scores, axis=-1, keepdims=True))
                share = (expo / jnp.sum(expo, axis=-1, keepdims=True)).astype(BF16)
                probs[b * 4 + 2 * pair + side] = share
                outs.append(dot(share, values))
            context[at, lanes : lanes + LANES] = jnp.where(low, outs[0], outs[1]).astype(BF16)
        return carry

    lax.fori_loop(0, RANKS, attend, 0)
    for n in range(4):
        columns = slice(n * third, (n + 1) * third)
        store_parts(dot(context[...], proj_weight[:, columns]), columns, rows, send, keep_own, keep_away)


def store_parts(product, columns, rows, send, keep_own, keep_away):
    keep_own[:, columns] = product[:rows]
    send[0, :, columns] = product[rows : 2 * rows].astype(BF16)
    keep_away[:, columns] = product[2 * rows : 3 * rows]
    send[1, :, columns] = product[3 * rows :].astype(BF16)


def total(keep_own, near, away):
    return keep_own[...] + near[0].astype(F32) + away[...].astype(F32)


def second_norm_body(tokens, keep_own, near, away, smalls, middle, normed):
    values = tokens[...].astype(F32) + smalls[2:3, :].astype(F32) + total(keep_own, near, away)
    middle[...] = values
    center, inverse = statistics(values)
    gain, shift = smalls[3:4, :].astype(F32), smalls[4:5, :].astype(F32)
    normed[...] = (center * inverse * gain + shift).astype(BF16)


def feed_body(info, *refs):
    inputs, d_outs = refs[:RANKS], refs[RANKS : 2 * RANKS]
    chunks, smalls = refs[2 * RANKS : 2 * RANKS + ORIGINS], refs[2 * RANKS + ORIGINS]
    given, d_out, hidden, d_pre, send, keep_own, keep_away, sums, out_weight = refs[
        2 * RANKS + ORIGINS + 1 : 2 * RANKS + ORIGINS + 10
    ]
    fc_weight, sems = refs[2 * RANKS + ORIGINS + 10 :]
    rows = inputs[0].shape[0]
    width = given.shape[1]
    chip_rows = chunks[0].shape[0] // 2
    copies = []
    for i, chunk in enumerate(chunks):
        at = pl.ds(pl.multiple_of(info[i] * chip_rows, chip_rows), chip_rows)
        if i != ORIGINS - 1:
            copies.append((chunk.at[pl.ds(0, chip_rows), :], fc_weight.at[at, :]))
        if i != ORIGINS - 2:
            start = 0 if i == ORIGINS - 1 else chip_rows
            copies.append((chunk.at[pl.ds(start, chip_rows), :], out_weight.at[at, :]))
    started = run_copies(copies, sems)
    for b in range(RANKS):
        given[b * rows : (b + 1) * rows, :] = inputs[b][...]
        d_out[b * rows : (b + 1) * rows, :] = d_outs[b][...]
    for copy in started:
        copy.wait()
    tile = 2 * LANES
    root = (2.0 / jnp.pi) ** 0.5
    sums[...] = jnp.zeros(sums.shape, F32)

    def units(n, carry):
        columns = pl.ds(pl.multiple_of(n * tile, tile), tile)
        pre = dot(given[...], fc_weight[:, columns]) + smalls[6:7, columns].astype(F32)
        d_hidden = dot_cols(d_out[...], out_weight[columns, :])
        square = pre * pre
        bend = jnp.tanh(root * pre * (1.0 + 0.044715 * square))
        hidden[:, columns] = (0.5 * pre * (1.0 + bend)).astype(BF16)
        slope = 0.5 * (1.0 + bend) + 0.5 * pre * (1.0 - bend * bend) * root * (
            1.0 + 3.0 * 0.044715 * square
        )
        low = (d_hidden * slope).astype(BF16)
        d_pre[:, columns] = low
        sums[6:7, columns] = jnp.sum(low.astype(F32), axis=0, keepdims=True)
        return carry

    lax.fori_loop(0, width // tile, units, 0)
    for n in range(width // tile):
        columns = slice(n * tile, (n + 1) * tile)
        product = dot_cols(d_pre[...], fc_weight[columns, :])
        store_parts(product, columns, rows, send, keep_own, keep_away)


def feed_out_body(hidden, out_weight, send, keep_own, keep_away):
    rows = keep_own.shape[0]
    tile = 2 * LANES
    for n in range(out_weight.shape[1] // tile):
        columns = slice(n * tile, (n + 1) * tile)
        store_parts(dot(hidden[...], out_weight[:, columns]), columns, rows, send, keep_own, keep_away)


def mixed_body(info, middle, keep_own, near, away, smalls, mixed):
    values = middle[...] + total(keep_own, near, away) + smalls[5:6, :].astype(F32)
    mixed[...] = (used_rows(info, middle.shape[0]) * values).astype(BF16)


def second_back_body(info, middle, cotangent, keep_own, near, away, smalls, d_middle, d_branch, sums):
    d_values = total(keep_own, near, away)
    d_top = used_rows(info, middle.shape[0]) * cotangent[...].astype(F32)
    center, inverse = statistics(middle[...])
    unit = center * inverse
    result = d_top + norm_back(unit, inverse, d_values * smalls[3:4, :].astype(F32))
    d_middle[...] = result
    low = result.astype(BF16)
    d_branch[...] = low
    sums[...] = jnp.zeros(sums.shape, F32)
    sums[2:3, :] = jnp.sum(low.astype(F32), axis=0, keepdims=True)
    sums[3:4, :] = jnp.sum(d_values * unit, axis=0, keepdims=True)
    sums[4:5, :] = jnp.sum(d_values, axis=0, keepdims=True)
    sums[5:6, :] = jnp.sum(d_top, axis=0, keepdims=True)


def attention_back_body(info, *refs):
    d_branches, blocks = refs[:RANKS], refs[RANKS : 2 * RANKS]
    qkv, probs, qkv_weight, proj_weight, sums_two, sums_fc = refs[2 * RANKS : 2 * RANKS + 6]
    d_branch, d_qkv, send, keep_own, keep_away, sums = refs[2 * RANKS + 6 : 2 * RANKS + 12]
    (d_context,) = refs[2 * RANKS + 12 :]
    rows = d_branches[0].shape[0]
    width = d_branch.shape[1]
    third = width // 4
    x = info[AT_X]
    for b in range(RANKS):
        d_branch[b * rows : (b + 1) * rows, :] = d_branches[b][...]
    d_context[...] = dot_cols(d_branch[...], proj_weight[...]).astype(BF16)
    scale = HALF ** (-0.5)
    low = low_half((1, LANES))
    keep_low = jnp.where(low, 1.0, 0.0).astype(BF16)
    keep_high = jnp.where(low, 0.0, 1.0).astype(BF16)

    def attend(b, carry):
        at = pl.ds(pl.multiple_of(b * rows, rows), rows)
        for pair in range(2):
            lanes = pair * LANES
            queries = qkv[at, lanes : lanes + LANES]
            keys = qkv[at, third + lanes : third + lanes + LANES]
            values = qkv[at, 2 * third + lanes : 2 * third + lanes + LANES]
            d_out = d_context[at, lanes : lanes + LANES]
            results = []
            for side, keep in enumerate((keep_low, keep_high)):
                share = probs[b * 4 + 2 * pair + side]
                wide = share.astype(F32)
                d_values = dot_rows(share, d_out)
                d_probs = dot_cols(d_out * keep, values)
                d_scores = wide * (d_probs - jnp.sum(wide * d_probs, axis=-1, keepdims=True))
                d_scores = d_scores.astype(BF16)
                results.append(
                    (scale * dot(d_scores, keys), scale * dot_rows(d_scores, queries), d_values)
                )
            for n in range(3):
                merged = jnp.where(low, results[0][n], results[1][n]).astype(BF16)
                d_qkv[at, n * third + lanes : n * third + lanes + LANES] = merged
        return carry

    lax.fori_loop(0, RANKS, attend, 0)
    sums[0:8, :] = sums_two[...] + sums_fc[...]
    sums[8:, :] = jnp.zeros((SMALL_ROWS - 8, width), F32)
    stats = []
    for block in blocks:
        values = block[:rows, :].astype(F32)
        mean = jnp.mean(values, axis=-1, keepdims=True)
        center = values - mean
        stats.append((mean, lax.rsqrt(jnp.mean(center * center, axis=-1, keepdims=True) + 1e-05)))
    for n in range(4):
        columns = slice(n * third, (n + 1) * third)
        product = dot_cols(d_qkv[...], qkv_weight[columns, :])
        store_parts(product, columns, rows, send, keep_own, keep_away)
        sums[1:2, columns] = jnp.sum(product, axis=0, keepdims=True)
        along = jnp.zeros((1, third), F32)
        for b, block in enumerate(blocks):
            mean, inverse = stats[b]
            unit = (block[:rows, columns].astype(F32) - mean) * inverse
            along = along + jnp.sum(product[b * rows : (b + 1) * rows] * unit, axis=0, keepdims=True)
        sums[0:1, columns] = along
    low_row = low_half((8, LANES))
    for pair in range(2):
        lanes = pair * LANES
        d_queries = jnp.sum(d_qkv[:, lanes : lanes + LANES].astype(F32), axis=0, keepdims=True)
        d_values = jnp.sum(
            d_qkv[:, 2 * third + lanes : 2 * third + lanes + LANES].astype(F32), axis=0, keepdims=True
        )
        d_queries = jnp.broadcast_to(d_queries, (8, LANES))
        d_values = jnp.broadcast_to(d_values, (8, LANES))
        even = jnp.where(low_row, d_queries, turn(d_values))[0:1]
        odd = jnp.where(low_row, turn(d_queries), d_values)[0:1]
        for z, group in ((2 * pair, even), (2 * pair + 1, odd)):
            for y in range(2):
                start = (2 * z + y) * LANES
                sums[7:8, start : start + LANES] = jnp.where(x == y, group, 0.0)


def first_back_body(tokens, d_middle, keep_own, near, away, smalls, result):
    center, inverse = statistics(tokens[...].astype(F32))
    d_unit = total(keep_own, near, away) * smalls[0:1, :].astype(F32)
    result[...] = d_middle[...] + norm_back(center * inverse, inverse, d_unit)


def hidden_grads_body(info, own_fc, near_fc, other, grad_fc, grad_out):
    x, c = info[AT_X], info[AT_C]
    own_rows = near_fc.shape[0]
    piece = own_fc.shape[0] - 2 * own_rows
    mine = own_fc[pl.ds(pl.multiple_of(c * own_rows, own_rows), own_rows), :].astype(F32)
    near = near_fc[...].astype(F32)
    far_mine = other[:own_rows, :].astype(F32)
    far_near = other[own_rows : 2 * own_rows, :].astype(F32)
    width = own_fc.shape[1]
    for copy in range(2):
        here = x == copy
        same = jnp.where(here, mine, far_mine)
        cross = jnp.where(here, near, far_near)
        for core in range(2):
            part = jnp.where(c == core, same, cross)
            for p in range(width // LANES):
                at = p * 4 * LANES + core * 2 * LANES + copy * LANES
                grad_fc[:, at : at + LANES] = part[:, p * LANES : (p + 1) * LANES]
        grad_out[copy * piece : (copy + 1) * piece, :] = jnp.where(
            here, own_fc[2 * own_rows :, :].astype(F32), other[2 * own_rows :, :].astype(F32)
        )


def first_message_body(info, own, near, given, message):
    c = info[AT_C]
    width = own.shape[1]
    qkv = 3 * width // 4
    own_rows = (own.shape[0] - SMALL_ROWS) // 2
    rows = pl.ds(pl.multiple_of(c * own_rows, own_rows), own_rows)
    message[:own_rows, :qkv] = own[rows, :qkv]
    message[:own_rows, qkv : 2 * qkv] = near[:own_rows, :qkv]
    at = 2 * qkv
    quarter = width // 4
    for source in (own, given):
        shift = qkv if source is own else 0
        for part in range(2):
            message[:own_rows, at : at + quarter] = source[
                part * own_rows : (part + 1) * own_rows, shift : shift + quarter
            ]
            at += quarter
    mine = own[2 * own_rows :, :LANES].astype(F32)
    summed = mine + near[own_rows:, :LANES].astype(F32)
    both = lax.broadcasted_iota(jnp.int32, mine.shape, 0) < 6
    message[own_rows:, :] = jnp.zeros((SMALL_ROWS, message.shape[1]), BF16)
    message[own_rows:, :LANES] = jnp.where(both, summed, mine).astype(BF16)


def first_grads_body(info, message, other, grad_qkv, grad_proj, small):
    x, c, y = info[AT_X], info[AT_C], info[AT_Y]
    own_rows, width = grad_proj.shape
    qkv = 3 * width // 4
    low = low_half((own_rows, LANES))
    for copy in range(2):
        here = x == copy
        same = jnp.where(here, message[:own_rows, :qkv], other[:own_rows, :qkv]).astype(F32)
        cross = jnp.where(
            here, message[:own_rows, qkv : 2 * qkv], other[:own_rows, qkv : 2 * qkv]
        ).astype(F32)
        first = jnp.where(c == 0, same, cross)
        second = jnp.where(c == 0, cross, same)
        for pair in range(qkv // LANES):
            one = first[:, pair * LANES : (pair + 1) * LANES]
            two = second[:, pair * LANES : (pair + 1) * LANES]
            at = pair * 8 * HALF + copy * LANES
            grad_qkv[:, at : at + LANES] = jnp.where(low, one, turn(two))
            at += 4 * HALF
            grad_qkv[:, at : at + LANES] = jnp.where(low, turn(one), two)
    grad_proj[...] = jnp.where(
        x == y, message[:own_rows, 2 * qkv :], other[:own_rows, 2 * qkv :]
    ).astype(F32)
    mine = message[own_rows:, :LANES].astype(F32)
    far = other[own_rows:, :LANES].astype(F32)
    summed = mine + far
    small[0:6, :] = jnp.where(c == 0, summed, turn(summed))[0:6]
    small[6:7, :] = jnp.where(x == 0, mine, far)[6:7]
    small[7:8, :] = jnp.where(x == 0, far, mine)[6:7]
    small[8:9, :] = jnp.where(x == y, mine, far)[7:8]
    small[9:, :] = jnp.zeros((SMALL_ROWS - 9, LANES), F32)


def make_kernel_local(n_replica, n_shard):
    n_pos = n_shard // 2
    half = n_pos // 2

    def every(move):
        pairs = []
        for r in range(n_replica):
            for p in range(n_pos):
                for c in range(2):
                    to = move(r, p, c)
                    if to is not None:
                        pairs.append((r * n_shard + p * 2 + c, to[0] * n_shard + to[1] * 2 + to[2]))
        return pairs

    ring = list(range(0, n_pos, 2)) + list(range(n_pos - 1, 0, -2))
    after = {p: ring[(i + 1) % n_pos] for i, p in enumerate(ring)}
    before = {p: ring[i - 1] for i, p in enumerate(ring)}

    def mover(move):
        pairs = every(move)
        return lambda v: lax.ppermute(v, MESH_AXES, pairs)

    to_core = mover(lambda r, p, c: (r, p, 1 - c))
    to_copy = mover(lambda r, p, c: (r ^ 1, p, c))
    to_next = mover(lambda r, p, c: (r, after[p], c))
    to_back = mover(lambda r, p, c: (r, before[p], c))
    lend = mover(lambda r, p, c: (r, p ^ 1, c) if p % 2 == r % 2 else None)
    give = mover(lambda r, p, c: (r, p ^ 1, c) if p % 2 != r % 2 else None)

    def ring_gather(chunk, low):
        chunks = [chunk]
        forth = back = chunk
        for _ in range(1, half):
            forth = to_next(forth)
            back = to_back(back)
            chunks += [forth, back]
        return chunks + [to_next(forth[:low]), to_back(back[low:])]

    def ring_scatter(term, low):
        def add(left, right):
            return (left.astype(F32) + right.astype(F32)).astype(BF16)

        far = term(half)
        forth = to_next(far[:low])
        back = to_back(far[low:])
        ahead = term(half - 1)
        behind = term(1 - half)
        forth = to_next(jnp.concatenate([add(forth, ahead[:low]), ahead[low:]]))
        back = to_back(jnp.concatenate([behind[:low], add(back, behind[low:])]))
        for step in range(half - 2, 0, -1):
            forth = to_next(add(forth, term(step)))
            back = to_back(add(back, term(-step)))
        return (term(0).astype(F32) + forth.astype(F32) + back.astype(F32)).astype(BF16)

    def group_gather(block):
        other = to_copy(block)
        return [block, to_core(block), other, to_core(other)]

    def group_scatter(send, keep_away):
        near = to_core(send)
        return near, to_copy((keep_away + near[1].astype(F32)).astype(BF16))

    def local(
        tokens,
        segments,
        counts,
        ln1_gain,
        ln1_bias,
        w_qkv,
        bias_query,
        bias_value,
        w_proj,
        bias_proj,
        ln2_gain,
        ln2_bias,
        w_fc,
        bias_fc,
        w_out,
        bias_out,
        cotangent,
    ):
        rows, width = tokens.shape
        own_rows = width // n_shard
        chip_rows = 2 * own_rows
        piece = w_out.shape[0] // 2
        units = n_pos * piece
        all_rows = RANKS * rows
        qkv_cols = 3 * width // 4
        replica_at = lax.axis_index("replica")
        shard_at = lax.axis_index("shard")
        x, c, p = replica_at % 2, shard_at % 2, shard_at // 2
        place = jnp.where(p % 2 == 0, p // 2, n_pos - 1 - p // 2)

        def origin(index):
            index = index % n_pos
            return jnp.where(index < half, 2 * index, 2 * (n_pos - 1 - index) + 1)

        offsets = [0]
        for step in range(1, half):
            offsets += [-step, step]
        offsets += [half, half]
        info = jnp.stack(
            [origin(place + offset) for offset in offsets] + [x, c, p % 2, counts[0]]
        ).astype(jnp.int32)

        position = jnp.arange(rows, dtype=jnp.int32)
        notes = jnp.stack([segments.astype(BF16), (position < counts[0]).astype(BF16)])
        notes = jnp.pad(notes, ((0, SMALL_ROWS - 2), (0, width - rows)))
        none = jnp.zeros((own_rows,), BF16)
        vectors = jnp.stack([ln1_gain, ln1_bias, bias_proj, ln2_gain, ln2_bias, bias_out, none, bias_query])
        others = jnp.stack([none] * 7 + [bias_value])
        vectors = jnp.concatenate([vectors, others], axis=1)
        lent = lend(w_proj[:, width // 2 :])
        block, d_top, sent, own = kernel_call(
            prepare_body,
            [SMEM_SPEC] + [VMEM_SPEC] * 7,
            [
                ((rows + SMALL_ROWS, width), BF16),
                ((rows, width), BF16),
                ((chip_rows + SMALL_ROWS, width), BF16),
                ((chip_rows + SMALL_ROWS, width), BF16),
            ],
        )(info, tokens, notes, cotangent, w_qkv, w_fc, vectors, bias_fc.reshape(2, piece))
        got = to_core(sent)
        first_chunk, second_chunk = kernel_call(
            chunks_body,
            [SMEM_SPEC] + [VMEM_SPEC] * 5,
            [((chip_rows + SMALL_ROWS, width), BF16), ((chip_rows + piece, width), BF16)],
        )(info, own, got, w_proj, lent, w_out)
        first_chunks = ring_gather(first_chunk, own_rows)
        blocks = group_gather(block)
        second_chunks = ring_gather(second_chunk, chip_rows)
        d_outs = group_gather(d_top)

        parts = [((2, rows, width), BF16), ((rows, width), F32), ((rows, width), F32)]
        normed, qkv, probs, context, send, keep_own, keep_away, qkv_weight, proj_weight, smalls = kernel_call(
            attention_body,
            [SMEM_SPEC] + [VMEM_SPEC] * RANKS + [ANY_SPEC] * ORIGINS,
            [
                ((all_rows, width), BF16),
                ((all_rows, qkv_cols), BF16),
                ((4 * RANKS, rows, rows), BF16),
                ((all_rows, width // 4), BF16),
                *parts,
                ((width, qkv_cols), BF16),
                ((width // 4, width), BF16),
                ((SMALL_ROWS, width), BF16),
            ],
            [pltpu.VMEM((RANKS, rows, rows), F32), pltpu.SemaphoreType.DMA((5 * n_pos,))],
            flops=3 * all_rows * width * width,
            moved=12 << 20,
        )(info, *blocks, *first_chunks)
        near, away = group_scatter(send, keep_away)
        middle, normed_two = kernel_call(
            second_norm_body, [VMEM_SPEC] * 5, [((rows, width), F32), ((rows, width), BF16)]
        )(tokens, keep_own, near, away, smalls)

        inputs = group_gather(normed_two)
        given, d_out, hidden, d_pre, send, keep_own, keep_away, sums_fc, out_weight = kernel_call(
            feed_body,
            [SMEM_SPEC] + [VMEM_SPEC] * (2 * RANKS) + [ANY_SPEC] * ORIGINS + [VMEM_SPEC],
            [
                ((all_rows, width), BF16),
                ((all_rows, width), BF16),
                ((all_rows, units), BF16),
                ((all_rows, units), BF16),
                *parts,
                ((8, units), F32),
                ((units, width), BF16),
            ],
            [pltpu.VMEM((width, units), BF16), pltpu.SemaphoreType.DMA((2 * n_pos,))],
            flops=6 * all_rows * width * units,
            moved=16 << 20,
        )(info, *inputs, *d_outs, *second_chunks, smalls)
        near, away = group_scatter(send, keep_away)
        d_middle, d_branch, sums_two = kernel_call(
            second_back_body,
            [SMEM_SPEC] + [VMEM_SPEC] * 6,
            [((rows, width), F32), ((rows, width), BF16), ((8, width), F32)],
        )(info, middle, cotangent, keep_own, near, away, smalls)

        grad_w_out = dot_rows(hidden, d_out).astype(BF16)
        grad_w_fc = dot_rows(given, d_pre).astype(BF16)
        send, keep_own, keep_away = kernel_call(
            feed_out_body, [VMEM_SPEC] * 2, parts, flops=2 * all_rows * width * units, moved=8 << 20
        )(hidden, out_weight)

        def second_term(offset):
            at = origin(place + offset)
            return jnp.concatenate(
                [
                    lax.dynamic_slice_in_dim(grad_w_fc, at * chip_rows, chip_rows, 0),
                    lax.dynamic_slice_in_dim(grad_w_out, at * piece, piece, 0),
                ]
            )

        own_second = ring_scatter(second_term, chip_rows)
        near, away = group_scatter(send, keep_away)
        (mixed,) = kernel_call(mixed_body, [SMEM_SPEC] + [VMEM_SPEC] * 5, [((rows, width), BF16)])(
            info, middle, keep_own, near, away, smalls
        )

        d_branches = group_gather(d_branch)
        d_branch, d_qkv, send, keep_own, keep_away, sums = kernel_call(
            attention_back_body,
            [SMEM_SPEC] + [VMEM_SPEC] * (2 * RANKS + 6),
            [
                ((all_rows, width), BF16),
                ((all_rows, qkv_cols), BF16),
                *parts,
                ((SMALL_ROWS, width), F32),
            ],
            [pltpu.VMEM((all_rows, width // 4), BF16)],
            flops=3 * all_rows * width * width,
            moved=12 << 20,
        )(info, *d_branches, *blocks, qkv, probs, qkv_weight, proj_weight, sums_two, sums_fc)
        near, away = group_scatter(send, keep_away)
        (grad_tokens,) = kernel_call(first_back_body, [VMEM_SPEC] * 6, [((rows, width), F32)])(
            tokens, d_middle, keep_own, near, away, smalls
        )

        grad_w_proj = dot_rows(context, d_branch).astype(BF16)
        grad_w_qkv = dot_rows(normed, d_qkv).astype(BF16).reshape(n_pos, chip_rows, qkv_cols)
        small_terms = sums.astype(BF16).reshape(SMALL_ROWS, n_pos, chip_rows).transpose(1, 0, 2)
        small_terms = jnp.pad(small_terms, ((0, 0), (0, 0), (0, width - chip_rows)))
        proj_terms = grad_w_proj.reshape(n_pos // 2, own_rows, 2, 2, width // 4)
        proj_terms = proj_terms.transpose(0, 2, 3, 1, 4)
        proj_terms = jnp.where(x == 0, proj_terms, proj_terms[:, ::-1])
        proj_terms = proj_terms.reshape(n_pos, chip_rows, width // 4)
        first_terms = jnp.concatenate(
            [jnp.concatenate([grad_w_qkv, proj_terms], axis=2), small_terms], axis=1
        )

        def first_term(offset):
            return lax.dynamic_index_in_dim(first_terms, origin(place + offset), 0, keepdims=False)

        own_first = ring_scatter(first_term, own_rows)

        near_fc = to_core(lax.dynamic_slice_in_dim(own_second, (1 - c) * own_rows, own_rows, 0))
        own_fc = lax.dynamic_slice_in_dim(own_second, c * own_rows, own_rows, 0)
        other = to_copy(jnp.concatenate([own_fc, near_fc, own_second[chip_rows:]]))
        grad_w_fc, grad_w_out = kernel_call(
            hidden_grads_body,
            [SMEM_SPEC] + [VMEM_SPEC] * 3,
            [((own_rows, 4 * units), F32), ((2 * piece, width), F32)],
        )(info, own_second, near_fc, other)

        near_first = to_core(
            jnp.concatenate(
                [
                    lax.dynamic_slice_in_dim(own_first, (1 - c) * own_rows, own_rows, 0)[:, :qkv_cols],
                    own_first[chip_rows:, :qkv_cols],
                ]
            )
        )
        given_proj = give(own_first[:chip_rows, qkv_cols:])
        (message,) = kernel_call(
            first_message_body,
            [SMEM_SPEC] + [VMEM_SPEC] * 3,
            [((own_rows + SMALL_ROWS, 2 * qkv_cols + width), BF16)],
        )(info, own_first, near_first, given_proj)
        grad_w_qkv, grad_w_proj, small = kernel_call(
            first_grads_body,
            [SMEM_SPEC] + [VMEM_SPEC] * 2,
            [((own_rows, 3 * width), F32), ((own_rows, width), F32), ((SMALL_ROWS, LANES), F32)],
        )(info, message, to_copy(message))
        return (
            mixed,
            grad_tokens,
            small[0, :own_rows],
            small[1, :own_rows],
            grad_w_qkv,
            small[8, :own_rows],
            small[8, own_rows:],
            grad_w_proj,
            small[2, :own_rows],
            small[3, :own_rows],
            small[4, :own_rows],
            grad_w_fc,
            small[6:8].reshape(-1),
            grad_w_out,
            small[5, :own_rows],
        )

    return local


def solution(mesh):
    tokens_spec = P(MESH_AXES, None)
    slots_spec = P(MESH_AXES)
    rows_spec = P("shard", None)
    vector_spec = P("shard")
    in_specs = (
        tokens_spec,
        slots_spec,
        slots_spec,
        vector_spec,
        vector_spec,
        rows_spec,
        vector_spec,
        vector_spec,
        rows_spec,
        vector_spec,
        vector_spec,
        vector_spec,
        rows_spec,
        vector_spec,
        rows_spec,
        vector_spec,
        tokens_spec,
    )
    out_specs = (
        tokens_spec,
        tokens_spec,
        vector_spec,
        vector_spec,
        rows_spec,
        vector_spec,
        vector_spec,
        rows_spec,
        vector_spec,
        vector_spec,
        vector_spec,
        rows_spec,
        vector_spec,
        rows_spec,
        vector_spec,
    )
    n_replica, n_shard = mesh.shape["replica"], mesh.shape["shard"]
    make = make_kernel_local if (n_replica, n_shard) == (2, HEADS) else make_local
    local = make(n_replica, n_shard)
    return jax.shard_map(local, mesh=mesh, in_specs=in_specs, out_specs=out_specs, check_vma=False)
```

```python
import functools

import jax
import jax.numpy as jnp
from jax import lax
from jax.experimental import pallas as pl
from jax.experimental.pallas import tpu as pltpu
from jax.sharding import PartitionSpec as P

HEADS = 16
RANKS = 4
MESH_AXES = ("replica", "shard")
BF16 = jnp.bfloat16
F32 = jnp.float32
SMALL_ROWS = 16


def layer_norm(values, gain, shift):
    center = values - jnp.mean(values, axis=-1, keepdims=True)
    spread = jnp.mean(center * center, axis=-1, keepdims=True)
    return center * lax.rsqrt(spread + 1e-05) * gain + shift


def unit_norm(values):
    center = values - jnp.mean(values, axis=-1, keepdims=True)
    spread = jnp.mean(center * center, axis=-1, keepdims=True)
    return center * lax.rsqrt(spread + 1e-05)


def smooth_gate(values):
    return jax.nn.gelu(values, approximate=True)


def dot_rows(left, right):
    return lax.dot_general(left, right, (((0,), (0,)), ((), ())), preferred_element_type=F32)


def dot_cols(left, right):
    return lax.dot_general(left, right, (((1,), (1,)), ((), ())), preferred_element_type=F32)


def dot(left, right):
    return jnp.dot(left, right, preferred_element_type=F32)


def make_local(n_replica, n_shard):
    n_pos = n_shard // 2
    half = n_pos // 2
    head_a_shard = n_shard == HEADS
    n_pairs = n_replica // 2
    pair_groups = [[2 * i + j for i in range(n_pairs)] for j in range(2)]

    def every(move):
        pairs = []
        for r in range(n_replica):
            for p in range(n_pos):
                for c in range(2):
                    to = move(r, p, c)
                    if to is not None:
                        pairs.append((r * n_shard + p * 2 + c, to[0] * n_shard + to[1] * 2 + to[2]))
        return pairs

    ring = list(range(0, n_pos, 2)) + list(range(n_pos - 1, 0, -2))
    after = {p: ring[(i + 1) % n_pos] for i, p in enumerate(ring)}
    before = {p: ring[i - 1] for i, p in enumerate(ring)}
    core_pairs = every(lambda r, p, c: (r, p, 1 - c))
    copy_pairs = every(lambda r, p, c: (r ^ 1, p, c))
    next_pairs = every(lambda r, p, c: (r, after[p], c))
    back_pairs = every(lambda r, p, c: (r, before[p], c))
    lend_pairs = every(lambda r, p, c: (r, p ^ 1, c) if p % 2 == r % 2 else None)
    give_pairs = every(lambda r, p, c: (r, p ^ 1, c) if p % 2 != r % 2 else None)
    share_pairs = every(lambda r, p, c: (r ^ 1, p, c) if p % 2 == r % 2 else None)

    def to_core(v):
        return lax.ppermute(v, MESH_AXES, core_pairs)

    def to_copy(v):
        return lax.ppermute(v, MESH_AXES, copy_pairs)

    def to_next(v):
        return lax.ppermute(v, MESH_AXES, next_pairs)

    def to_back(v):
        return lax.ppermute(v, MESH_AXES, back_pairs)

    def cut(rows):
        return max(16, rows // 32 * 16)

    def ring_gather(chunk, place, origin):
        low = cut(chunk.shape[0])
        full = jnp.zeros((n_pos,) + chunk.shape, chunk.dtype)

        def put(full, value, offset, row=0):
            return lax.dynamic_update_slice(full, value[None], (origin(place + offset), row, 0))

        full = put(full, chunk, 0)
        forth = back = chunk
        for step in range(1, half):
            forth = to_next(forth)
            back = to_back(back)
            full = put(full, forth, -step)
            full = put(full, back, step)
        forth = to_next(forth[:low])
        back = to_back(back[low:])
        full = put(full, forth, half)
        full = put(full, back, half, low)
        return full

    def ring_scatter(full, place, origin):
        low = cut(full.shape[1])

        def term(offset):
            return lax.dynamic_index_in_dim(full, origin(place + offset), 0, keepdims=False)

        def add(left, right):
            return (left.astype(F32) + right.astype(F32)).astype(BF16)

        far = term(half)
        forth = to_next(far[:low])
        back = to_back(far[low:])
        ahead = term(half - 1)
        behind = term(1 - half)
        forth = to_next(jnp.concatenate([add(forth, ahead[:low]), ahead[low:]]))
        back = to_back(jnp.concatenate([behind[:low], add(back, behind[low:])]))
        for step in range(half - 2, 0, -1):
            forth = to_next(add(forth, term(step)))
            back = to_back(add(back, term(-step)))
        return term(0).astype(F32) + forth.astype(F32) + back.astype(F32)

    def group_gather(block):
        other = to_copy(block)
        return jnp.stack([block, to_core(block), other, to_core(other)])

    def group_scatter(parts):
        near = to_core(jnp.stack([parts[1], parts[3]]).astype(BF16)).astype(F32)
        away = to_copy((parts[2] + near[1]).astype(BF16)).astype(F32)
        return parts[0] + near[0] + away

    def local(
        tokens,
        segments,
        counts,
        ln1_gain,
        ln1_bias,
        w_qkv,
        bias_query,
        bias_value,
        w_proj,
        bias_proj,
        ln2_gain,
        ln2_bias,
        w_fc,
        bias_fc,
        w_out,
        bias_out,
        cotangent,
    ):
        row_count, width = tokens.shape
        head_width = width // HEADS
        own_rows = width // n_shard
        chip_rows = 2 * own_rows
        own_hidden = w_out.shape[0]
        piece = own_hidden // 2
        groups = HEADS // RANKS
        scale = head_width ** (-0.5)
        replica_at = lax.axis_index("replica")
        shard_at = lax.axis_index("shard")
        x = replica_at % 2
        c = shard_at % 2
        p = shard_at // 2
        rank = 2 * x + c
        place = jnp.where(p % 2 == 0, p // 2, n_pos - 1 - p // 2)

        def origin(index):
            index = index % n_pos
            return jnp.where(index < half, 2 * index, 2 * (n_pos - 1 - index) + 1)

        def by_core(mine, other):
            return jnp.where(c == 0, jnp.stack([mine, other]), jnp.stack([other, mine]))

        position = jnp.arange(row_count, dtype=jnp.int32)
        in_use = (position < counts[0]).astype(F32)
        notes = jnp.stack([segments.astype(BF16), in_use.astype(BF16)])
        notes = jnp.pad(notes, ((0, SMALL_ROWS - 2), (0, width - row_count)))
        seen = group_gather(jnp.concatenate([tokens, notes]))
        tokens_all = seen[:, :row_count].reshape(RANKS * row_count, width)
        seg_all = seen[:, row_count, :row_count]
        use_all = seen[:, row_count + 1, :row_count]

        def qkv_part(which):
            view = w_qkv.reshape(own_rows, 3, groups, RANKS, head_width)
            return lax.dynamic_index_in_dim(view, which, 3, keepdims=False).reshape(own_rows, -1)

        def fc_part(core):
            view = w_fc.reshape(own_rows, n_pos, 4, piece)
            part = lax.dynamic_index_in_dim(view, 2 * core + x, 2, keepdims=False)
            return part.reshape(own_rows, -1)

        vectors = [ln1_gain, ln1_bias, bias_query, bias_value, bias_proj, ln2_gain, ln2_bias, bias_out, bias_fc]
        starts = [0]
        for vector in vectors:
            starts.append(starts[-1] + vector.shape[0])
        n_small = starts[-1]
        qkv_width = 3 * groups * head_width
        small = jnp.concatenate(vectors)[None]
        small = jnp.pad(small, ((0, SMALL_ROWS - 1), (0, 0)))
        both_small = by_core(small[0], to_core(small)[0])
        qkv_chunk = by_core(qkv_part(rank), to_core(qkv_part(rank ^ 1))).reshape(chip_rows, qkv_width)
        if head_a_shard:
            lent = lax.ppermute(w_proj[:, width // 2 :], MESH_AXES, lend_pairs)
            proj_half = jnp.where(p % 2 == x, w_proj[:, : width // 2], lent)
            proj_chunk = jnp.concatenate([proj_half[:, : width // 4], proj_half[:, width // 4 :]])
        else:
            proj_chunk = jnp.zeros((chip_rows, width // 4), BF16)
        small_chunk = jnp.pad(both_small, ((0, SMALL_ROWS - 2), (0, width - n_small)))
        first_chunk = jnp.concatenate(
            [jnp.concatenate([qkv_chunk, proj_chunk], axis=1), small_chunk]
        )
        fc_chunk = by_core(fc_part(c), to_core(fc_part(1 - c))).reshape(chip_rows, n_pos * piece)
        out_chunk = lax.dynamic_slice_in_dim(w_out, x * piece, piece, 0)

        first_full = ring_gather(first_chunk, place, origin)
        fc_weight = ring_gather(fc_chunk, place, origin).reshape(width, n_pos * piece)
        out_weight = ring_gather(out_chunk, place, origin).reshape(n_pos * piece, width)

        qkv_weight = first_full[:, :chip_rows, :qkv_width].reshape(width, qkv_width)
        if head_a_shard:
            proj_full = first_full[:, :chip_rows, qkv_width:].reshape(
                n_pos // 2, 2, 2, own_rows, width // 4
            )
            proj_full = jnp.where(x == 0, proj_full, proj_full[:, ::-1])
            proj_weight = proj_full.transpose(0, 3, 1, 2, 4).reshape(groups * head_width, width)
        else:
            proj_full = lax.all_gather(w_proj, "shard", axis=0, tiled=True)
            proj_full = proj_full.reshape(groups, RANKS, head_width, width)
            proj_weight = lax.dynamic_index_in_dim(proj_full, rank, 1, keepdims=False)
            proj_weight = proj_weight.reshape(groups * head_width, width)
        smalls = first_full[:, chip_rows : chip_rows + 2, :n_small].reshape(n_shard, n_small)
        params = [
            smalls[:, starts[i] : starts[i + 1]].reshape(-1).astype(F32) for i in range(len(vectors))
        ]
        gain_one, shift_one, query_shift, value_shift, proj_shift, gain_two, shift_two, out_shift, fc_shift = params

        def rank_heads(vector):
            view = vector.reshape(groups, RANKS, head_width)
            return lax.dynamic_index_in_dim(view, rank, 1, keepdims=False).reshape(-1)

        fc_shift = lax.dynamic_index_in_dim(
            fc_shift.reshape(n_pos, 4, piece), 2 * c + x, 1, keepdims=False
        ).reshape(-1)
        qkv_shift = jnp.concatenate(
            [
                rank_heads(query_shift),
                jnp.zeros((groups * head_width,), F32),
                rank_heads(value_shift),
            ]
        )

        unit_one = unit_norm(tokens_all.astype(F32))
        input_one = (unit_one * gain_one + shift_one).astype(BF16)
        qkv_rows = (dot(input_one, qkv_weight) + qkv_shift).astype(BF16)
        qkv_view = qkv_rows.reshape(RANKS, row_count, 3, groups, head_width)
        queries, keys_rows, values_rows = qkv_view[:, :, 0], qkv_view[:, :, 1], qkv_view[:, :, 2]
        visible = (
            (seg_all[:, :, None] == seg_all[:, None, :])
            & (position[None, None, :] <= position[None, :, None])
            & (use_all[:, None, :] > 0)
        )[:, None]
        scores = scale * jnp.einsum("bqhd,bkhd->bhqk", queries, keys_rows, preferred_element_type=F32)
        scores = jnp.where(visible, scores, -1e30)
        top_score = jnp.max(scores, axis=-1, keepdims=True)
        expo = jnp.exp(scores - top_score)
        probs = expo / jnp.sum(expo, axis=-1, keepdims=True)
        probs_low = probs.astype(BF16)
        context = (
            jnp.einsum("bhqk,bkhd->bqhd", probs_low, values_rows, preferred_element_type=F32)
            .reshape(RANKS * row_count, groups * head_width)
            .astype(BF16)
        )
        block_shape = (RANKS, row_count, width)
        stream = tokens.astype(F32)
        middle = stream + proj_shift + group_scatter(dot(context, proj_weight).reshape(block_shape))

        normed_two, norm_two_back = jax.vjp(layer_norm, middle, gain_two, shift_two)
        input_two = group_gather(normed_two.astype(BF16)).reshape(RANKS * row_count, width)
        pre_act = dot(input_two, fc_weight) + fc_shift
        gate_value, gate_back = jax.vjp(smooth_gate, pre_act)
        hidden = gate_value.astype(BF16)
        branch_two = group_scatter(dot(hidden, out_weight).reshape(block_shape)) + out_shift
        mixed = (in_use[:, None] * (middle + branch_two)).astype(BF16)

        d_top = in_use[:, None] * cotangent.astype(F32)
        d_out = group_gather(d_top.astype(BF16)).reshape(RANKS * row_count, width)
        grad_w_out = dot_rows(hidden, d_out).astype(BF16).reshape(n_pos, piece, width)
        d_pre = gate_back(dot_cols(d_out, out_weight))[0].astype(BF16)
        grad_w_fc = dot_rows(input_two, d_pre).astype(BF16).reshape(n_pos, chip_rows, n_pos * piece)
        d_input_two = group_scatter(dot_cols(d_pre, fc_weight).reshape(block_shape))
        d_mid_norm, grad_gain_two, grad_shift_two = norm_two_back(d_input_two)
        d_middle = d_top + d_mid_norm
        own_w_out = ring_scatter(grad_w_out, place, origin)
        own_w_fc = ring_scatter(grad_w_fc, place, origin)

        d_branch = group_gather(d_middle.astype(BF16)).reshape(RANKS * row_count, width)
        grad_w_proj = dot_rows(context, d_branch)
        d_context = (
            dot_cols(d_branch, proj_weight)
            .astype(BF16)
            .reshape(RANKS, row_count, groups, head_width)
        )
        d_values = jnp.einsum("bhqk,bqhd->bkhd", probs_low, d_context, preferred_element_type=F32)
        d_probs = jnp.einsum("bqhd,bkhd->bhqk", d_context, values_rows, preferred_element_type=F32)
        d_scores = (
            probs * (d_probs - jnp.sum(probs * d_probs, axis=-1, keepdims=True))
        ).astype(BF16)
        d_queries = scale * jnp.einsum(
            "bhqk,bkhd->bqhd", d_scores, keys_rows, preferred_element_type=F32
        )
        d_keys = scale * jnp.einsum("bhqk,bqhd->bkhd", d_scores, queries, preferred_element_type=F32)
        d_qkv = (
            jnp.stack([d_queries, d_keys, d_values], axis=2)
            .reshape(RANKS * row_count, qkv_width)
            .astype(BF16)
        )
        grad_w_qkv = dot_rows(input_one, d_qkv).astype(BF16).reshape(n_pos, chip_rows, qkv_width)
        d_input_one = dot_cols(d_qkv, qkv_weight)
        grad_gain_one = jnp.sum(d_input_one * unit_one, axis=0)
        grad_shift_one = jnp.sum(d_input_one, axis=0)
        d_qkv_sums = jnp.sum(d_qkv.astype(F32), axis=0)

        def own_term(values):
            return jnp.sum(values.astype(BF16).astype(F32), axis=0)

        def at_rank(sums):
            view = sums.reshape(groups, 1, head_width)
            mine = jnp.arange(RANKS)[None, :, None] == rank
            return jnp.where(mine, view, 0.0).reshape(-1)

        fc_sums = jnp.sum(d_pre.astype(F32), axis=0).reshape(n_pos, 1, piece)
        fc_sums = jnp.where(jnp.arange(4)[None, :, None] == 2 * c + x, fc_sums, 0.0).reshape(-1)
        small_terms = [
            grad_gain_one,
            grad_shift_one,
            at_rank(d_qkv_sums[: groups * head_width]),
            at_rank(d_qkv_sums[2 * groups * head_width :]),
            own_term(d_middle),
            grad_gain_two,
            grad_shift_two,
            own_term(d_top),
            fc_sums,
        ]
        small_terms = jnp.concatenate(
            [term.reshape(n_shard, -1) for term in small_terms], axis=1
        ).astype(BF16)
        small_terms = jnp.pad(
            small_terms.reshape(n_pos, 2, n_small),
            ((0, 0), (0, SMALL_ROWS - 2), (0, width - n_small)),
        )
        if head_a_shard:
            proj_terms = grad_w_proj.astype(BF16).reshape(n_pos // 2, own_rows, 2, 2, width // 4)
            proj_terms = proj_terms.transpose(0, 2, 3, 1, 4)
            proj_terms = jnp.where(x == 0, proj_terms, proj_terms[:, ::-1])
            proj_terms = proj_terms.reshape(n_pos, chip_rows, width // 4)
        else:
            proj_terms = jnp.zeros((n_pos, chip_rows, width // 4), BF16)
        first_terms = jnp.concatenate(
            [jnp.concatenate([grad_w_qkv, proj_terms], axis=2), small_terms], axis=1
        )
        own_first = ring_scatter(first_terms, place, origin)
        d_in_norm = jax.vjp(unit_norm, stream)[1](
            group_scatter(d_input_one.reshape(block_shape)) * gain_one
        )[0]
        grad_tokens = d_middle + d_in_norm

        def rows_of(chunk, core):
            return lax.dynamic_slice_in_dim(chunk, core * own_rows, own_rows, 0)

        def by_copy(mine, other):
            return jnp.where(x == 0, jnp.stack([mine, other]), jnp.stack([other, mine]))

        own_w_out = own_w_out.astype(BF16)
        grad_w_out = by_copy(own_w_out, to_copy(own_w_out)).reshape(own_hidden, width)

        own_w_fc = own_w_fc.astype(BF16)
        fc_rows = by_core(rows_of(own_w_fc, c), to_core(rows_of(own_w_fc, 1 - c)))
        fc_rows = by_copy(fc_rows, to_copy(fc_rows))
        fc_rows = fc_rows.reshape(2, 2, own_rows, n_pos, piece)
        grad_w_fc = fc_rows.transpose(2, 3, 1, 0, 4).reshape(own_rows, -1)

        own_first = own_first.astype(BF16)
        own_qkv = own_first[:chip_rows, :qkv_width]
        qkv_grad = by_core(rows_of(own_qkv, c), to_core(rows_of(own_qkv, 1 - c)))
        qkv_grad = by_copy(qkv_grad, to_copy(qkv_grad))
        qkv_grad = qkv_grad.reshape(2, 2, own_rows, 3, groups, head_width)
        grad_w_qkv = qkv_grad.transpose(2, 3, 4, 0, 1, 5).reshape(own_rows, -1)

        own_small = own_first[chip_rows:, :n_small]
        near_small = to_core(own_small)
        small_sum = jnp.where(
            c == 0,
            own_small[0].astype(F32) + near_small[0].astype(F32),
            own_small[1].astype(F32) + near_small[1].astype(F32),
        )
        small_send = jnp.pad(small_sum[None].astype(BF16), ((0, SMALL_ROWS - 1), (0, 0)))
        small_sum = small_sum + to_copy(small_send)[0].astype(F32)

        if head_a_shard:
            own_proj = own_first[:chip_rows, qkv_width:]
            given = lax.ppermute(own_proj, MESH_AXES, give_pairs)
            proj_rows = jnp.stack([own_proj, given]).reshape(2, 2, own_rows, width // 4)
            proj_rows = proj_rows.transpose(2, 0, 1, 3).reshape(own_rows, width)
            shared = lax.ppermute(proj_rows, MESH_AXES, share_pairs)
            grad_w_proj = jnp.where(p % 2 == x, proj_rows, shared)
        else:
            proj_rows = grad_w_proj.astype(BF16).reshape(groups, 1, head_width, width)
            mine = jnp.arange(RANKS)[None, :, None, None] == rank
            proj_rows = jnp.where(mine, proj_rows, 0).reshape(width, width)
            proj_rows = lax.psum_scatter(proj_rows, "shard", scatter_dimension=0, tiled=True)
            grad_w_proj = proj_rows.astype(F32) + to_copy(proj_rows).astype(F32)

        if n_pairs > 1:
            grad_w_out, grad_w_fc, grad_w_qkv, grad_w_proj, small_sum = lax.psum(
                tuple(
                    value.astype(BF16)
                    for value in (grad_w_out, grad_w_fc, grad_w_qkv, grad_w_proj, small_sum)
                ),
                "replica",
                axis_index_groups=pair_groups,
            )
        small_sum = small_sum.astype(F32)
        small_grads = [small_sum[starts[i] : starts[i + 1]] for i in range(len(vectors))]
        g_gain_one, g_shift_one, g_query, g_value, g_proj, g_gain_two, g_shift_two, g_out, g_fc = small_grads
        return (
            mixed,
            grad_tokens,
            g_gain_one,
            g_shift_one,
            grad_w_qkv.astype(F32),
            g_query,
            g_value,
            grad_w_proj.astype(F32),
            g_proj,
            g_gain_two,
            g_shift_two,
            grad_w_fc.astype(F32),
            g_fc,
            grad_w_out.astype(F32),
            g_out,
        )

    return local

LANES = 128
HALF = 64
VMEM_BYTES = 26 * 1024 * 1024
ORIGINS = 9
AT_X, AT_C, AT_Y, AT_COUNT = 9, 10, 11, 12
VMEM_SPEC = pl.BlockSpec(memory_space=pltpu.VMEM)
SMEM_SPEC = pl.BlockSpec(memory_space=pltpu.SMEM)
ANY_SPEC = pl.BlockSpec(memory_space=pl.ANY)


def kernel_call(body, in_specs, outs, scratch=(), micros=1):
    return pl.pallas_call(
        body,
        out_shape=tuple(jax.ShapeDtypeStruct(shape, dtype) for shape, dtype in outs),
        in_specs=list(in_specs),
        out_specs=tuple(VMEM_SPEC for _ in outs),
        scratch_shapes=list(scratch),
        compiler_params=pltpu.CompilerParams(vmem_limit_bytes=VMEM_BYTES),
        cost_estimate=pl.CostEstimate(
            flops=0, bytes_accessed=micros * 3_000_000, transcendentals=0
        ),
    )


def low_half(shape):
    return lax.broadcasted_iota(jnp.int32, shape, len(shape) - 1) < HALF


def turn(values):
    return jnp.concatenate([values[:, HALF:], values[:, :HALF]], axis=1)


def join(c, first, second, low):
    even = jnp.where(low, first, turn(second))
    odd = jnp.where(low, turn(first), second)
    return jnp.where(c == 0, even, odd)


def statistics(values):
    center = values - jnp.mean(values, axis=-1, keepdims=True)
    spread = jnp.mean(center * center, axis=-1, keepdims=True)
    return center, lax.rsqrt(spread + 1e-05)


def norm_back(unit, inverse, d_unit):
    along = jnp.mean(d_unit * unit, axis=-1, keepdims=True)
    return inverse * (d_unit - jnp.mean(d_unit, axis=-1, keepdims=True) - unit * along)


def used_rows(info, rows):
    return (lax.broadcasted_iota(jnp.int32, (rows, 1), 0) < info[AT_COUNT]).astype(F32)


def tokens_body(info, tokens, segments, cotangent, block, d_out):
    rows = tokens.shape[0]
    block[:rows, :] = tokens[...]
    down = lax.broadcasted_iota(jnp.int32, (SMALL_ROWS, rows), 0)
    across = lax.broadcasted_iota(jnp.int32, (SMALL_ROWS, rows), 1)
    used = jnp.where(across < info[AT_COUNT], 1.0, 0.0)
    notes = jnp.where(down == 0, segments[...].astype(F32), jnp.where(down == 1, used, 0.0))
    block[rows:, :rows] = notes.astype(BF16)
    d_out[...] = (used_rows(info, rows) * cotangent[...].astype(F32)).astype(BF16)


def chunks_body(info, w_qkv, got_qkv, w_fc, got_fc, w_proj, lent, w_out, vectors, got_vectors, shifts, first, second):
    own_rows, width = w_proj.shape
    x, c, y = info[AT_X], info[AT_C], info[AT_Y]
    qkv = 3 * width // 4
    low = low_half((own_rows, LANES))
    for core in range(2):
        rows = slice(core * own_rows, (core + 1) * own_rows)
        mine = c == core
        for pair in range(w_qkv.shape[1] // (8 * HALF)):
            groups = []
            for z in range(2):
                at = pl.ds(pl.multiple_of((2 * pair + z) * 4 * HALF + x * LANES, LANES), LANES)
                groups.append(jnp.where(mine, w_qkv[:, at], got_qkv[:, at]).astype(F32))
            first[rows, pair * LANES : (pair + 1) * LANES] = join(c, *groups, low).astype(BF16)
        for p in range(w_fc.shape[1] // (4 * LANES)):
            at = pl.ds(pl.multiple_of(p * 4 * LANES + (2 * c + x) * LANES, LANES), LANES)
            second[rows, p * LANES : (p + 1) * LANES] = jnp.where(mine, w_fc[:, at], got_fc[:, at])
    half = jnp.where(x == y, w_proj[:, : width // 2], lent[:, width // 2 :])
    first[:own_rows, qkv:] = half[:, : width // 4]
    first[own_rows : 2 * own_rows, qkv:] = half[:, width // 4 :]
    piece = w_out.shape[0] // 2
    second[2 * own_rows :, :] = w_out[pl.ds(pl.multiple_of(x * piece, piece), piece), :]
    mine = vectors[...].astype(F32)
    other = got_vectors[...].astype(F32)
    lower = jnp.where(c == 0, mine[0:8], other[0:8])
    upper = jnp.where(c == 0, other[0:8], mine[0:8])
    blank = jnp.zeros(lower.shape, F32)
    small = jnp.concatenate([lower, blank], axis=1) + turn(jnp.concatenate([upper, blank], axis=1))
    heads = jnp.concatenate([mine[8:16], blank], axis=1)
    heads = heads + turn(jnp.concatenate([mine[16:24], blank], axis=1))
    both = shifts[...].astype(F32)
    shift = jnp.broadcast_to(jnp.where(x == 0, both[0:1], both[1:2]), small.shape)
    row = lax.broadcasted_iota(jnp.int32, small.shape, 0)
    small = jnp.where(row == 6, shift, jnp.where(row == 7, heads, small))
    first[2 * own_rows :, :] = jnp.zeros((SMALL_ROWS, width), BF16)
    first[2 * own_rows : 2 * own_rows + 8, :LANES] = small.astype(BF16)


def run_copies(copies, sems):
    started = []
    for i, (source, target) in enumerate(copies):
        copy = pltpu.make_async_copy(source, target, sems.at[i])
        copy.start()
        started.append(copy)
    return started


def attention_body(info, *refs):
    blocks, chunks = refs[:RANKS], refs[RANKS : RANKS + ORIGINS]
    normed, qkv, probs, context, send, keep_own, keep_away, qkv_weight, proj_weight, smalls = refs[
        RANKS + ORIGINS : RANKS + ORIGINS + 10
    ]
    masks, sems = refs[RANKS + ORIGINS + 10 :]
    x = info[AT_X]
    width = normed.shape[1]
    rows = normed.shape[0] // RANKS
    chip_rows = chunks[0].shape[0] - SMALL_ROWS
    own_rows = chip_rows // 2
    cols = 3 * width // 4
    copies = []
    for i, chunk in enumerate(chunks):
        at = info[i]
        start = chunks[i - 1].shape[0] if i == ORIGINS - 1 else 0
        stop = start + chunk.shape[0]
        for part in range(2):
            top = part * own_rows
            if start <= top and top + own_rows <= stop:
                source = pl.ds(top - start, own_rows)
                copies.append(
                    (
                        chunk.at[source, pl.ds(0, cols)],
                        qkv_weight.at[pl.ds(pl.multiple_of(at * chip_rows + top, own_rows), own_rows), :],
                    )
                )
                side = lax.rem(at + x, 2) * (width // 2) + part * (width // 4)
                copies.append(
                    (
                        chunk.at[source, pl.ds(cols, width // 4)],
                        proj_weight.at[
                            pl.ds(pl.multiple_of(lax.div(at, 2) * own_rows, own_rows), own_rows),
                            pl.ds(pl.multiple_of(side, LANES), width // 4),
                        ],
                    )
                )
        if stop > chip_rows:
            copies.append(
                (
                    chunk.at[pl.ds(chip_rows - start, SMALL_ROWS), pl.ds(0, LANES)],
                    smalls.at[:, pl.ds(pl.multiple_of(at * LANES, LANES), LANES)],
                )
            )
    started = run_copies(copies, sems)

    down = lax.broadcasted_iota(jnp.int32, (rows, rows), 0)
    across = lax.broadcasted_iota(jnp.int32, (rows, rows), 1)
    for b, block in enumerate(blocks):
        notes = block[rows : rows + SMALL_ROWS, : 2 * LANES].astype(F32)
        seg_row, use_row = notes[0:1, :rows], notes[1:2, :rows]
        seg_column = jnp.sum(jnp.where(down == across, seg_row, 0.0), axis=1, keepdims=True)
        visible = (seg_column == seg_row) & (across <= down) & (use_row > 0)
        masks[b] = jnp.where(visible, 1.0, 0.0)
    for copy in started:
        copy.wait()
    gain = smalls[0:1, :].astype(F32)
    shift = smalls[1:2, :].astype(F32)
    for b, block in enumerate(blocks):
        center, inverse = statistics(block[:rows, :].astype(F32))
        normed[b * rows : (b + 1) * rows, :] = (center * inverse * gain + shift).astype(BF16)

    low_row = low_half((8, LANES))
    biases = jnp.broadcast_to(smalls[7:8, :].astype(F32), (8, width))
    query_shift, value_shift = [], []
    for pair in range(2):
        first, second = (
            jnp.where(
                x == 0,
                biases[:, z * 2 * LANES : z * 2 * LANES + LANES],
                biases[:, z * 2 * LANES + LANES : (z + 1) * 2 * LANES],
            )
            for z in (2 * pair, 2 * pair + 1)
        )
        query_shift.append(jnp.where(low_row, first, turn(second))[0:1])
        value_shift.append(jnp.where(low_row, turn(first), second)[0:1])
    third = width // 4
    for n in range(3):
        product = dot(normed[...], qkv_weight[:, n * third : (n + 1) * third])
        if n != 1:
            product = product + jnp.concatenate(value_shift if n else query_shift, axis=1)
        qkv[:, n * third : (n + 1) * third] = product.astype(BF16)

    scale = HALF ** (-0.5)
    low = low_half((1, LANES))
    keep_low = jnp.where(low, 1.0, 0.0).astype(BF16)
    keep_high = jnp.where(low, 0.0, 1.0).astype(BF16)

    def attend(b, carry):
        at = pl.ds(pl.multiple_of(b * rows, rows), rows)
        mask = masks[b] > 0.5
        for pair in range(2):
            lanes = pair * LANES
            queries = qkv[at, lanes : lanes + LANES]
            keys = qkv[at, third + lanes : third + lanes + LANES]
            values = qkv[at, 2 * third + lanes : 2 * third + lanes + LANES]
            outs = []
            for side, keep in enumerate((keep_low, keep_high)):
                scores = jnp.where(mask, scale * dot_cols(queries * keep, keys), -1e30)
                expo = jnp.exp(scores - jnp.max(scores, axis=-1, keepdims=True))
                share = (expo / jnp.sum(expo, axis=-1, keepdims=True)).astype(BF16)
                probs[b * 4 + 2 * pair + side] = share
                outs.append(dot(share, values))
            context[at, lanes : lanes + LANES] = jnp.where(low, outs[0], outs[1]).astype(BF16)
        return carry

    lax.fori_loop(0, RANKS, attend, 0)
    for n in range(4):
        columns = slice(n * third, (n + 1) * third)
        store_parts(dot(context[...], proj_weight[:, columns]), columns, rows, send, keep_own, keep_away)


def store_parts(product, columns, rows, send, keep_own, keep_away):
    keep_own[:, columns] = product[:rows]
    send[0, :, columns] = product[rows : 2 * rows].astype(BF16)
    keep_away[:, columns] = product[2 * rows : 3 * rows]
    send[1, :, columns] = product[3 * rows :].astype(BF16)


def total(keep_own, near, away):
    return keep_own[...] + near[0].astype(F32) + away[...].astype(F32)


def second_norm_body(tokens, keep_own, near, away, smalls, middle, normed):
    values = tokens[...].astype(F32) + smalls[2:3, :].astype(F32) + total(keep_own, near, away)
    middle[...] = values
    center, inverse = statistics(values)
    gain, shift = smalls[3:4, :].astype(F32), smalls[4:5, :].astype(F32)
    normed[...] = (center * inverse * gain + shift).astype(BF16)


def feed_body(info, *refs):
    inputs, d_outs = refs[:RANKS], refs[RANKS : 2 * RANKS]
    chunks, smalls = refs[2 * RANKS : 2 * RANKS + ORIGINS], refs[2 * RANKS + ORIGINS]
    given, d_out, hidden, d_pre, send, keep_own, keep_away, sums, out_weight = refs[
        2 * RANKS + ORIGINS + 1 : 2 * RANKS + ORIGINS + 10
    ]
    fc_weight, sems = refs[2 * RANKS + ORIGINS + 10 :]
    rows = inputs[0].shape[0]
    width = given.shape[1]
    chip_rows = chunks[0].shape[0] // 2
    copies = []
    for i, chunk in enumerate(chunks):
        at = pl.ds(pl.multiple_of(info[i] * chip_rows, chip_rows), chip_rows)
        if i != ORIGINS - 1:
            copies.append((chunk.at[pl.ds(0, chip_rows), :], fc_weight.at[at, :]))
        if i != ORIGINS - 2:
            start = 0 if i == ORIGINS - 1 else chip_rows
            copies.append((chunk.at[pl.ds(start, chip_rows), :], out_weight.at[at, :]))
    started = run_copies(copies, sems)
    for b in range(RANKS):
        given[b * rows : (b + 1) * rows, :] = inputs[b][...]
        d_out[b * rows : (b + 1) * rows, :] = d_outs[b][...]
    for copy in started:
        copy.wait()
    tile = 2 * LANES
    root = (2.0 / jnp.pi) ** 0.5
    sums[...] = jnp.zeros(sums.shape, F32)

    def units(n, carry):
        columns = pl.ds(pl.multiple_of(n * tile, tile), tile)
        pre = dot(given[...], fc_weight[:, columns]) + smalls[6:7, columns].astype(F32)
        d_hidden = dot_cols(d_out[...], out_weight[columns, :])
        square = pre * pre
        bend = jnp.tanh(root * pre * (1.0 + 0.044715 * square))
        hidden[:, columns] = (0.5 * pre * (1.0 + bend)).astype(BF16)
        slope = 0.5 * (1.0 + bend) + 0.5 * pre * (1.0 - bend * bend) * root * (
            1.0 + 3.0 * 0.044715 * square
        )
        low = (d_hidden * slope).astype(BF16)
        d_pre[:, columns] = low
        sums[6:7, columns] = jnp.sum(low.astype(F32), axis=0, keepdims=True)
        return carry

    lax.fori_loop(0, width // tile, units, 0)
    for n in range(width // tile):
        columns = slice(n * tile, (n + 1) * tile)
        product = dot_cols(d_pre[...], fc_weight[columns, :])
        store_parts(product, columns, rows, send, keep_own, keep_away)


def feed_out_body(hidden, out_weight, send, keep_own, keep_away):
    rows = keep_own.shape[0]
    tile = 2 * LANES
    for n in range(out_weight.shape[1] // tile):
        columns = slice(n * tile, (n + 1) * tile)
        store_parts(dot(hidden[...], out_weight[:, columns]), columns, rows, send, keep_own, keep_away)


def mixed_body(info, middle, keep_own, near, away, smalls, mixed):
    values = middle[...] + total(keep_own, near, away) + smalls[5:6, :].astype(F32)
    mixed[...] = (used_rows(info, middle.shape[0]) * values).astype(BF16)


def second_back_body(info, middle, cotangent, keep_own, near, away, smalls, d_middle, d_branch, sums):
    d_values = total(keep_own, near, away)
    d_top = used_rows(info, middle.shape[0]) * cotangent[...].astype(F32)
    center, inverse = statistics(middle[...])
    unit = center * inverse
    result = d_top + norm_back(unit, inverse, d_values * smalls[3:4, :].astype(F32))
    d_middle[...] = result
    low = result.astype(BF16)
    d_branch[...] = low
    sums[...] = jnp.zeros(sums.shape, F32)
    sums[2:3, :] = jnp.sum(low.astype(F32), axis=0, keepdims=True)
    sums[3:4, :] = jnp.sum(d_values * unit, axis=0, keepdims=True)
    sums[4:5, :] = jnp.sum(d_values, axis=0, keepdims=True)
    sums[5:6, :] = jnp.sum(d_top, axis=0, keepdims=True)


def attention_back_body(info, *refs):
    d_branches, blocks = refs[:RANKS], refs[RANKS : 2 * RANKS]
    qkv, probs, qkv_weight, proj_weight, sums_two, sums_fc = refs[2 * RANKS : 2 * RANKS + 6]
    d_branch, d_qkv, send, keep_own, keep_away, sums = refs[2 * RANKS + 6 : 2 * RANKS + 12]
    (d_context,) = refs[2 * RANKS + 12 :]
    rows = d_branches[0].shape[0]
    width = d_branch.shape[1]
    third = width // 4
    x = info[AT_X]
    for b in range(RANKS):
        d_branch[b * rows : (b + 1) * rows, :] = d_branches[b][...]
    d_context[...] = dot_cols(d_branch[...], proj_weight[...]).astype(BF16)
    scale = HALF ** (-0.5)
    low = low_half((1, LANES))
    keep_low = jnp.where(low, 1.0, 0.0).astype(BF16)
    keep_high = jnp.where(low, 0.0, 1.0).astype(BF16)

    def attend(b, carry):
        at = pl.ds(pl.multiple_of(b * rows, rows), rows)
        for pair in range(2):
            lanes = pair * LANES
            queries = qkv[at, lanes : lanes + LANES]
            keys = qkv[at, third + lanes : third + lanes + LANES]
            values = qkv[at, 2 * third + lanes : 2 * third + lanes + LANES]
            d_out = d_context[at, lanes : lanes + LANES]
            results = []
            for side, keep in enumerate((keep_low, keep_high)):
                share = probs[b * 4 + 2 * pair + side]
                wide = share.astype(F32)
                d_values = dot_rows(share, d_out)
                d_probs = dot_cols(d_out * keep, values)
                d_scores = wide * (d_probs - jnp.sum(wide * d_probs, axis=-1, keepdims=True))
                d_scores = d_scores.astype(BF16)
                results.append(
                    (scale * dot(d_scores, keys), scale * dot_rows(d_scores, queries), d_values)
                )
            for n in range(3):
                merged = jnp.where(low, results[0][n], results[1][n]).astype(BF16)
                d_qkv[at, n * third + lanes : n * third + lanes + LANES] = merged
        return carry

    lax.fori_loop(0, RANKS, attend, 0)
    sums[0:8, :] = sums_two[...] + sums_fc[...]
    sums[8:, :] = jnp.zeros((SMALL_ROWS - 8, width), F32)
    stats = []
    for block in blocks:
        values = block[:rows, :].astype(F32)
        mean = jnp.mean(values, axis=-1, keepdims=True)
        center = values - mean
        stats.append((mean, lax.rsqrt(jnp.mean(center * center, axis=-1, keepdims=True) + 1e-05)))
    for n in range(4):
        columns = slice(n * third, (n + 1) * third)
        product = dot_cols(d_qkv[...], qkv_weight[columns, :])
        store_parts(product, columns, rows, send, keep_own, keep_away)
        sums[1:2, columns] = jnp.sum(product, axis=0, keepdims=True)
        along = jnp.zeros((1, third), F32)
        for b, block in enumerate(blocks):
            mean, inverse = stats[b]
            unit = (block[:rows, columns].astype(F32) - mean) * inverse
            along = along + jnp.sum(product[b * rows : (b + 1) * rows] * unit, axis=0, keepdims=True)
        sums[0:1, columns] = along
    low_row = low_half((8, LANES))
    for pair in range(2):
        lanes = pair * LANES
        d_queries = jnp.sum(d_qkv[:, lanes : lanes + LANES].astype(F32), axis=0, keepdims=True)
        d_values = jnp.sum(
            d_qkv[:, 2 * third + lanes : 2 * third + lanes + LANES].astype(F32), axis=0, keepdims=True
        )
        d_queries = jnp.broadcast_to(d_queries, (8, LANES))
        d_values = jnp.broadcast_to(d_values, (8, LANES))
        even = jnp.where(low_row, d_queries, turn(d_values))[0:1]
        odd = jnp.where(low_row, turn(d_queries), d_values)[0:1]
        for z, group in ((2 * pair, even), (2 * pair + 1, odd)):
            for y in range(2):
                start = (2 * z + y) * LANES
                sums[7:8, start : start + LANES] = jnp.where(x == y, group, 0.0)


def first_back_body(tokens, d_middle, keep_own, near, away, smalls, result):
    center, inverse = statistics(tokens[...].astype(F32))
    d_unit = total(keep_own, near, away) * smalls[0:1, :].astype(F32)
    result[...] = d_middle[...] + norm_back(center * inverse, inverse, d_unit)


def second_term(info, index, grad_fc, grad_out):
    at = info[index]
    results = []
    for grad in (grad_fc, grad_out):
        chip_rows = grad.shape[0] * 2 // HEADS
        results.append(grad[pl.ds(pl.multiple_of(at * chip_rows, chip_rows), chip_rows), :])
    return results


def add(left, right):
    return (left.astype(F32) + right.astype(F32)).astype(BF16)


def second_far_body(info, grad_fc, grad_out, forth, back):
    forth[...], back[...] = second_term(info, ORIGINS - 1, grad_fc, grad_out)


def second_hop_body(step, info, got_forth, got_back, grad_fc, grad_out, forth, back):
    rows = forth.shape[0] // 2
    for target, got, index, part in ((forth, got_forth, 2 * step, 0), (back, got_back, 2 * step - 1, 1)):
        terms = second_term(info, index, grad_fc, grad_out)
        for i in range(2):
            where = slice(i * rows, (i + 1) * rows)
            if got.shape[0] == rows:
                target[where, :] = add(terms[i], got[...]) if i == part else terms[i]
            else:
                target[where, :] = add(terms[i], got[where, :])


def second_last_body(info, got_forth, got_back, grad_fc, grad_out, own):
    terms = second_term(info, 0, grad_fc, grad_out)
    rows = own.shape[0] // 2
    for i in range(2):
        where = slice(i * rows, (i + 1) * rows)
        values = got_forth[where, :].astype(F32) + got_back[where, :].astype(F32)
        own[where, :] = add(values, terms[i])


def first_term(info, index, grad_qkv, grad_proj, sums):
    at = info[index]
    chip_rows = grad_qkv.shape[0] * 2 // HEADS
    own_rows = chip_rows // 2
    quarter = grad_proj.shape[1] // 4
    side = lax.rem(at + info[AT_X], 2) * 2 * quarter
    head = pl.ds(pl.multiple_of(lax.div(at, 2) * own_rows, own_rows), own_rows)
    results = []
    for part in range(2):
        rows = pl.ds(pl.multiple_of(at * chip_rows + part * own_rows, own_rows), own_rows)
        lanes = pl.ds(pl.multiple_of(side + part * quarter, LANES), quarter)
        results.append((grad_qkv[rows, :], grad_proj[head, lanes]))
    small = sums[:, pl.ds(pl.multiple_of(at * LANES, LANES), LANES)].astype(BF16)
    return results, small


def put_first(target, row, values, got, got_row):
    at = 0
    rows = values[0].shape[0]
    for value in values:
        lanes = slice(at, at + value.shape[1])
        if got is not None:
            value = add(value, got[got_row : got_row + rows, lanes])
        target[row : row + rows, lanes] = value
        at += value.shape[1]


def first_far_body(info, grad_qkv, grad_proj, sums, forth, back):
    (upper, lower), small = first_term(info, ORIGINS - 1, grad_qkv, grad_proj, sums)
    own_rows = forth.shape[0]
    put_first(forth, 0, upper, None, 0)
    put_first(back, 0, lower, None, 0)
    back[own_rows:, :] = jnp.zeros((SMALL_ROWS, back.shape[1]), BF16)
    put_first(back, own_rows, (small,), None, 0)


def first_hop_body(step, info, got_forth, got_back, grad_qkv, grad_proj, sums, forth, back):
    own_rows = (forth.shape[0] - SMALL_ROWS) // 2
    for target, got, index in ((forth, got_forth, 2 * step), (back, got_back, 2 * step - 1)):
        terms, small = first_term(info, index, grad_qkv, grad_proj, sums)
        shift = 0
        if got.shape[0] == own_rows:
            came = (got, None, None)
        elif got.shape[0] == own_rows + SMALL_ROWS:
            came, shift = (None, got, got), own_rows
        else:
            came = (got, got, got)
        target[2 * own_rows :, :] = jnp.zeros((SMALL_ROWS, target.shape[1]), BF16)
        for i, values in enumerate((*terms, (small,))):
            put_first(target, i * own_rows, values, came[i], i * own_rows - shift)


def first_last_body(info, got_forth, got_back, grad_qkv, grad_proj, sums, own):
    own_rows = (own.shape[0] - SMALL_ROWS) // 2
    terms, small = first_term(info, 0, grad_qkv, grad_proj, sums)
    own[2 * own_rows :, :] = jnp.zeros((SMALL_ROWS, own.shape[1]), BF16)
    for i, values in enumerate((*terms, (small,))):
        at = 0
        rows = slice(i * own_rows, i * own_rows + values[0].shape[0])
        for value in values:
            lanes = slice(at, at + value.shape[1])
            came = got_forth[rows, lanes].astype(F32) + got_back[rows, lanes].astype(F32)
            own[rows, lanes] = add(came, value)
            at += value.shape[1]


def four_parts(info, own, near, other, cross):
    x, c = info[AT_X], info[AT_C]

    def reader(copy, core):
        def read(rows, lanes):
            same = jnp.where(c == core, own[rows, lanes], near[rows, lanes])
            far = jnp.where(c == core, other[rows, lanes], cross[rows, lanes])
            return jnp.where(x == copy, same, far).astype(F32)

        return read

    return reader


def hidden_grads_body(info, own, near, other, cross, grad_fc, grad_out):
    x, c = info[AT_X], info[AT_C]
    own_rows = grad_fc.shape[0]
    width = own.shape[1]
    piece = grad_out.shape[0] // 2
    reader = four_parts(info, own, near, other, cross)
    rows = pl.ds(pl.multiple_of(c * own_rows, own_rows), own_rows)
    for copy in range(2):
        for core in range(2):
            read = reader(copy, core)
            for p in range(width // LANES):
                at = p * 4 * LANES + core * 2 * LANES + copy * LANES
                grad_fc[:, at : at + LANES] = read(rows, slice(p * LANES, (p + 1) * LANES))
        grad_out[copy * piece : (copy + 1) * piece, :] = jnp.where(
            x == copy, own[2 * own_rows :, :], other[2 * own_rows :, :]
        ).astype(F32)


def first_grads_body(info, own, near, other, cross, given, grad_qkv, grad_proj, *small_outs):
    x, c, y = info[AT_X], info[AT_C], info[AT_Y]
    own_rows, width = grad_proj.shape
    qkv = 3 * width // 4
    quarter = width // 4
    low = low_half((own_rows, LANES))
    reader = four_parts(info, own, near, other, cross)
    rows = pl.ds(pl.multiple_of(c * own_rows, own_rows), own_rows)
    for copy in range(2):
        first, second = reader(copy, 0), reader(copy, 1)
        for pair in range(qkv // LANES):
            lanes = slice(pair * LANES, (pair + 1) * LANES)
            one, two = first(rows, lanes), second(rows, lanes)
            at = pair * 8 * HALF + copy * LANES
            grad_qkv[:, at : at + LANES] = jnp.where(low, one, turn(two))
            at += 4 * HALF
            grad_qkv[:, at : at + LANES] = jnp.where(low, turn(one), two)
    for part in range(2):
        block = slice(part * own_rows, (part + 1) * own_rows)
        left = jnp.where(x == y, own[block, qkv:], other[block, qkv:]).astype(F32)
        grad_proj[:, part * quarter : (part + 1) * quarter] = left
        right = given[block, :].astype(F32)
        grad_proj[:, 2 * quarter + part * quarter : 2 * quarter + (part + 1) * quarter] = right
    mine, side, far, corner = (
        ref[2 * own_rows :, :LANES].astype(F32) for ref in (own, near, other, cross)
    )
    summed = (mine + side) + (far + corner)
    summed = jnp.where(c == 0, summed, turn(summed))
    heads = jnp.where(x == y, mine, far)
    for i in range(6):
        small_outs[i][...] = summed[i : i + 1, :HALF]
    small_outs[6][0:1, :] = jnp.where(x == 0, mine, far)[6:7]
    small_outs[6][1:2, :] = jnp.where(x == 0, far, mine)[6:7]
    small_outs[7][...] = heads[7:8, :HALF]
    small_outs[8][...] = turn(heads)[7:8, :HALF]


def tie(*values):
    return lax.optimization_barrier(values)


def make_kernel_local(n_replica, n_shard):
    n_pos = n_shard // 2
    half = n_pos // 2

    def every(move):
        pairs = []
        for r in range(n_replica):
            for p in range(n_pos):
                for c in range(2):
                    to = move(r, p, c)
                    pairs.append((r * n_shard + p * 2 + c, to[0] * n_shard + to[1] * 2 + to[2]))
        return pairs

    ring = list(range(0, n_pos, 2)) + list(range(n_pos - 1, 0, -2))
    after = {p: ring[(i + 1) % n_pos] for i, p in enumerate(ring)}
    before = {p: ring[i - 1] for i, p in enumerate(ring)}

    def mover(move):
        pairs = every(move)
        return lambda v: lax.ppermute(v, MESH_AXES, pairs)

    to_core = mover(lambda r, p, c: (r, p, 1 - c))
    to_copy = mover(lambda r, p, c: (r ^ 1, p, c))
    to_next = mover(lambda r, p, c: (r, after[p], c))
    to_back = mover(lambda r, p, c: (r, before[p], c))
    to_side = mover(lambda r, p, c: (r, p ^ 1, c))

    def local(
        tokens,
        segments,
        counts,
        ln1_gain,
        ln1_bias,
        w_qkv,
        bias_query,
        bias_value,
        w_proj,
        bias_proj,
        ln2_gain,
        ln2_bias,
        w_fc,
        bias_fc,
        w_out,
        bias_out,
        cotangent,
    ):
        rows, width = tokens.shape
        own_rows = width // n_shard
        chip_rows = 2 * own_rows
        piece = w_out.shape[0] // 2
        units = n_pos * piece
        all_rows = RANKS * rows
        qkv_cols = 3 * width // 4
        first_shape = ((chip_rows + SMALL_ROWS, width), BF16)
        second_shape = ((chip_rows + piece, width), BF16)
        replica_at = lax.axis_index("replica")
        shard_at = lax.axis_index("shard")
        x, c, p = replica_at % 2, shard_at % 2, shard_at // 2
        place = jnp.where(p % 2 == 0, p // 2, n_pos - 1 - p // 2)

        def origin(index):
            index = index % n_pos
            return jnp.where(index < half, 2 * index, 2 * (n_pos - 1 - index) + 1)

        offsets = [0]
        for step in range(1, half):
            offsets += [-step, step]
        offsets += [half, half]
        info = jnp.stack(
            [origin(place + offset) for offset in offsets] + [x, c, p % 2, counts[0]]
        ).astype(jnp.int32)

        got_qkv, got_fc, lent = to_core(w_qkv), to_core(w_fc), to_side(w_proj)
        none = jnp.zeros((own_rows,), BF16)
        vectors = jnp.stack(
            [ln1_gain, ln1_bias, bias_proj, ln2_gain, ln2_bias, bias_out]
            + [none] * 9
            + [bias_query]
            + [none] * 7
            + [bias_value]
        )
        got_vectors = to_core(vectors)
        block, d_top = kernel_call(
            tokens_body,
            [SMEM_SPEC] + [VMEM_SPEC] * 3,
            [((rows + SMALL_ROWS, width), BF16), ((rows, width), BF16)],
        )(info, tokens, segments.reshape(1, rows), cotangent)
        first_chunk, second_chunk = kernel_call(
            chunks_body, [SMEM_SPEC] + [VMEM_SPEC] * 10, [first_shape, second_shape], micros=2
        )(
            info, w_qkv, got_qkv, w_fc, got_fc, w_proj, lent, w_out, vectors, got_vectors,
            bias_fc.reshape(2, piece),
        )

        firsts = [first_chunk]
        forth, back = to_next(first_chunk), to_back(first_chunk)
        block_other = to_copy(block)
        for step in range(1, half):
            firsts += [forth, back]
            if step < half - 1:
                forth, back = to_next(forth), to_back(back)
            if step == 1:
                block_other, d_top, forth, back = tie(block_other, d_top, forth, back)
                blocks = [block, to_core(block), block_other, to_core(block_other)]
                d_other = to_copy(d_top)
            if step == half - 2:
                second_chunk, forth, back = tie(second_chunk, forth, back)
                seconds = [second_chunk]
                second_forth, second_back = to_next(second_chunk), to_back(second_chunk)
        d_outs = [d_top, to_core(d_top), d_other, to_core(d_other)]
        firsts += [to_next(forth[:own_rows]), to_back(back[own_rows:])]

        parts = [((2, rows, width), BF16), ((rows, width), F32), ((rows, width), F32)]
        tied = tie(*firsts, *blocks, *d_outs)
        firsts, blocks, d_outs = tied[:ORIGINS], tied[ORIGINS : ORIGINS + RANKS], tied[ORIGINS + RANKS :]
        normed, qkv, probs, context, send, keep_own, keep_away, qkv_weight, proj_weight, smalls = kernel_call(
            attention_body,
            [SMEM_SPEC] + [VMEM_SPEC] * RANKS + [ANY_SPEC] * ORIGINS,
            [
                ((all_rows, width), BF16),
                ((all_rows, qkv_cols), BF16),
                ((4 * RANKS, rows, rows), BF16),
                ((all_rows, width // 4), BF16),
                *parts,
                ((width, qkv_cols), BF16),
                ((width // 4, width), BF16),
                ((SMALL_ROWS, width), BF16),
            ],
            [pltpu.VMEM((RANKS, rows, rows), F32), pltpu.SemaphoreType.DMA((5 * n_pos,))],
            micros=8,
        )(info, *blocks, *firsts)
        send, second_forth, second_back = tie(send, second_forth, second_back)
        seconds += [second_forth, second_back]
        near = to_core(send)
        second_forth, second_back = to_next(second_forth), to_back(second_back)
        away = to_copy(add(keep_away, near[1]))
        away, second_forth, second_back = tie(away, second_forth, second_back)
        seconds += [second_forth, second_back]
        middle, normed_two = kernel_call(
            second_norm_body, [VMEM_SPEC] * 5, [((rows, width), F32), ((rows, width), BF16)]
        )(tokens, keep_own, near, away, smalls)
        second_forth, second_back = to_next(second_forth), to_back(second_back)
        other = to_copy(normed_two)
        beside = to_core(normed_two)
        other, beside, second_forth, second_back = tie(other, beside, second_forth, second_back)
        seconds += [second_forth, second_back]
        seconds += [to_next(second_forth[:chip_rows]), to_back(second_back[chip_rows:])]
        inputs = [normed_two, beside, other, to_core(other)]

        given, d_out, hidden, d_pre, send, keep_own, keep_away, sums_fc, out_weight = kernel_call(
            feed_body,
            [SMEM_SPEC] + [VMEM_SPEC] * (2 * RANKS) + [ANY_SPEC] * ORIGINS + [VMEM_SPEC],
            [
                ((all_rows, width), BF16),
                ((all_rows, width), BF16),
                ((all_rows, units), BF16),
                ((all_rows, units), BF16),
                *parts,
                ((8, units), F32),
                ((units, width), BF16),
            ],
            [pltpu.VMEM((width, units), BF16), pltpu.SemaphoreType.DMA((2 * n_pos,))],
            micros=10,
        )(info, *inputs, *d_outs, *seconds, smalls)

        near = to_core(send)
        near, given, d_out, hidden, d_pre = tie(near, given, d_out, hidden, d_pre)
        away = to_copy(add(keep_away, near[1]))
        grad_w_out = dot_rows(hidden, d_out).astype(BF16)
        grad_w_fc = dot_rows(given, d_pre).astype(BF16)
        away, grad_w_out, grad_w_fc = tie(away, grad_w_out, grad_w_fc)
        far_forth, far_back = kernel_call(
            second_far_body,
            [SMEM_SPEC] + [VMEM_SPEC] * 2,
            [((chip_rows, width), BF16), ((piece, width), BF16)],
        )(info, grad_w_fc, grad_w_out)
        far_forth, far_back = to_next(far_forth), to_back(far_back)

        def second_hop(step, got_forth, got_back):
            forth, back = kernel_call(
                functools.partial(second_hop_body, step),
                [SMEM_SPEC] + [VMEM_SPEC] * 4,
                [second_shape, second_shape],
            )(info, got_forth, got_back, grad_w_fc, grad_w_out)
            return to_next(forth), to_back(back)

        d_middle, d_branch, sums_two = kernel_call(
            second_back_body,
            [SMEM_SPEC] + [VMEM_SPEC] * 6,
            [((rows, width), F32), ((rows, width), BF16), ((8, width), F32)],
        )(info, middle, cotangent, keep_own, near, away, smalls)
        other, beside = to_copy(d_branch), to_core(d_branch)
        hidden, out_weight, d_branch = tie(hidden, out_weight, d_branch)
        mix_send, mix_keep, mix_away = kernel_call(
            feed_out_body, [VMEM_SPEC] * 2, parts, micros=2
        )(hidden, out_weight)
        mix_near = to_core(mix_send)
        other, beside, far_forth, far_back, mix_near = tie(
            other, beside, far_forth, far_back, mix_near
        )
        d_branches = [d_branch, beside, other, to_core(other)]
        second_forth, second_back = second_hop(half - 1, far_forth, far_back)
        mix_away = to_copy(add(mix_away, mix_near[1]))

        d_branch, d_qkv, send, keep_own, keep_away, sums = kernel_call(
            attention_back_body,
            [SMEM_SPEC] + [VMEM_SPEC] * (2 * RANKS + 6),
            [
                ((all_rows, width), BF16),
                ((all_rows, qkv_cols), BF16),
                *parts,
                ((SMALL_ROWS, width), F32),
            ],
            [pltpu.VMEM((all_rows, width // 4), BF16)],
            micros=9,
        )(info, *d_branches, *blocks, qkv, probs, qkv_weight, proj_weight, sums_two, sums_fc)
        send, d_branch, d_qkv, second_forth, second_back, mix_away = tie(
            send, d_branch, d_qkv, second_forth, second_back, mix_away
        )
        second_forth, second_back = second_hop(half - 2, second_forth, second_back)
        grad_w_proj = dot_rows(context, d_branch).astype(BF16)
        grad_w_qkv = dot_rows(normed, d_qkv).astype(BF16)
        firsts = (grad_w_qkv, grad_w_proj, sums)
        forth, back = kernel_call(
            first_far_body,
            [SMEM_SPEC] + [VMEM_SPEC] * 3,
            [((own_rows, width), BF16), ((own_rows + SMALL_ROWS, width), BF16)],
        )(info, *firsts)
        near = to_core(send)
        forth, back = to_next(forth), to_back(back)
        (mixed,) = kernel_call(mixed_body, [SMEM_SPEC] + [VMEM_SPEC] * 5, [((rows, width), BF16)])(
            info, middle, mix_keep, mix_near, mix_away, smalls
        )
        away = to_copy(add(keep_away, near[1]))
        for step in range(half - 1, 0, -1):
            forth, back = kernel_call(
                functools.partial(first_hop_body, step),
                [SMEM_SPEC] + [VMEM_SPEC] * 5,
                [first_shape, first_shape],
            )(info, forth, back, *firsts)
            forth, back = to_next(forth), to_back(back)
            if step == half - 1:
                second_forth, second_back, mixed = tie(second_forth, second_back, mixed)
                for last in range(half - 3, 0, -1):
                    second_forth, second_back = second_hop(last, second_forth, second_back)
                forth, back, away = tie(forth, back, away)
            elif step == half - 2:
                forth, back, second_forth, second_back = tie(forth, back, second_forth, second_back)
                (own_second,) = kernel_call(
                    second_last_body, [SMEM_SPEC] + [VMEM_SPEC] * 4, [second_shape]
                )(info, second_forth, second_back, grad_w_fc, grad_w_out)
                near_second, other_second = to_core(own_second), to_copy(own_second)
        (own_first,) = kernel_call(
            first_last_body, [SMEM_SPEC] + [VMEM_SPEC] * 5, [first_shape]
        )(info, forth, back, *firsts)
        near_first, other_first = to_core(own_first), to_copy(own_first)
        (grad_tokens,) = kernel_call(first_back_body, [VMEM_SPEC] * 6, [((rows, width), F32)])(
            tokens, d_middle, keep_own, near, away, smalls
        )

        grad_w_fc, grad_w_out = kernel_call(
            hidden_grads_body,
            [SMEM_SPEC] + [VMEM_SPEC] * 4,
            [((own_rows, 4 * units), F32), ((2 * piece, width), F32)],
        )(info, own_second, near_second, other_second, to_core(other_second))

        given = jnp.where(
            x == p % 2, other_first[:chip_rows, qkv_cols:], own_first[:chip_rows, qkv_cols:]
        )
        vector_shape = ((1, own_rows), F32)
        grad_w_qkv, grad_w_proj, *small = kernel_call(
            first_grads_body,
            [SMEM_SPEC] + [VMEM_SPEC] * 5,
            [((own_rows, 3 * width), F32), ((own_rows, width), F32)]
            + [vector_shape] * 6
            + [((2, piece), F32)]
            + [vector_shape] * 2,
        )(info, own_first, near_first, other_first, to_core(other_first), to_side(given))
        small = [value.reshape(-1) for value in small]
        return (
            mixed,
            grad_tokens,
            small[0],
            small[1],
            grad_w_qkv,
            small[7],
            small[8],
            grad_w_proj,
            small[2],
            small[3],
            small[4],
            grad_w_fc,
            small[6],
            grad_w_out,
            small[5],
        )

    return local


def solution(mesh):
    tokens_spec = P(MESH_AXES, None)
    slots_spec = P(MESH_AXES)
    rows_spec = P("shard", None)
    vector_spec = P("shard")
    in_specs = (
        tokens_spec,
        slots_spec,
        slots_spec,
        vector_spec,
        vector_spec,
        rows_spec,
        vector_spec,
        vector_spec,
        rows_spec,
        vector_spec,
        vector_spec,
        vector_spec,
        rows_spec,
        vector_spec,
        rows_spec,
        vector_spec,
        tokens_spec,
    )
    out_specs = (
        tokens_spec,
        tokens_spec,
        vector_spec,
        vector_spec,
        rows_spec,
        vector_spec,
        vector_spec,
        rows_spec,
        vector_spec,
        vector_spec,
        vector_spec,
        rows_spec,
        vector_spec,
        rows_spec,
        vector_spec,
    )
    n_replica, n_shard = mesh.shape["replica"], mesh.shape["shard"]
    make = make_kernel_local if (n_replica, n_shard) == (2, HEADS) else make_local
    local = make(n_replica, n_shard)
    return jax.shard_map(local, mesh=mesh, in_specs=in_specs, out_specs=out_specs, check_vma=False)
```

```python
import functools

import jax
import jax.numpy as jnp
from jax import lax
from jax.experimental import pallas as pl
from jax.experimental.pallas import tpu as pltpu
from jax.sharding import PartitionSpec as P

HEADS = 16
RANKS = 4
MESH_AXES = ("replica", "shard")
BF16 = jnp.bfloat16
F32 = jnp.float32
SMALL_ROWS = 16


def layer_norm(values, gain, shift):
    center = values - jnp.mean(values, axis=-1, keepdims=True)
    spread = jnp.mean(center * center, axis=-1, keepdims=True)
    return center * lax.rsqrt(spread + 1e-05) * gain + shift


def unit_norm(values):
    center = values - jnp.mean(values, axis=-1, keepdims=True)
    spread = jnp.mean(center * center, axis=-1, keepdims=True)
    return center * lax.rsqrt(spread + 1e-05)


def smooth_gate(values):
    return jax.nn.gelu(values, approximate=True)


def dot_rows(left, right):
    return lax.dot_general(left, right, (((0,), (0,)), ((), ())), preferred_element_type=F32)


def dot_cols(left, right):
    return lax.dot_general(left, right, (((1,), (1,)), ((), ())), preferred_element_type=F32)


def dot(left, right):
    return jnp.dot(left, right, preferred_element_type=F32)


def make_local(n_replica, n_shard):
    n_pos = n_shard // 2
    half = n_pos // 2
    head_a_shard = n_shard == HEADS
    n_pairs = n_replica // 2
    pair_groups = [[2 * i + j for i in range(n_pairs)] for j in range(2)]

    def every(move):
        pairs = []
        for r in range(n_replica):
            for p in range(n_pos):
                for c in range(2):
                    to = move(r, p, c)
                    if to is not None:
                        pairs.append((r * n_shard + p * 2 + c, to[0] * n_shard + to[1] * 2 + to[2]))
        return pairs

    ring = list(range(0, n_pos, 2)) + list(range(n_pos - 1, 0, -2))
    after = {p: ring[(i + 1) % n_pos] for i, p in enumerate(ring)}
    before = {p: ring[i - 1] for i, p in enumerate(ring)}
    core_pairs = every(lambda r, p, c: (r, p, 1 - c))
    copy_pairs = every(lambda r, p, c: (r ^ 1, p, c))
    next_pairs = every(lambda r, p, c: (r, after[p], c))
    back_pairs = every(lambda r, p, c: (r, before[p], c))
    lend_pairs = every(lambda r, p, c: (r, p ^ 1, c) if p % 2 == r % 2 else None)
    give_pairs = every(lambda r, p, c: (r, p ^ 1, c) if p % 2 != r % 2 else None)
    share_pairs = every(lambda r, p, c: (r ^ 1, p, c) if p % 2 == r % 2 else None)

    def to_core(v):
        return lax.ppermute(v, MESH_AXES, core_pairs)

    def to_copy(v):
        return lax.ppermute(v, MESH_AXES, copy_pairs)

    def to_next(v):
        return lax.ppermute(v, MESH_AXES, next_pairs)

    def to_back(v):
        return lax.ppermute(v, MESH_AXES, back_pairs)

    def cut(rows):
        return max(16, rows // 32 * 16)

    def ring_gather(chunk, place, origin):
        low = cut(chunk.shape[0])
        full = jnp.zeros((n_pos,) + chunk.shape, chunk.dtype)

        def put(full, value, offset, row=0):
            return lax.dynamic_update_slice(full, value[None], (origin(place + offset), row, 0))

        full = put(full, chunk, 0)
        forth = back = chunk
        for step in range(1, half):
            forth = to_next(forth)
            back = to_back(back)
            full = put(full, forth, -step)
            full = put(full, back, step)
        forth = to_next(forth[:low])
        back = to_back(back[low:])
        full = put(full, forth, half)
        full = put(full, back, half, low)
        return full

    def ring_scatter(full, place, origin):
        low = cut(full.shape[1])

        def term(offset):
            return lax.dynamic_index_in_dim(full, origin(place + offset), 0, keepdims=False)

        def add(left, right):
            return (left.astype(F32) + right.astype(F32)).astype(BF16)

        far = term(half)
        forth = to_next(far[:low])
        back = to_back(far[low:])
        ahead = term(half - 1)
        behind = term(1 - half)
        forth = to_next(jnp.concatenate([add(forth, ahead[:low]), ahead[low:]]))
        back = to_back(jnp.concatenate([behind[:low], add(back, behind[low:])]))
        for step in range(half - 2, 0, -1):
            forth = to_next(add(forth, term(step)))
            back = to_back(add(back, term(-step)))
        return term(0).astype(F32) + forth.astype(F32) + back.astype(F32)

    def group_gather(block):
        other = to_copy(block)
        return jnp.stack([block, to_core(block), other, to_core(other)])

    def group_scatter(parts):
        near = to_core(jnp.stack([parts[1], parts[3]]).astype(BF16)).astype(F32)
        away = to_copy((parts[2] + near[1]).astype(BF16)).astype(F32)
        return parts[0] + near[0] + away

    def local(
        tokens,
        segments,
        counts,
        ln1_gain,
        ln1_bias,
        w_qkv,
        bias_query,
        bias_value,
        w_proj,
        bias_proj,
        ln2_gain,
        ln2_bias,
        w_fc,
        bias_fc,
        w_out,
        bias_out,
        cotangent,
    ):
        row_count, width = tokens.shape
        head_width = width // HEADS
        own_rows = width // n_shard
        chip_rows = 2 * own_rows
        own_hidden = w_out.shape[0]
        piece = own_hidden // 2
        groups = HEADS // RANKS
        scale = head_width ** (-0.5)
        replica_at = lax.axis_index("replica")
        shard_at = lax.axis_index("shard")
        x = replica_at % 2
        c = shard_at % 2
        p = shard_at // 2
        rank = 2 * x + c
        place = jnp.where(p % 2 == 0, p // 2, n_pos - 1 - p // 2)

        def origin(index):
            index = index % n_pos
            return jnp.where(index < half, 2 * index, 2 * (n_pos - 1 - index) + 1)

        def by_core(mine, other):
            return jnp.where(c == 0, jnp.stack([mine, other]), jnp.stack([other, mine]))

        position = jnp.arange(row_count, dtype=jnp.int32)
        in_use = (position < counts[0]).astype(F32)
        notes = jnp.stack([segments.astype(BF16), in_use.astype(BF16)])
        notes = jnp.pad(notes, ((0, SMALL_ROWS - 2), (0, width - row_count)))
        seen = group_gather(jnp.concatenate([tokens, notes]))
        tokens_all = seen[:, :row_count].reshape(RANKS * row_count, width)
        seg_all = seen[:, row_count, :row_count]
        use_all = seen[:, row_count + 1, :row_count]

        def qkv_part(which):
            view = w_qkv.reshape(own_rows, 3, groups, RANKS, head_width)
            return lax.dynamic_index_in_dim(view, which, 3, keepdims=False).reshape(own_rows, -1)

        def fc_part(core):
            view = w_fc.reshape(own_rows, n_pos, 4, piece)
            part = lax.dynamic_index_in_dim(view, 2 * core + x, 2, keepdims=False)
            return part.reshape(own_rows, -1)

        vectors = [ln1_gain, ln1_bias, bias_query, bias_value, bias_proj, ln2_gain, ln2_bias, bias_out, bias_fc]
        starts = [0]
        for vector in vectors:
            starts.append(starts[-1] + vector.shape[0])
        n_small = starts[-1]
        qkv_width = 3 * groups * head_width
        small = jnp.concatenate(vectors)[None]
        small = jnp.pad(small, ((0, SMALL_ROWS - 1), (0, 0)))
        both_small = by_core(small[0], to_core(small)[0])
        qkv_chunk = by_core(qkv_part(rank), to_core(qkv_part(rank ^ 1))).reshape(chip_rows, qkv_width)
        if head_a_shard:
            lent = lax.ppermute(w_proj[:, width // 2 :], MESH_AXES, lend_pairs)
            proj_half = jnp.where(p % 2 == x, w_proj[:, : width // 2], lent)
            proj_chunk = jnp.concatenate([proj_half[:, : width // 4], proj_half[:, width // 4 :]])
        else:
            proj_chunk = jnp.zeros((chip_rows, width // 4), BF16)
        small_chunk = jnp.pad(both_small, ((0, SMALL_ROWS - 2), (0, width - n_small)))
        first_chunk = jnp.concatenate(
            [jnp.concatenate([qkv_chunk, proj_chunk], axis=1), small_chunk]
        )
        fc_chunk = by_core(fc_part(c), to_core(fc_part(1 - c))).reshape(chip_rows, n_pos * piece)
        out_chunk = lax.dynamic_slice_in_dim(w_out, x * piece, piece, 0)

        first_full = ring_gather(first_chunk, place, origin)
        fc_weight = ring_gather(fc_chunk, place, origin).reshape(width, n_pos * piece)
        out_weight = ring_gather(out_chunk, place, origin).reshape(n_pos * piece, width)

        qkv_weight = first_full[:, :chip_rows, :qkv_width].reshape(width, qkv_width)
        if head_a_shard:
            proj_full = first_full[:, :chip_rows, qkv_width:].reshape(
                n_pos // 2, 2, 2, own_rows, width // 4
            )
            proj_full = jnp.where(x == 0, proj_full, proj_full[:, ::-1])
            proj_weight = proj_full.transpose(0, 3, 1, 2, 4).reshape(groups * head_width, width)
        else:
            proj_full = lax.all_gather(w_proj, "shard", axis=0, tiled=True)
            proj_full = proj_full.reshape(groups, RANKS, head_width, width)
            proj_weight = lax.dynamic_index_in_dim(proj_full, rank, 1, keepdims=False)
            proj_weight = proj_weight.reshape(groups * head_width, width)
        smalls = first_full[:, chip_rows : chip_rows + 2, :n_small].reshape(n_shard, n_small)
        params = [
            smalls[:, starts[i] : starts[i + 1]].reshape(-1).astype(F32) for i in range(len(vectors))
        ]
        gain_one, shift_one, query_shift, value_shift, proj_shift, gain_two, shift_two, out_shift, fc_shift = params

        def rank_heads(vector):
            view = vector.reshape(groups, RANKS, head_width)
            return lax.dynamic_index_in_dim(view, rank, 1, keepdims=False).reshape(-1)

        fc_shift = lax.dynamic_index_in_dim(
            fc_shift.reshape(n_pos, 4, piece), 2 * c + x, 1, keepdims=False
        ).reshape(-1)
        qkv_shift = jnp.concatenate(
            [
                rank_heads(query_shift),
                jnp.zeros((groups * head_width,), F32),
                rank_heads(value_shift),
            ]
        )

        unit_one = unit_norm(tokens_all.astype(F32))
        input_one = (unit_one * gain_one + shift_one).astype(BF16)
        qkv_rows = (dot(input_one, qkv_weight) + qkv_shift).astype(BF16)
        qkv_view = qkv_rows.reshape(RANKS, row_count, 3, groups, head_width)
        queries, keys_rows, values_rows = qkv_view[:, :, 0], qkv_view[:, :, 1], qkv_view[:, :, 2]
        visible = (
            (seg_all[:, :, None] == seg_all[:, None, :])
            & (position[None, None, :] <= position[None, :, None])
            & (use_all[:, None, :] > 0)
        )[:, None]
        scores = scale * jnp.einsum("bqhd,bkhd->bhqk", queries, keys_rows, preferred_element_type=F32)
        scores = jnp.where(visible, scores, -1e30)
        top_score = jnp.max(scores, axis=-1, keepdims=True)
        expo = jnp.exp(scores - top_score)
        probs = expo / jnp.sum(expo, axis=-1, keepdims=True)
        probs_low = probs.astype(BF16)
        context = (
            jnp.einsum("bhqk,bkhd->bqhd", probs_low, values_rows, preferred_element_type=F32)
            .reshape(RANKS * row_count, groups * head_width)
            .astype(BF16)
        )
        block_shape = (RANKS, row_count, width)
        stream = tokens.astype(F32)
        middle = stream + proj_shift + group_scatter(dot(context, proj_weight).reshape(block_shape))

        normed_two, norm_two_back = jax.vjp(layer_norm, middle, gain_two, shift_two)
        input_two = group_gather(normed_two.astype(BF16)).reshape(RANKS * row_count, width)
        pre_act = dot(input_two, fc_weight) + fc_shift
        gate_value, gate_back = jax.vjp(smooth_gate, pre_act)
        hidden = gate_value.astype(BF16)
        branch_two = group_scatter(dot(hidden, out_weight).reshape(block_shape)) + out_shift
        mixed = (in_use[:, None] * (middle + branch_two)).astype(BF16)

        d_top = in_use[:, None] * cotangent.astype(F32)
        d_out = group_gather(d_top.astype(BF16)).reshape(RANKS * row_count, width)
        grad_w_out = dot_rows(hidden, d_out).astype(BF16).reshape(n_pos, piece, width)
        d_pre = gate_back(dot_cols(d_out, out_weight))[0].astype(BF16)
        grad_w_fc = dot_rows(input_two, d_pre).astype(BF16).reshape(n_pos, chip_rows, n_pos * piece)
        d_input_two = group_scatter(dot_cols(d_pre, fc_weight).reshape(block_shape))
        d_mid_norm, grad_gain_two, grad_shift_two = norm_two_back(d_input_two)
        d_middle = d_top + d_mid_norm
        own_w_out = ring_scatter(grad_w_out, place, origin)
        own_w_fc = ring_scatter(grad_w_fc, place, origin)

        d_branch = group_gather(d_middle.astype(BF16)).reshape(RANKS * row_count, width)
        grad_w_proj = dot_rows(context, d_branch)
        d_context = (
            dot_cols(d_branch, proj_weight)
            .astype(BF16)
            .reshape(RANKS, row_count, groups, head_width)
        )
        d_values = jnp.einsum("bhqk,bqhd->bkhd", probs_low, d_context, preferred_element_type=F32)
        d_probs = jnp.einsum("bqhd,bkhd->bhqk", d_context, values_rows, preferred_element_type=F32)
        d_scores = (
            probs * (d_probs - jnp.sum(probs * d_probs, axis=-1, keepdims=True))
        ).astype(BF16)
        d_queries = scale * jnp.einsum(
            "bhqk,bkhd->bqhd", d_scores, keys_rows, preferred_element_type=F32
        )
        d_keys = scale * jnp.einsum("bhqk,bqhd->bkhd", d_scores, queries, preferred_element_type=F32)
        d_qkv = (
            jnp.stack([d_queries, d_keys, d_values], axis=2)
            .reshape(RANKS * row_count, qkv_width)
            .astype(BF16)
        )
        grad_w_qkv = dot_rows(input_one, d_qkv).astype(BF16).reshape(n_pos, chip_rows, qkv_width)
        d_input_one = dot_cols(d_qkv, qkv_weight)
        grad_gain_one = jnp.sum(d_input_one * unit_one, axis=0)
        grad_shift_one = jnp.sum(d_input_one, axis=0)
        d_qkv_sums = jnp.sum(d_qkv.astype(F32), axis=0)

        def own_term(values):
            return jnp.sum(values.astype(BF16).astype(F32), axis=0)

        def at_rank(sums):
            view = sums.reshape(groups, 1, head_width)
            mine = jnp.arange(RANKS)[None, :, None] == rank
            return jnp.where(mine, view, 0.0).reshape(-1)

        fc_sums = jnp.sum(d_pre.astype(F32), axis=0).reshape(n_pos, 1, piece)
        fc_sums = jnp.where(jnp.arange(4)[None, :, None] == 2 * c + x, fc_sums, 0.0).reshape(-1)
        small_terms = [
            grad_gain_one,
            grad_shift_one,
            at_rank(d_qkv_sums[: groups * head_width]),
            at_rank(d_qkv_sums[2 * groups * head_width :]),
            own_term(d_middle),
            grad_gain_two,
            grad_shift_two,
            own_term(d_top),
            fc_sums,
        ]
        small_terms = jnp.concatenate(
            [term.reshape(n_shard, -1) for term in small_terms], axis=1
        ).astype(BF16)
        small_terms = jnp.pad(
            small_terms.reshape(n_pos, 2, n_small),
            ((0, 0), (0, SMALL_ROWS - 2), (0, width - n_small)),
        )
        if head_a_shard:
            proj_terms = grad_w_proj.astype(BF16).reshape(n_pos // 2, own_rows, 2, 2, width // 4)
            proj_terms = proj_terms.transpose(0, 2, 3, 1, 4)
            proj_terms = jnp.where(x == 0, proj_terms, proj_terms[:, ::-1])
            proj_terms = proj_terms.reshape(n_pos, chip_rows, width // 4)
        else:
            proj_terms = jnp.zeros((n_pos, chip_rows, width // 4), BF16)
        first_terms = jnp.concatenate(
            [jnp.concatenate([grad_w_qkv, proj_terms], axis=2), small_terms], axis=1
        )
        own_first = ring_scatter(first_terms, place, origin)
        d_in_norm = jax.vjp(unit_norm, stream)[1](
            group_scatter(d_input_one.reshape(block_shape)) * gain_one
        )[0]
        grad_tokens = d_middle + d_in_norm

        def rows_of(chunk, core):
            return lax.dynamic_slice_in_dim(chunk, core * own_rows, own_rows, 0)

        def by_copy(mine, other):
            return jnp.where(x == 0, jnp.stack([mine, other]), jnp.stack([other, mine]))

        own_w_out = own_w_out.astype(BF16)
        grad_w_out = by_copy(own_w_out, to_copy(own_w_out)).reshape(own_hidden, width)

        own_w_fc = own_w_fc.astype(BF16)
        fc_rows = by_core(rows_of(own_w_fc, c), to_core(rows_of(own_w_fc, 1 - c)))
        fc_rows = by_copy(fc_rows, to_copy(fc_rows))
        fc_rows = fc_rows.reshape(2, 2, own_rows, n_pos, piece)
        grad_w_fc = fc_rows.transpose(2, 3, 1, 0, 4).reshape(own_rows, -1)

        own_first = own_first.astype(BF16)
        own_qkv = own_first[:chip_rows, :qkv_width]
        qkv_grad = by_core(rows_of(own_qkv, c), to_core(rows_of(own_qkv, 1 - c)))
        qkv_grad = by_copy(qkv_grad, to_copy(qkv_grad))
        qkv_grad = qkv_grad.reshape(2, 2, own_rows, 3, groups, head_width)
        grad_w_qkv = qkv_grad.transpose(2, 3, 4, 0, 1, 5).reshape(own_rows, -1)

        own_small = own_first[chip_rows:, :n_small]
        near_small = to_core(own_small)
        small_sum = jnp.where(
            c == 0,
            own_small[0].astype(F32) + near_small[0].astype(F32),
            own_small[1].astype(F32) + near_small[1].astype(F32),
        )
        small_send = jnp.pad(small_sum[None].astype(BF16), ((0, SMALL_ROWS - 1), (0, 0)))
        small_sum = small_sum + to_copy(small_send)[0].astype(F32)

        if head_a_shard:
            own_proj = own_first[:chip_rows, qkv_width:]
            given = lax.ppermute(own_proj, MESH_AXES, give_pairs)
            proj_rows = jnp.stack([own_proj, given]).reshape(2, 2, own_rows, width // 4)
            proj_rows = proj_rows.transpose(2, 0, 1, 3).reshape(own_rows, width)
            shared = lax.ppermute(proj_rows, MESH_AXES, share_pairs)
            grad_w_proj = jnp.where(p % 2 == x, proj_rows, shared)
        else:
            proj_rows = grad_w_proj.astype(BF16).reshape(groups, 1, head_width, width)
            mine = jnp.arange(RANKS)[None, :, None, None] == rank
            proj_rows = jnp.where(mine, proj_rows, 0).reshape(width, width)
            proj_rows = lax.psum_scatter(proj_rows, "shard", scatter_dimension=0, tiled=True)
            grad_w_proj = proj_rows.astype(F32) + to_copy(proj_rows).astype(F32)

        if n_pairs > 1:
            grad_w_out, grad_w_fc, grad_w_qkv, grad_w_proj, small_sum = lax.psum(
                tuple(
                    value.astype(BF16)
                    for value in (grad_w_out, grad_w_fc, grad_w_qkv, grad_w_proj, small_sum)
                ),
                "replica",
                axis_index_groups=pair_groups,
            )
        small_sum = small_sum.astype(F32)
        small_grads = [small_sum[starts[i] : starts[i + 1]] for i in range(len(vectors))]
        g_gain_one, g_shift_one, g_query, g_value, g_proj, g_gain_two, g_shift_two, g_out, g_fc = small_grads
        return (
            mixed,
            grad_tokens,
            g_gain_one,
            g_shift_one,
            grad_w_qkv.astype(F32),
            g_query,
            g_value,
            grad_w_proj.astype(F32),
            g_proj,
            g_gain_two,
            g_shift_two,
            grad_w_fc.astype(F32),
            g_fc,
            grad_w_out.astype(F32),
            g_out,
        )

    return local

LANES = 128
HALF = 64
VMEM_BYTES = 26 * 1024 * 1024
ORIGINS = 9
AT_X, AT_C, AT_Y, AT_COUNT = 9, 10, 11, 12
VMEM_SPEC = pl.BlockSpec(memory_space=pltpu.VMEM)
SMEM_SPEC = pl.BlockSpec(memory_space=pltpu.SMEM)
ANY_SPEC = pl.BlockSpec(memory_space=pl.ANY)
HBM_SPEC = pl.BlockSpec(memory_space=pltpu.HBM)


def kernel_call(body, in_specs, outs, scratch=(), micros=1):
    return pl.pallas_call(
        body,
        out_shape=tuple(jax.ShapeDtypeStruct(shape, dtype) for shape, dtype in outs),
        in_specs=list(in_specs),
        out_specs=tuple(VMEM_SPEC for _ in outs),
        scratch_shapes=list(scratch),
        compiler_params=pltpu.CompilerParams(vmem_limit_bytes=VMEM_BYTES),
        cost_estimate=pl.CostEstimate(
            flops=0, bytes_accessed=micros * 3_000_000, transcendentals=0
        ),
    )


def low_half(shape):
    return lax.broadcasted_iota(jnp.int32, shape, len(shape) - 1) < HALF


def turn(values):
    return jnp.concatenate([values[:, HALF:], values[:, :HALF]], axis=1)


def join(c, first, second, low):
    even = jnp.where(low, first, turn(second))
    odd = jnp.where(low, turn(first), second)
    return jnp.where(c == 0, even, odd)


def statistics(values):
    center = values - jnp.mean(values, axis=-1, keepdims=True)
    spread = jnp.mean(center * center, axis=-1, keepdims=True)
    return center, lax.rsqrt(spread + 1e-05)


def norm_back(unit, inverse, d_unit):
    along = jnp.mean(d_unit * unit, axis=-1, keepdims=True)
    return inverse * (d_unit - jnp.mean(d_unit, axis=-1, keepdims=True) - unit * along)


def used_rows(info, rows):
    return (lax.broadcasted_iota(jnp.int32, (rows, 1), 0) < info[AT_COUNT]).astype(F32)


def tokens_body(info, tokens, segments, cotangent, block, d_out):
    rows = tokens.shape[0]
    block[:rows, :] = tokens[...]
    down = lax.broadcasted_iota(jnp.int32, (SMALL_ROWS, rows), 0)
    across = lax.broadcasted_iota(jnp.int32, (SMALL_ROWS, rows), 1)
    used = jnp.where(across < info[AT_COUNT], 1.0, 0.0)
    notes = jnp.where(down == 0, segments[...].astype(F32), jnp.where(down == 1, used, 0.0))
    block[rows:, :rows] = notes.astype(BF16)
    d_out[...] = (used_rows(info, rows) * cotangent[...].astype(F32)).astype(BF16)


def own_part_body(info, w_qkv, w_proj, groups, half):
    x = info[AT_X]
    for z in range(w_qkv.shape[1] // (4 * HALF)):
        at = pl.ds(pl.multiple_of(z * 4 * HALF + x * LANES, LANES), LANES)
        groups[:, z * LANES : (z + 1) * LANES] = w_qkv[:, at]
    half[...] = w_proj[:, : half.shape[1]]


def first_chunk_body(info, groups, got_qkv, left, lent, vectors, got_vectors, first):
    own_rows = left.shape[0]
    width = 2 * left.shape[1]
    x, c, y = info[AT_X], info[AT_C], info[AT_Y]
    qkv = 3 * width // 4
    low = low_half((own_rows, LANES))
    for core in range(2):
        rows = slice(core * own_rows, (core + 1) * own_rows)
        for pair in range(groups.shape[1] // (2 * LANES)):
            both = []
            for z in (2 * pair, 2 * pair + 1):
                at = pl.ds(pl.multiple_of(z * 4 * HALF + x * LANES, LANES), LANES)
                mine = groups[:, z * LANES : (z + 1) * LANES]
                both.append(jnp.where(c == core, mine, got_qkv[:, at]).astype(F32))
            first[rows, pair * LANES : (pair + 1) * LANES] = join(c, *both, low).astype(BF16)
    half = jnp.where(x == y, left[...], lent[:, width // 2 :])
    first[:own_rows, qkv:] = half[:, : width // 4]
    first[own_rows : 2 * own_rows, qkv:] = half[:, width // 4 :]
    mine = vectors[0:8, :].astype(F32)
    other = got_vectors[0:8, :].astype(F32)
    shifts = vectors[8:16, :].astype(F32)
    blank = jnp.zeros(mine.shape, F32)
    lower = jnp.concatenate([jnp.where(c == 0, mine, other), blank], axis=1)
    upper = jnp.concatenate([blank, jnp.where(c == 0, other, mine)], axis=1)
    small = lower + upper
    wide = jnp.concatenate([mine, blank], axis=1)
    heads = jnp.where(low_half((1, LANES)), wide[6:7], turn(wide)[7:8])
    shifts = jnp.concatenate([shifts, blank], axis=1)
    shifts = jnp.where(x == 0, shifts, jnp.concatenate([shifts[2:], shifts[:2]], axis=0))
    shift = jnp.where(low_half((1, LANES)), shifts[0:1], turn(shifts)[1:2])
    row = lax.broadcasted_iota(jnp.int32, small.shape, 0)
    small = jnp.where(row == 6, shift, jnp.where(row == 7, heads, small))
    first[2 * own_rows :, :] = jnp.zeros((SMALL_ROWS, width), BF16)
    first[2 * own_rows : 2 * own_rows + 8, :LANES] = small.astype(BF16)


def second_chunks_body(info, w_fc, got_fc, came_forth, came_back, forth, back, sems):
    own_rows = w_fc.shape[0]
    chip_rows = 2 * own_rows
    x, c = info[AT_X], info[AT_C]
    copies = [
        (came_forth, forth.at[pl.ds(chip_rows, chip_rows), :]),
        (came_back, back.at[pl.ds(0, chip_rows), :]),
    ]
    for p in range(w_fc.shape[1] // (4 * LANES)):
        source = pl.ds(pl.multiple_of(p * 4 * LANES + (2 * c + x) * LANES, LANES), LANES)
        lanes = pl.ds(p * LANES, LANES)
        for weight, core in ((w_fc, c), (got_fc, 1 - c)):
            row = pl.multiple_of(core * own_rows, own_rows)
            copies.append((weight.at[:, source], forth.at[pl.ds(row, own_rows), lanes]))
    for copy in run_copies(copies, sems):
        copy.wait()
    back[chip_rows:, :] = forth[:chip_rows, :]


def run_copies(copies, sems):
    started = []
    for i, (source, target) in enumerate(copies):
        copy = pltpu.make_async_copy(source, target, sems.at[i])
        copy.start()
        started.append(copy)
    return started


def blocks_body(*refs):
    blocks = refs[:RANKS]
    units, masks = refs[RANKS:]
    rows = units.shape[0] // RANKS
    down = lax.broadcasted_iota(jnp.int32, (rows, rows), 0)
    across = lax.broadcasted_iota(jnp.int32, (rows, rows), 1)
    for b, block in enumerate(blocks):
        center, inverse = statistics(block[:rows, :].astype(F32))
        units[b * rows : (b + 1) * rows, :] = center * inverse
        notes = block[rows : rows + SMALL_ROWS, : 2 * LANES].astype(F32)
        seg_row, use_row = notes[0:1, :rows], notes[1:2, :rows]
        seg_column = jnp.sum(jnp.where(down == across, seg_row, 0.0), axis=1, keepdims=True)
        visible = (seg_column == seg_row) & (across <= down) & (use_row > 0)
        masks[b] = jnp.where(visible, 1.0, 0.0)


def attention_body(info, *refs):
    units, masks, chunks = refs[0], refs[1], refs[2 : 2 + ORIGINS]
    normed, qkv, probs, context, send, keep_own, keep_away, qkv_weight, proj_weight, smalls = refs[
        2 + ORIGINS : 2 + ORIGINS + 10
    ]
    (sems,) = refs[2 + ORIGINS + 10 :]
    x = info[AT_X]
    width = normed.shape[1]
    rows = normed.shape[0] // RANKS
    chip_rows = chunks[0].shape[0] - SMALL_ROWS
    own_rows = chip_rows // 2
    cols = 3 * width // 4
    copies = []
    for i, chunk in enumerate(chunks):
        at = info[i]
        start = chunks[i - 1].shape[0] if i == ORIGINS - 1 else 0
        stop = start + chunk.shape[0]
        for part in range(2):
            top = part * own_rows
            if start <= top and top + own_rows <= stop:
                source = pl.ds(top - start, own_rows)
                copies.append(
                    (
                        chunk.at[source, pl.ds(0, cols)],
                        qkv_weight.at[pl.ds(pl.multiple_of(at * chip_rows + top, own_rows), own_rows), :],
                    )
                )
                side = lax.rem(at + x, 2) * (width // 2) + part * (width // 4)
                copies.append(
                    (
                        chunk.at[source, pl.ds(cols, width // 4)],
                        proj_weight.at[
                            pl.ds(pl.multiple_of(lax.div(at, 2) * own_rows, own_rows), own_rows),
                            pl.ds(pl.multiple_of(side, LANES), width // 4),
                        ],
                    )
                )
        if stop > chip_rows:
            copies.append(
                (
                    chunk.at[pl.ds(chip_rows - start, SMALL_ROWS), pl.ds(0, LANES)],
                    smalls.at[:, pl.ds(pl.multiple_of(at * LANES, LANES), LANES)],
                )
            )
    started = run_copies(copies, sems)

    for copy in started:
        copy.wait()
    gain = smalls[0:1, :].astype(F32)
    shift = smalls[1:2, :].astype(F32)
    normed[...] = (units[...] * gain + shift).astype(BF16)

    low_row = low_half((8, LANES))
    biases = jnp.broadcast_to(smalls[7:8, :].astype(F32), (8, width))
    query_shift, value_shift = [], []
    for pair in range(2):
        first, second = (
            jnp.where(
                x == 0,
                biases[:, z * 2 * LANES : z * 2 * LANES + LANES],
                biases[:, z * 2 * LANES + LANES : (z + 1) * 2 * LANES],
            )
            for z in (2 * pair, 2 * pair + 1)
        )
        query_shift.append(jnp.where(low_row, first, turn(second))[0:1])
        value_shift.append(jnp.where(low_row, turn(first), second)[0:1])
    third = width // 4
    for n in range(3):
        product = dot(normed[...], qkv_weight[:, n * third : (n + 1) * third])
        if n != 1:
            product = product + jnp.concatenate(value_shift if n else query_shift, axis=1)
        qkv[:, n * third : (n + 1) * third] = product.astype(BF16)

    scale = HALF ** (-0.5)
    low = low_half((1, LANES))
    keep_low = jnp.where(low, 1.0, 0.0).astype(BF16)
    keep_high = jnp.where(low, 0.0, 1.0).astype(BF16)

    def attend(b, carry):
        at = pl.ds(pl.multiple_of(b * rows, rows), rows)
        mask = masks[b] > 0.5
        for pair in range(2):
            lanes = pair * LANES
            queries = qkv[at, lanes : lanes + LANES]
            keys = qkv[at, third + lanes : third + lanes + LANES]
            values = qkv[at, 2 * third + lanes : 2 * third + lanes + LANES]
            outs = []
            for side, keep in enumerate((keep_low, keep_high)):
                scores = jnp.where(mask, scale * dot_cols(queries * keep, keys), -1e30)
                expo = jnp.exp(scores - jnp.max(scores, axis=-1, keepdims=True))
                share = (expo / jnp.sum(expo, axis=-1, keepdims=True)).astype(BF16)
                probs[b * 4 + 2 * pair + side] = share
                outs.append(dot(share, values))
            context[at, lanes : lanes + LANES] = jnp.where(low, outs[0], outs[1]).astype(BF16)
        return carry

    lax.fori_loop(0, RANKS, attend, 0)
    for n in range(4):
        columns = slice(n * third, (n + 1) * third)
        store_parts(dot(context[...], proj_weight[:, columns]), columns, rows, send, keep_own, keep_away)


def store_parts(product, columns, rows, send, keep_own, keep_away):
    keep_own[:, columns] = product[:rows]
    send[0, :, columns] = product[rows : 2 * rows].astype(BF16)
    keep_away[:, columns] = product[2 * rows : 3 * rows]
    send[1, :, columns] = product[3 * rows :].astype(BF16)


def total(keep_own, near, away):
    return keep_own[...] + near[0].astype(F32) + away[...].astype(F32)


def message_body(keep_own, keep_away, near, message):
    message[0] = (keep_own[...] + near[0].astype(F32)).astype(BF16)
    message[1] = (keep_away[...] + near[1].astype(F32)).astype(BF16)


def ends_body(forth, back, forth_end, back_end):
    forth_end[...] = forth[: forth_end.shape[0], :]
    back_end[...] = back[back.shape[0] - back_end.shape[0] :, :]


def second_norm_body(block, block_other, keep_own, keep_away, near, got, smalls, middle, normed):
    rows = keep_own.shape[0]
    gain, shift = smalls[3:4, :].astype(F32), smalls[4:5, :].astype(F32)
    for i, (tokens, keep) in enumerate(((block, keep_own), (block_other, keep_away))):
        values = tokens[:rows, :].astype(F32) + smalls[2:3, :].astype(F32)
        values = values + (keep[...] + near[i].astype(F32) + got[1 - i].astype(F32))
        middle[i] = values
        center, inverse = statistics(values)
        normed[i] = (center * inverse * gain + shift).astype(BF16)


def feed_body(info, normed, beside, *refs):
    d_outs = refs[:RANKS]
    (out_chunk, two_forth, two_back, three_forth, three_back, four_forth, four_back) = refs[RANKS : RANKS + 7]
    five_forth, five_back, six_forth, six_back, smalls = refs[RANKS + 7 : RANKS + 12]
    given, d_out, hidden, d_pre, send, keep_own, keep_away, sums, out_weight, fc_weight, sems = refs[RANKS + 12 :]
    rows = normed.shape[1]
    width = given.shape[1]
    size = out_chunk.shape[0]
    half = size // 2
    copies = []
    for ref, start, count, weight, index, row in (
        (two_forth, 0, size, fc_weight, 0, 0),
        (three_forth, 0, size, fc_weight, 1, 0),
        (three_back, size, size, fc_weight, 2, 0),
        (four_forth, 0, size, fc_weight, 3, 0),
        (four_back, size, size, fc_weight, 4, 0),
        (five_forth, 0, size, fc_weight, 5, 0),
        (five_back, half, size, fc_weight, 6, 0),
        (six_forth, 0, half, fc_weight, 7, 0),
        (six_back, 0, half, fc_weight, 7, half),
        (out_chunk, 0, size, out_weight, 0, 0),
        (two_forth, size, size, out_weight, 1, 0),
        (two_back, 0, size, out_weight, 2, 0),
        (three_forth, size, size, out_weight, 3, 0),
        (three_back, 0, size, out_weight, 4, 0),
        (four_forth, size, size, out_weight, 5, 0),
        (four_back, 0, size, out_weight, 6, 0),
        (five_forth, size, half, out_weight, 7, 0),
        (five_back, 0, half, out_weight, 7, half),
    ):
        at = pl.multiple_of(info[index] * size + row, half)
        copies.append((ref.at[pl.ds(start, count), :], weight.at[pl.ds(at, count), :]))
    started = run_copies(copies, sems)
    for b in range(RANKS):
        given[b * rows : (b + 1) * rows, :] = (beside if b % 2 else normed)[b // 2]
        d_out[b * rows : (b + 1) * rows, :] = d_outs[b][...]
    for copy in started:
        copy.wait()
    tile = 2 * LANES
    root = (2.0 / jnp.pi) ** 0.5
    sums[...] = jnp.zeros(sums.shape, F32)

    def units(n, carry):
        columns = pl.ds(pl.multiple_of(n * tile, tile), tile)
        pre = dot(given[...], fc_weight[:, columns]) + smalls[6:7, columns].astype(F32)
        d_hidden = dot_cols(d_out[...], out_weight[columns, :])
        square = pre * pre
        bend = jnp.tanh(root * pre * (1.0 + 0.044715 * square))
        hidden[:, columns] = (0.5 * pre * (1.0 + bend)).astype(BF16)
        slope = 0.5 * (1.0 + bend) + 0.5 * pre * (1.0 - bend * bend) * root * (
            1.0 + 3.0 * 0.044715 * square
        )
        low = (d_hidden * slope).astype(BF16)
        d_pre[:, columns] = low
        sums[6:7, columns] = jnp.sum(low.astype(F32), axis=0, keepdims=True)
        return carry

    lax.fori_loop(0, width // tile, units, 0)
    for n in range(width // tile):
        columns = slice(n * tile, (n + 1) * tile)
        product = dot_cols(d_pre[...], fc_weight[columns, :])
        store_parts(product, columns, rows, send, keep_own, keep_away)


def feed_out_body(hidden, out_weight, send, keep_own, keep_away):
    rows = keep_own.shape[0]
    tile = 2 * LANES
    for n in range(out_weight.shape[1] // tile):
        columns = slice(n * tile, (n + 1) * tile)
        store_parts(dot(hidden[...], out_weight[:, columns]), columns, rows, send, keep_own, keep_away)


def mixed_body(info, middle, keep_own, near, away, smalls, mixed):
    values = middle[0] + total(keep_own, near, away) + smalls[5:6, :].astype(F32)
    mixed[...] = (used_rows(info, keep_own.shape[0]) * values).astype(BF16)


def second_back_body(middle, d_top, d_other, keep_own, keep_away, near, got, smalls, d_middle, d_branch, sums):
    gain = smalls[3:4, :].astype(F32)
    for i, (d_out, keep) in enumerate(((d_top, keep_own), (d_other, keep_away))):
        d_values = keep[...] + near[i].astype(F32) + got[1 - i].astype(F32)
        center, inverse = statistics(middle[i])
        unit = center * inverse
        result = d_out[...].astype(F32) + norm_back(unit, inverse, d_values * gain)
        low = result.astype(BF16)
        d_branch[i] = low
        if i == 0:
            d_middle[...] = result
            sums[...] = jnp.zeros(sums.shape, F32)
            sums[2:3, :] = jnp.sum(low.astype(F32), axis=0, keepdims=True)
            sums[3:4, :] = jnp.sum(d_values * unit, axis=0, keepdims=True)
            sums[4:5, :] = jnp.sum(d_values, axis=0, keepdims=True)
            sums[5:6, :] = jnp.sum(d_out[...].astype(F32), axis=0, keepdims=True)


def attention_back_body(info, branches, beside, units, *refs):
    qkv, probs, qkv_weight, proj_weight, sums_two, sums_fc = refs[:6]
    d_branch, d_qkv, send, keep_own, keep_away, sums = refs[6:12]
    (d_context,) = refs[12:]
    rows = branches.shape[1]
    width = d_branch.shape[1]
    third = width // 4
    x = info[AT_X]
    for b in range(RANKS):
        d_branch[b * rows : (b + 1) * rows, :] = (beside if b % 2 else branches)[b // 2]
    d_context[...] = dot_cols(d_branch[...], proj_weight[...]).astype(BF16)
    scale = HALF ** (-0.5)
    low = low_half((1, LANES))
    keep_low = jnp.where(low, 1.0, 0.0).astype(BF16)
    keep_high = jnp.where(low, 0.0, 1.0).astype(BF16)

    def attend(b, carry):
        at = pl.ds(pl.multiple_of(b * rows, rows), rows)
        for pair in range(2):
            lanes = pair * LANES
            queries = qkv[at, lanes : lanes + LANES]
            keys = qkv[at, third + lanes : third + lanes + LANES]
            values = qkv[at, 2 * third + lanes : 2 * third + lanes + LANES]
            d_out = d_context[at, lanes : lanes + LANES]
            results = []
            for side, keep in enumerate((keep_low, keep_high)):
                share = probs[b * 4 + 2 * pair + side]
                wide = share.astype(F32)
                d_values = dot_rows(share, d_out)
                d_probs = dot_cols(d_out * keep, values)
                d_scores = wide * (d_probs - jnp.sum(wide * d_probs, axis=-1, keepdims=True))
                d_scores = d_scores.astype(BF16)
                results.append(
                    (scale * dot(d_scores, keys), scale * dot_rows(d_scores, queries), d_values)
                )
            for n in range(3):
                merged = jnp.where(low, results[0][n], results[1][n]).astype(BF16)
                d_qkv[at, n * third + lanes : n * third + lanes + LANES] = merged
        return carry

    lax.fori_loop(0, RANKS, attend, 0)
    sums[0:8, :] = sums_two[...] + sums_fc[...]
    sums[8:, :] = jnp.zeros((SMALL_ROWS - 8, width), F32)
    for n in range(4):
        columns = slice(n * third, (n + 1) * third)
        product = dot_cols(d_qkv[...], qkv_weight[columns, :])
        store_parts(product, columns, rows, send, keep_own, keep_away)
        sums[1:2, columns] = jnp.sum(product, axis=0, keepdims=True)
        sums[0:1, columns] = jnp.sum(product * units[:, columns], axis=0, keepdims=True)
    low_row = low_half((8, LANES))
    for pair in range(2):
        lanes = pair * LANES
        d_queries = jnp.sum(d_qkv[:, lanes : lanes + LANES].astype(F32), axis=0, keepdims=True)
        d_values = jnp.sum(
            d_qkv[:, 2 * third + lanes : 2 * third + lanes + LANES].astype(F32), axis=0, keepdims=True
        )
        d_queries = jnp.broadcast_to(d_queries, (8, LANES))
        d_values = jnp.broadcast_to(d_values, (8, LANES))
        even = jnp.where(low_row, d_queries, turn(d_values))[0:1]
        odd = jnp.where(low_row, turn(d_queries), d_values)[0:1]
        for z, group in ((2 * pair, even), (2 * pair + 1, odd)):
            for y in range(2):
                start = (2 * z + y) * LANES
                sums[7:8, start : start + LANES] = jnp.where(x == y, group, 0.0)


def first_back_body(tokens, d_middle, keep_own, near, away, smalls, result):
    center, inverse = statistics(tokens[...].astype(F32))
    d_unit = total(keep_own, near, away) * smalls[0:1, :].astype(F32)
    result[...] = d_middle[...] + norm_back(center * inverse, inverse, d_unit)


def second_term(info, index, grad_fc, grad_out):
    at = info[index]
    results = []
    for grad in (grad_fc, grad_out):
        chip_rows = grad.shape[0] * 2 // HEADS
        results.append(grad[pl.ds(pl.multiple_of(at * chip_rows, chip_rows), chip_rows), :])
    return results


def add(left, right):
    return (left.astype(F32) + right.astype(F32)).astype(BF16)


def second_far_body(info, grad_fc, grad_out, forth, back):
    forth[...], back[...] = second_term(info, ORIGINS - 1, grad_fc, grad_out)


def second_hop_body(step, info, got_forth, got_back, grad_fc, grad_out, forth, back):
    rows = forth.shape[0] // 2
    for target, got, index, part in ((forth, got_forth, 2 * step, 0), (back, got_back, 2 * step - 1, 1)):
        terms = second_term(info, index, grad_fc, grad_out)
        for i in range(2):
            where = slice(i * rows, (i + 1) * rows)
            if got.shape[0] == rows:
                target[where, :] = add(terms[i], got[...]) if i == part else terms[i]
            else:
                target[where, :] = add(terms[i], got[where, :])


def second_last_body(info, got_forth, got_back, grad_fc, grad_out, own):
    terms = second_term(info, 0, grad_fc, grad_out)
    rows = own.shape[0] // 2
    for i in range(2):
        where = slice(i * rows, (i + 1) * rows)
        values = got_forth[where, :].astype(F32) + got_back[where, :].astype(F32)
        own[where, :] = add(values, terms[i])


def first_term(info, index, grad_qkv, grad_proj, sums):
    at = info[index]
    chip_rows = grad_qkv.shape[0] * 2 // HEADS
    own_rows = chip_rows // 2
    quarter = grad_proj.shape[1] // 4
    side = lax.rem(at + info[AT_X], 2) * 2 * quarter
    head = pl.ds(pl.multiple_of(lax.div(at, 2) * own_rows, own_rows), own_rows)
    results = []
    for part in range(2):
        rows = pl.ds(pl.multiple_of(at * chip_rows + part * own_rows, own_rows), own_rows)
        lanes = pl.ds(pl.multiple_of(side + part * quarter, LANES), quarter)
        results.append((grad_qkv[rows, :], grad_proj[head, lanes]))
    small = sums[:, pl.ds(pl.multiple_of(at * LANES, LANES), LANES)].astype(BF16)
    return results, small


def put_first(target, row, values, got, got_row):
    at = 0
    rows = values[0].shape[0]
    for value in values:
        lanes = slice(at, at + value.shape[1])
        if got is not None:
            value = add(value, got[got_row : got_row + rows, lanes])
        target[row : row + rows, lanes] = value
        at += value.shape[1]


def first_far_body(info, grad_qkv, grad_proj, sums, forth, back):
    (upper, lower), small = first_term(info, ORIGINS - 1, grad_qkv, grad_proj, sums)
    own_rows = forth.shape[0]
    put_first(forth, 0, upper, None, 0)
    put_first(back, 0, lower, None, 0)
    back[own_rows:, :] = jnp.zeros((SMALL_ROWS, back.shape[1]), BF16)
    put_first(back, own_rows, (small,), None, 0)


def first_hop_body(step, info, got_forth, got_back, grad_qkv, grad_proj, sums, forth, back):
    own_rows = (forth.shape[0] - SMALL_ROWS) // 2
    for target, got, index in ((forth, got_forth, 2 * step), (back, got_back, 2 * step - 1)):
        terms, small = first_term(info, index, grad_qkv, grad_proj, sums)
        shift = 0
        if got.shape[0] == own_rows:
            came = (got, None, None)
        elif got.shape[0] == own_rows + SMALL_ROWS:
            came, shift = (None, got, got), own_rows
        else:
            came = (got, got, got)
        target[2 * own_rows :, :] = jnp.zeros((SMALL_ROWS, target.shape[1]), BF16)
        for i, values in enumerate((*terms, (small,))):
            put_first(target, i * own_rows, values, came[i], i * own_rows - shift)


def first_last_body(info, got_forth, got_back, grad_qkv, grad_proj, sums, own):
    own_rows = (own.shape[0] - SMALL_ROWS) // 2
    terms, small = first_term(info, 0, grad_qkv, grad_proj, sums)
    own[2 * own_rows :, :] = jnp.zeros((SMALL_ROWS, own.shape[1]), BF16)
    for i, values in enumerate((*terms, (small,))):
        at = 0
        rows = slice(i * own_rows, i * own_rows + values[0].shape[0])
        for value in values:
            lanes = slice(at, at + value.shape[1])
            came = got_forth[rows, lanes].astype(F32) + got_back[rows, lanes].astype(F32)
            own[rows, lanes] = add(came, value)
            at += value.shape[1]


def four_parts(info, own, near, other, cross):
    x, c = info[AT_X], info[AT_C]

    def reader(copy, core):
        def read(rows, lanes):
            same = jnp.where(c == core, own[rows, lanes], near[rows, lanes])
            far = jnp.where(c == core, other[rows, lanes], cross[rows, lanes])
            return jnp.where(x == copy, same, far).astype(F32)

        return read

    return reader


def hidden_grads_body(info, own, near, other, cross, grad_fc, grad_out):
    x, c = info[AT_X], info[AT_C]
    own_rows = grad_fc.shape[0]
    width = own.shape[1]
    piece = grad_out.shape[0] // 2
    reader = four_parts(info, own, near, other, cross)
    rows = pl.ds(pl.multiple_of(c * own_rows, own_rows), own_rows)
    for copy in range(2):
        for core in range(2):
            read = reader(copy, core)
            for p in range(width // LANES):
                at = p * 4 * LANES + core * 2 * LANES + copy * LANES
                grad_fc[:, at : at + LANES] = read(rows, slice(p * LANES, (p + 1) * LANES))
        grad_out[copy * piece : (copy + 1) * piece, :] = jnp.where(
            x == copy, own[2 * own_rows :, :], other[2 * own_rows :, :]
        ).astype(F32)


def first_grads_body(info, own, near, other, cross, side, corner, grad_qkv, grad_proj, *small_outs):
    x, c, y = info[AT_X], info[AT_C], info[AT_Y]
    own_rows, width = grad_proj.shape
    qkv = 3 * width // 4
    quarter = width // 4
    low = low_half((own_rows, LANES))
    reader = four_parts(info, own, near, other, cross)
    rows = pl.ds(pl.multiple_of(c * own_rows, own_rows), own_rows)
    for copy in range(2):
        first, second = reader(copy, 0), reader(copy, 1)
        for pair in range(qkv // LANES):
            lanes = slice(pair * LANES, (pair + 1) * LANES)
            one, two = first(rows, lanes), second(rows, lanes)
            at = pair * 8 * HALF + copy * LANES
            grad_qkv[:, at : at + LANES] = jnp.where(low, one, turn(two))
            at += 4 * HALF
            grad_qkv[:, at : at + LANES] = jnp.where(low, turn(one), two)
    for part in range(2):
        block = slice(part * own_rows, (part + 1) * own_rows)
        left = jnp.where(x == y, own[block, qkv:], other[block, qkv:]).astype(F32)
        grad_proj[:, part * quarter : (part + 1) * quarter] = left
        right = jnp.where(x == y, side[block, :], corner[block, :]).astype(F32)
        grad_proj[:, 2 * quarter + part * quarter : 2 * quarter + (part + 1) * quarter] = right
    mine, beside, far, across = (
        ref[2 * own_rows :, :LANES].astype(F32) for ref in (own, near, other, cross)
    )
    summed = (mine + beside) + (far + across)
    summed = jnp.where(c == 0, summed, turn(summed))
    heads = jnp.where(x == y, mine, far)
    for i in range(6):
        small_outs[i][...] = summed[i : i + 1, :HALF]
    small_outs[6][0:1, :] = jnp.where(x == 0, mine, far)[6:7]
    small_outs[6][1:2, :] = jnp.where(x == 0, far, mine)[6:7]
    small_outs[7][...] = heads[7:8, :HALF]
    small_outs[8][...] = turn(heads)[7:8, :HALF]


def tie(*values):
    return lax.optimization_barrier(values)


def make_kernel_local(n_replica, n_shard):
    n_pos = n_shard // 2
    half = n_pos // 2

    def every(move):
        pairs = []
        for r in range(n_replica):
            for p in range(n_pos):
                for c in range(2):
                    to = move(r, p, c)
                    pairs.append((r * n_shard + p * 2 + c, to[0] * n_shard + to[1] * 2 + to[2]))
        return pairs

    ring = list(range(0, n_pos, 2)) + list(range(n_pos - 1, 0, -2))
    after = {p: ring[(i + 1) % n_pos] for i, p in enumerate(ring)}
    before = {p: ring[i - 1] for i, p in enumerate(ring)}

    def mover(move):
        pairs = every(move)
        return lambda v: lax.ppermute(v, MESH_AXES, pairs)

    to_core = mover(lambda r, p, c: (r, p, 1 - c))
    to_copy = mover(lambda r, p, c: (r ^ 1, p, c))
    to_next = mover(lambda r, p, c: (r, after[p], c))
    to_back = mover(lambda r, p, c: (r, before[p], c))
    to_side = mover(lambda r, p, c: (r, p ^ 1, c))
    to_corner = mover(lambda r, p, c: (r ^ 1, p ^ 1, c))

    def local(
        tokens,
        segments,
        counts,
        ln1_gain,
        ln1_bias,
        w_qkv,
        bias_query,
        bias_value,
        w_proj,
        bias_proj,
        ln2_gain,
        ln2_bias,
        w_fc,
        bias_fc,
        w_out,
        bias_out,
        cotangent,
    ):
        rows, width = tokens.shape
        own_rows = width // n_shard
        chip_rows = 2 * own_rows
        piece = w_out.shape[0] // 2
        units = n_pos * piece
        all_rows = RANKS * rows
        qkv_cols = 3 * width // 4
        first_shape = ((chip_rows + SMALL_ROWS, width), BF16)
        second_shape = ((chip_rows + piece, width), BF16)
        replica_at = lax.axis_index("replica")
        shard_at = lax.axis_index("shard")
        x, c, p = replica_at % 2, shard_at % 2, shard_at // 2
        place = jnp.where(p % 2 == 0, p // 2, n_pos - 1 - p // 2)

        def origin(index):
            index = index % n_pos
            return jnp.where(index < half, 2 * index, 2 * (n_pos - 1 - index) + 1)

        offsets = [0]
        for step in range(1, half):
            offsets += [-step, step]
        offsets += [half, half]
        info = jnp.stack(
            [origin(place + offset) for offset in offsets] + [x, c, p % 2, counts[0]]
        ).astype(jnp.int32)

        got_qkv, lent = to_core(w_qkv), to_side(w_proj)
        vectors = jnp.stack(
            [ln1_gain, ln1_bias, bias_proj, ln2_gain, ln2_bias, bias_out, bias_query, bias_value]
            + [bias_fc[i * own_rows : (i + 1) * own_rows] for i in range(4)]
            + [jnp.zeros((own_rows,), BF16)] * 4
        )
        got_vectors = to_core(vectors)
        groups, left = kernel_call(
            own_part_body,
            [SMEM_SPEC] + [VMEM_SPEC] * 2,
            [((own_rows, 3 * width // 2), BF16), ((own_rows, width // 2), BF16)],
        )(info, w_qkv, w_proj)
        out_chunk = lax.dynamic_slice_in_dim(w_out, x * piece, piece, 0)
        groups, out_chunk = tie(groups, out_chunk)
        out_forth, out_back = to_next(out_chunk), to_back(out_chunk)
        block, d_top = kernel_call(
            tokens_body,
            [SMEM_SPEC] + [VMEM_SPEC] * 3,
            [((rows + SMALL_ROWS, width), BF16), ((rows, width), BF16)],
        )(info, tokens, segments.reshape(1, rows), cotangent)
        (first_chunk,) = kernel_call(
            first_chunk_body, [SMEM_SPEC] + [VMEM_SPEC] * 6, [first_shape], micros=2
        )(info, groups, got_qkv, left, lent, vectors, got_vectors)

        first_chunk, later_fc = tie(first_chunk, w_fc)
        forth, back = to_next(first_chunk), to_back(first_chunk)
        got_fc = to_core(later_fc)
        firsts = [first_chunk, forth, back]
        forth, back, block = tie(forth, back, block)
        block_other = to_copy(block)
        blocks = [block, to_core(block), block_other, to_core(block_other)]
        forth, back = to_next(forth), to_back(back)
        firsts += [forth, back]
        forth, back = to_next(forth), to_back(back)
        firsts += [forth, back]
        two_forth, two_back = kernel_call(
            second_chunks_body,
            [SMEM_SPEC] + [HBM_SPEC] * 4,
            [second_shape, second_shape],
            [pltpu.SemaphoreType.DMA((2 + 2 * n_pos,))],
            micros=2,
        )(info, w_fc, got_fc, out_forth, out_back)
        blocks = tie(*blocks, forth[:own_rows], back[own_rows:], two_forth, two_back)
        forth, back, two_forth, two_back = blocks[RANKS:]
        blocks = blocks[:RANKS]
        unit, masks = kernel_call(
            blocks_body,
            [VMEM_SPEC] * RANKS,
            [((all_rows, width), F32), ((RANKS, rows, rows), F32)],
            micros=2,
        )(*blocks)
        forth, back, two_forth, two_back, d_top = tie(
            to_next(forth), to_back(back), two_forth, two_back, d_top
        )
        firsts += [forth, back]
        three_forth, three_back = to_next(two_forth), to_back(two_back)

        parts = [((2, rows, width), BF16), ((rows, width), F32), ((rows, width), F32)]
        two_blocks = ((2, rows, width), BF16)
        d_other = to_copy(d_top)
        normed, qkv, probs, context, send, keep_own, keep_away, qkv_weight, proj_weight, smalls = kernel_call(
            attention_body,
            [SMEM_SPEC] + [VMEM_SPEC] * 2 + [ANY_SPEC] * ORIGINS,
            [
                ((all_rows, width), BF16),
                ((all_rows, qkv_cols), BF16),
                ((4 * RANKS, rows, rows), BF16),
                ((all_rows, width // 4), BF16),
                *parts,
                ((width, qkv_cols), BF16),
                ((width // 4, width), BF16),
                ((SMALL_ROWS, width), BF16),
            ],
            [pltpu.SemaphoreType.DMA((5 * n_pos,))],
            micros=8,
        )(info, unit, masks, *firsts)
        send, d_top, d_other, three_forth, three_back = tie(
            send, d_top, d_other, three_forth, three_back
        )
        near = to_core(send)
        four_forth, four_back = to_next(three_forth), to_back(three_back)

        def message(keep_own, keep_away, near):
            return kernel_call(message_body, [VMEM_SPEC] * 3, [two_blocks], micros=0)(
                keep_own, keep_away, near
            )[0]

        got = to_copy(message(keep_own, keep_away, near))
        d_outs = [d_top, to_core(d_top), d_other, to_core(d_other)]
        five_forth, five_back = kernel_call(
            ends_body, [VMEM_SPEC] * 2, [((chip_rows + own_rows, width), BF16)] * 2, micros=6
        )(four_forth, four_back)
        five_forth, five_back = to_next(five_forth), to_back(five_back)
        got, five_forth, five_back = tie(got, five_forth, five_back)
        middle, normed_two = kernel_call(
            second_norm_body, [VMEM_SPEC] * 7, [((2, rows, width), F32), two_blocks], micros=2
        )(block, block_other, keep_own, keep_away, near, got, smalls)
        beside = to_core(normed_two)
        six_forth = to_next(five_forth[:own_rows])
        six_back = to_back(five_back[chip_rows:])

        given, d_out, hidden, d_pre, send, keep_own, keep_away, sums_fc, out_weight = kernel_call(
            feed_body,
            [SMEM_SPEC] + [VMEM_SPEC] * (2 + RANKS) + [ANY_SPEC] * 11 + [VMEM_SPEC],
            [
                ((all_rows, width), BF16),
                ((all_rows, width), BF16),
                ((all_rows, units), BF16),
                ((all_rows, units), BF16),
                *parts,
                ((8, units), F32),
                ((units, width), BF16),
            ],
            [pltpu.VMEM((width, units), BF16), pltpu.SemaphoreType.DMA((18,))],
            micros=8,
        )(
            info, normed_two, beside, *d_outs, out_chunk, two_forth, two_back, three_forth, three_back,
            four_forth, four_back, five_forth, five_back, six_forth, six_back, smalls,
        )

        near = to_core(send)
        near, given, d_out, hidden, d_pre = tie(near, given, d_out, hidden, d_pre)
        got = to_copy(message(keep_own, keep_away, near))
        grad_w_out = dot_rows(hidden, d_out).astype(BF16)
        grad_w_fc = dot_rows(given, d_pre).astype(BF16)
        far_forth, far_back = kernel_call(
            second_far_body,
            [SMEM_SPEC] + [VMEM_SPEC] * 2,
            [((chip_rows, width), BF16), ((piece, width), BF16)],
        )(info, grad_w_fc, grad_w_out)
        far_forth, far_back, hidden = tie(far_forth, far_back, hidden)
        far_forth, far_back = to_next(far_forth), to_back(far_back)
        mix_send, mix_keep, mix_away = kernel_call(
            feed_out_body, [VMEM_SPEC] * 2, parts, micros=2
        )(hidden, out_weight)
        mix_near = to_core(mix_send)

        def second_sums(step, got_forth, got_back):
            return kernel_call(
                functools.partial(second_hop_body, step),
                [SMEM_SPEC] + [VMEM_SPEC] * 4,
                [second_shape, second_shape],
            )(info, got_forth, got_back, grad_w_fc, grad_w_out)

        second_forth, second_back = second_sums(half - 1, far_forth, far_back)
        got, second_forth, second_back, mix_near = tie(got, second_forth, second_back, mix_near)
        second_forth, second_back = to_next(second_forth), to_back(second_back)
        d_middle, d_branches, sums_two = kernel_call(
            second_back_body,
            [VMEM_SPEC] * 8,
            [((rows, width), F32), two_blocks, ((8, width), F32)],
            micros=2,
        )(middle, d_top, d_other, keep_own, keep_away, near, got, smalls)
        beside = to_core(d_branches)
        mix_away = to_copy(add(mix_away, mix_near[1]))

        d_branch, d_qkv, send, keep_own, keep_away, sums = kernel_call(
            attention_back_body,
            [SMEM_SPEC] + [VMEM_SPEC] * 9,
            [
                ((all_rows, width), BF16),
                ((all_rows, qkv_cols), BF16),
                *parts,
                ((SMALL_ROWS, width), F32),
            ],
            [pltpu.VMEM((all_rows, width // 4), BF16)],
            micros=9,
        )(info, d_branches, beside, unit, qkv, probs, qkv_weight, proj_weight, sums_two, sums_fc)
        grad_w_proj = dot_rows(context, d_branch).astype(BF16)
        grad_w_qkv = dot_rows(normed, d_qkv).astype(BF16)
        firsts = (grad_w_qkv, grad_w_proj, sums)
        forth, back = kernel_call(
            first_far_body,
            [SMEM_SPEC] + [VMEM_SPEC] * 3,
            [((own_rows, width), BF16), ((own_rows + SMALL_ROWS, width), BF16)],
        )(info, *firsts)
        send, forth, back, second_forth, second_back, mix_away = tie(
            send, forth, back, second_forth, second_back, mix_away
        )
        forth, back = to_next(forth), to_back(back)
        second_forth, second_back = second_sums(half - 2, second_forth, second_back)

        def first_sums(step, forth, back):
            return kernel_call(
                functools.partial(first_hop_body, step),
                [SMEM_SPEC] + [VMEM_SPEC] * 5,
                [first_shape, first_shape],
            )(info, forth, back, *firsts)

        second_forth, second_back = to_next(second_forth), to_back(second_back)
        forth, back, send = tie(forth, back, send)
        near = to_core(send)
        away = to_copy(add(keep_away, near[1]))
        forth, back = first_sums(3, forth, back)
        forth, back = to_next(forth), to_back(back)
        second_forth, second_back, away = tie(second_forth, second_back, away)
        second_forth, second_back = second_sums(1, second_forth, second_back)
        second_forth, second_back = to_next(second_forth), to_back(second_back)
        (grad_tokens,) = kernel_call(first_back_body, [VMEM_SPEC] * 6, [((rows, width), F32)])(
            tokens, d_middle, keep_own, near, away, smalls
        )
        forth, back, grad_tokens = tie(forth, back, grad_tokens)
        forth, back = first_sums(2, forth, back)
        forth, back = to_next(forth), to_back(back)
        (mixed,) = kernel_call(mixed_body, [SMEM_SPEC] + [VMEM_SPEC] * 5, [((rows, width), BF16)])(
            info, middle, mix_keep, mix_near, mix_away, smalls
        )
        forth, back, second_forth, second_back, mixed = tie(
            forth, back, second_forth, second_back, mixed
        )
        (own_second,) = kernel_call(
            second_last_body, [SMEM_SPEC] + [VMEM_SPEC] * 4, [second_shape]
        )(info, second_forth, second_back, grad_w_fc, grad_w_out)
        near_second, other_second = to_core(own_second), to_copy(own_second)
        forth, back = first_sums(1, forth, back)
        forth, back = to_next(forth), to_back(back)
        forth, back, mixed = tie(forth, back, mixed)
        (own_first,) = kernel_call(
            first_last_body, [SMEM_SPEC] + [VMEM_SPEC] * 5, [first_shape]
        )(info, forth, back, *firsts)
        near_first, other_first = to_core(own_first), to_copy(own_first)
        own_proj = own_first[:chip_rows, qkv_cols:]
        given_side, given_far = to_side(own_proj), to_corner(own_proj)

        grad_w_fc, grad_w_out = kernel_call(
            hidden_grads_body,
            [SMEM_SPEC] + [VMEM_SPEC] * 4,
            [((own_rows, 4 * units), F32), ((2 * piece, width), F32)],
        )(info, own_second, near_second, other_second, to_core(other_second))

        other_first, given_side, given_far, grad_w_fc, grad_w_out = tie(
            other_first, given_side, given_far, grad_w_fc, grad_w_out
        )
        vector_shape = ((1, own_rows), F32)
        grad_w_qkv, grad_w_proj, *small = kernel_call(
            first_grads_body,
            [SMEM_SPEC] + [VMEM_SPEC] * 6,
            [((own_rows, 3 * width), F32), ((own_rows, width), F32)]
            + [vector_shape] * 6
            + [((2, piece), F32)]
            + [vector_shape] * 2,
        )(info, own_first, near_first, other_first, to_core(other_first), given_side, given_far)
        small = [value.reshape(-1) for value in small]
        return (
            mixed,
            grad_tokens,
            small[0],
            small[1],
            grad_w_qkv,
            small[7],
            small[8],
            grad_w_proj,
            small[2],
            small[3],
            small[4],
            grad_w_fc,
            small[6],
            grad_w_out,
            small[5],
        )

    return local


def solution(mesh):
    tokens_spec = P(MESH_AXES, None)
    slots_spec = P(MESH_AXES)
    rows_spec = P("shard", None)
    vector_spec = P("shard")
    in_specs = (
        tokens_spec,
        slots_spec,
        slots_spec,
        vector_spec,
        vector_spec,
        rows_spec,
        vector_spec,
        vector_spec,
        rows_spec,
        vector_spec,
        vector_spec,
        vector_spec,
        rows_spec,
        vector_spec,
        rows_spec,
        vector_spec,
        tokens_spec,
    )
    out_specs = (
        tokens_spec,
        tokens_spec,
        vector_spec,
        vector_spec,
        rows_spec,
        vector_spec,
        vector_spec,
        rows_spec,
        vector_spec,
        vector_spec,
        vector_spec,
        rows_spec,
        vector_spec,
        rows_spec,
        vector_spec,
    )
    n_replica, n_shard = mesh.shape["replica"], mesh.shape["shard"]
    make = make_kernel_local if (n_replica, n_shard) == (2, HEADS) else make_local
    local = make(n_replica, n_shard)
    return jax.shard_map(local, mesh=mesh, in_specs=in_specs, out_specs=out_specs, check_vma=False)
```

```python
import functools

import jax
import jax.numpy as jnp
from jax import lax
from jax.experimental import pallas as pl
from jax.experimental.pallas import tpu as pltpu
from jax.sharding import PartitionSpec as P

HEADS = 16
RANKS = 4
MESH_AXES = ("replica", "shard")
BF16 = jnp.bfloat16
F32 = jnp.float32
SMALL_ROWS = 16


def layer_norm(values, gain, shift):
    center = values - jnp.mean(values, axis=-1, keepdims=True)
    spread = jnp.mean(center * center, axis=-1, keepdims=True)
    return center * lax.rsqrt(spread + 1e-05) * gain + shift


def unit_norm(values):
    center = values - jnp.mean(values, axis=-1, keepdims=True)
    spread = jnp.mean(center * center, axis=-1, keepdims=True)
    return center * lax.rsqrt(spread + 1e-05)


def smooth_gate(values):
    return jax.nn.gelu(values, approximate=True)


def dot_rows(left, right):
    return lax.dot_general(left, right, (((0,), (0,)), ((), ())), preferred_element_type=F32)


def dot_cols(left, right):
    return lax.dot_general(left, right, (((1,), (1,)), ((), ())), preferred_element_type=F32)


def dot(left, right):
    return jnp.dot(left, right, preferred_element_type=F32)


def make_local(n_replica, n_shard):
    n_pos = n_shard // 2
    half = n_pos // 2
    head_a_shard = n_shard == HEADS
    n_pairs = n_replica // 2
    pair_groups = [[2 * i + j for i in range(n_pairs)] for j in range(2)]

    def every(move):
        pairs = []
        for r in range(n_replica):
            for p in range(n_pos):
                for c in range(2):
                    to = move(r, p, c)
                    if to is not None:
                        pairs.append((r * n_shard + p * 2 + c, to[0] * n_shard + to[1] * 2 + to[2]))
        return pairs

    ring = list(range(0, n_pos, 2)) + list(range(n_pos - 1, 0, -2))
    after = {p: ring[(i + 1) % n_pos] for i, p in enumerate(ring)}
    before = {p: ring[i - 1] for i, p in enumerate(ring)}
    core_pairs = every(lambda r, p, c: (r, p, 1 - c))
    copy_pairs = every(lambda r, p, c: (r ^ 1, p, c))
    next_pairs = every(lambda r, p, c: (r, after[p], c))
    back_pairs = every(lambda r, p, c: (r, before[p], c))
    lend_pairs = every(lambda r, p, c: (r, p ^ 1, c) if p % 2 == r % 2 else None)
    give_pairs = every(lambda r, p, c: (r, p ^ 1, c) if p % 2 != r % 2 else None)
    share_pairs = every(lambda r, p, c: (r ^ 1, p, c) if p % 2 == r % 2 else None)

    def to_core(v):
        return lax.ppermute(v, MESH_AXES, core_pairs)

    def to_copy(v):
        return lax.ppermute(v, MESH_AXES, copy_pairs)

    def to_next(v):
        return lax.ppermute(v, MESH_AXES, next_pairs)

    def to_back(v):
        return lax.ppermute(v, MESH_AXES, back_pairs)

    def cut(rows):
        return max(16, rows // 32 * 16)

    def ring_gather(chunk, place, origin):
        low = cut(chunk.shape[0])
        full = jnp.zeros((n_pos,) + chunk.shape, chunk.dtype)

        def put(full, value, offset, row=0):
            return lax.dynamic_update_slice(full, value[None], (origin(place + offset), row, 0))

        full = put(full, chunk, 0)
        forth = back = chunk
        for step in range(1, half):
            forth = to_next(forth)
            back = to_back(back)
            full = put(full, forth, -step)
            full = put(full, back, step)
        forth = to_next(forth[:low])
        back = to_back(back[low:])
        full = put(full, forth, half)
        full = put(full, back, half, low)
        return full

    def ring_scatter(full, place, origin):
        low = cut(full.shape[1])

        def term(offset):
            return lax.dynamic_index_in_dim(full, origin(place + offset), 0, keepdims=False)

        def add(left, right):
            return (left.astype(F32) + right.astype(F32)).astype(BF16)

        far = term(half)
        forth = to_next(far[:low])
        back = to_back(far[low:])
        ahead = term(half - 1)
        behind = term(1 - half)
        forth = to_next(jnp.concatenate([add(forth, ahead[:low]), ahead[low:]]))
        back = to_back(jnp.concatenate([behind[:low], add(back, behind[low:])]))
        for step in range(half - 2, 0, -1):
            forth = to_next(add(forth, term(step)))
            back = to_back(add(back, term(-step)))
        return term(0).astype(F32) + forth.astype(F32) + back.astype(F32)

    def group_gather(block):
        other = to_copy(block)
        return jnp.stack([block, to_core(block), other, to_core(other)])

    def group_scatter(parts):
        near = to_core(jnp.stack([parts[1], parts[3]]).astype(BF16)).astype(F32)
        away = to_copy((parts[2] + near[1]).astype(BF16)).astype(F32)
        return parts[0] + near[0] + away

    def local(
        tokens,
        segments,
        counts,
        ln1_gain,
        ln1_bias,
        w_qkv,
        bias_query,
        bias_value,
        w_proj,
        bias_proj,
        ln2_gain,
        ln2_bias,
        w_fc,
        bias_fc,
        w_out,
        bias_out,
        cotangent,
    ):
        row_count, width = tokens.shape
        head_width = width // HEADS
        own_rows = width // n_shard
        chip_rows = 2 * own_rows
        own_hidden = w_out.shape[0]
        piece = own_hidden // 2
        groups = HEADS // RANKS
        scale = head_width ** (-0.5)
        replica_at = lax.axis_index("replica")
        shard_at = lax.axis_index("shard")
        x = replica_at % 2
        c = shard_at % 2
        p = shard_at // 2
        rank = 2 * x + c
        place = jnp.where(p % 2 == 0, p // 2, n_pos - 1 - p // 2)

        def origin(index):
            index = index % n_pos
            return jnp.where(index < half, 2 * index, 2 * (n_pos - 1 - index) + 1)

        def by_core(mine, other):
            return jnp.where(c == 0, jnp.stack([mine, other]), jnp.stack([other, mine]))

        position = jnp.arange(row_count, dtype=jnp.int32)
        in_use = (position < counts[0]).astype(F32)
        notes = jnp.stack([segments.astype(BF16), in_use.astype(BF16)])
        notes = jnp.pad(notes, ((0, SMALL_ROWS - 2), (0, width - row_count)))
        seen = group_gather(jnp.concatenate([tokens, notes]))
        tokens_all = seen[:, :row_count].reshape(RANKS * row_count, width)
        seg_all = seen[:, row_count, :row_count]
        use_all = seen[:, row_count + 1, :row_count]

        def qkv_part(which):
            view = w_qkv.reshape(own_rows, 3, groups, RANKS, head_width)
            return lax.dynamic_index_in_dim(view, which, 3, keepdims=False).reshape(own_rows, -1)

        def fc_part(core):
            view = w_fc.reshape(own_rows, n_pos, 4, piece)
            part = lax.dynamic_index_in_dim(view, 2 * core + x, 2, keepdims=False)
            return part.reshape(own_rows, -1)

        vectors = [ln1_gain, ln1_bias, bias_query, bias_value, bias_proj, ln2_gain, ln2_bias, bias_out, bias_fc]
        starts = [0]
        for vector in vectors:
            starts.append(starts[-1] + vector.shape[0])
        n_small = starts[-1]
        qkv_width = 3 * groups * head_width
        small = jnp.concatenate(vectors)[None]
        small = jnp.pad(small, ((0, SMALL_ROWS - 1), (0, 0)))
        both_small = by_core(small[0], to_core(small)[0])
        qkv_chunk = by_core(qkv_part(rank), to_core(qkv_part(rank ^ 1))).reshape(chip_rows, qkv_width)
        if head_a_shard:
            lent = lax.ppermute(w_proj[:, width // 2 :], MESH_AXES, lend_pairs)
            proj_half = jnp.where(p % 2 == x, w_proj[:, : width // 2], lent)
            proj_chunk = jnp.concatenate([proj_half[:, : width // 4], proj_half[:, width // 4 :]])
        else:
            proj_chunk = jnp.zeros((chip_rows, width // 4), BF16)
        small_chunk = jnp.pad(both_small, ((0, SMALL_ROWS - 2), (0, width - n_small)))
        first_chunk = jnp.concatenate(
            [jnp.concatenate([qkv_chunk, proj_chunk], axis=1), small_chunk]
        )
        fc_chunk = by_core(fc_part(c), to_core(fc_part(1 - c))).reshape(chip_rows, n_pos * piece)
        out_chunk = lax.dynamic_slice_in_dim(w_out, x * piece, piece, 0)

        first_full = ring_gather(first_chunk, place, origin)
        fc_weight = ring_gather(fc_chunk, place, origin).reshape(width, n_pos * piece)
        out_weight = ring_gather(out_chunk, place, origin).reshape(n_pos * piece, width)

        qkv_weight = first_full[:, :chip_rows, :qkv_width].reshape(width, qkv_width)
        if head_a_shard:
            proj_full = first_full[:, :chip_rows, qkv_width:].reshape(
                n_pos // 2, 2, 2, own_rows, width // 4
            )
            proj_full = jnp.where(x == 0, proj_full, proj_full[:, ::-1])
            proj_weight = proj_full.transpose(0, 3, 1, 2, 4).reshape(groups * head_width, width)
        else:
            proj_full = lax.all_gather(w_proj, "shard", axis=0, tiled=True)
            proj_full = proj_full.reshape(groups, RANKS, head_width, width)
            proj_weight = lax.dynamic_index_in_dim(proj_full, rank, 1, keepdims=False)
            proj_weight = proj_weight.reshape(groups * head_width, width)
        smalls = first_full[:, chip_rows : chip_rows + 2, :n_small].reshape(n_shard, n_small)
        params = [
            smalls[:, starts[i] : starts[i + 1]].reshape(-1).astype(F32) for i in range(len(vectors))
        ]
        gain_one, shift_one, query_shift, value_shift, proj_shift, gain_two, shift_two, out_shift, fc_shift = params

        def rank_heads(vector):
            view = vector.reshape(groups, RANKS, head_width)
            return lax.dynamic_index_in_dim(view, rank, 1, keepdims=False).reshape(-1)

        fc_shift = lax.dynamic_index_in_dim(
            fc_shift.reshape(n_pos, 4, piece), 2 * c + x, 1, keepdims=False
        ).reshape(-1)
        qkv_shift = jnp.concatenate(
            [
                rank_heads(query_shift),
                jnp.zeros((groups * head_width,), F32),
                rank_heads(value_shift),
            ]
        )

        unit_one = unit_norm(tokens_all.astype(F32))
        input_one = (unit_one * gain_one + shift_one).astype(BF16)
        qkv_rows = (dot(input_one, qkv_weight) + qkv_shift).astype(BF16)
        qkv_view = qkv_rows.reshape(RANKS, row_count, 3, groups, head_width)
        queries, keys_rows, values_rows = qkv_view[:, :, 0], qkv_view[:, :, 1], qkv_view[:, :, 2]
        visible = (
            (seg_all[:, :, None] == seg_all[:, None, :])
            & (position[None, None, :] <= position[None, :, None])
            & (use_all[:, None, :] > 0)
        )[:, None]
        scores = scale * jnp.einsum("bqhd,bkhd->bhqk", queries, keys_rows, preferred_element_type=F32)
        scores = jnp.where(visible, scores, -1e30)
        top_score = jnp.max(scores, axis=-1, keepdims=True)
        expo = jnp.exp(scores - top_score)
        probs = expo / jnp.sum(expo, axis=-1, keepdims=True)
        probs_low = probs.astype(BF16)
        context = (
            jnp.einsum("bhqk,bkhd->bqhd", probs_low, values_rows, preferred_element_type=F32)
            .reshape(RANKS * row_count, groups * head_width)
            .astype(BF16)
        )
        block_shape = (RANKS, row_count, width)
        stream = tokens.astype(F32)
        middle = stream + proj_shift + group_scatter(dot(context, proj_weight).reshape(block_shape))

        normed_two, norm_two_back = jax.vjp(layer_norm, middle, gain_two, shift_two)
        input_two = group_gather(normed_two.astype(BF16)).reshape(RANKS * row_count, width)
        pre_act = dot(input_two, fc_weight) + fc_shift
        gate_value, gate_back = jax.vjp(smooth_gate, pre_act)
        hidden = gate_value.astype(BF16)
        branch_two = group_scatter(dot(hidden, out_weight).reshape(block_shape)) + out_shift
        mixed = (in_use[:, None] * (middle + branch_two)).astype(BF16)

        d_top = in_use[:, None] * cotangent.astype(F32)
        d_out = group_gather(d_top.astype(BF16)).reshape(RANKS * row_count, width)
        grad_w_out = dot_rows(hidden, d_out).astype(BF16).reshape(n_pos, piece, width)
        d_pre = gate_back(dot_cols(d_out, out_weight))[0].astype(BF16)
        grad_w_fc = dot_rows(input_two, d_pre).astype(BF16).reshape(n_pos, chip_rows, n_pos * piece)
        d_input_two = group_scatter(dot_cols(d_pre, fc_weight).reshape(block_shape))
        d_mid_norm, grad_gain_two, grad_shift_two = norm_two_back(d_input_two)
        d_middle = d_top + d_mid_norm
        own_w_out = ring_scatter(grad_w_out, place, origin)
        own_w_fc = ring_scatter(grad_w_fc, place, origin)

        d_branch = group_gather(d_middle.astype(BF16)).reshape(RANKS * row_count, width)
        grad_w_proj = dot_rows(context, d_branch)
        d_context = (
            dot_cols(d_branch, proj_weight)
            .astype(BF16)
            .reshape(RANKS, row_count, groups, head_width)
        )
        d_values = jnp.einsum("bhqk,bqhd->bkhd", probs_low, d_context, preferred_element_type=F32)
        d_probs = jnp.einsum("bqhd,bkhd->bhqk", d_context, values_rows, preferred_element_type=F32)
        d_scores = (
            probs * (d_probs - jnp.sum(probs * d_probs, axis=-1, keepdims=True))
        ).astype(BF16)
        d_queries = scale * jnp.einsum(
            "bhqk,bkhd->bqhd", d_scores, keys_rows, preferred_element_type=F32
        )
        d_keys = scale * jnp.einsum("bhqk,bqhd->bkhd", d_scores, queries, preferred_element_type=F32)
        d_qkv = (
            jnp.stack([d_queries, d_keys, d_values], axis=2)
            .reshape(RANKS * row_count, qkv_width)
            .astype(BF16)
        )
        grad_w_qkv = dot_rows(input_one, d_qkv).astype(BF16).reshape(n_pos, chip_rows, qkv_width)
        d_input_one = dot_cols(d_qkv, qkv_weight)
        grad_gain_one = jnp.sum(d_input_one * unit_one, axis=0)
        grad_shift_one = jnp.sum(d_input_one, axis=0)
        d_qkv_sums = jnp.sum(d_qkv.astype(F32), axis=0)

        def own_term(values):
            return jnp.sum(values.astype(BF16).astype(F32), axis=0)

        def at_rank(sums):
            view = sums.reshape(groups, 1, head_width)
            mine = jnp.arange(RANKS)[None, :, None] == rank
            return jnp.where(mine, view, 0.0).reshape(-1)

        fc_sums = jnp.sum(d_pre.astype(F32), axis=0).reshape(n_pos, 1, piece)
        fc_sums = jnp.where(jnp.arange(4)[None, :, None] == 2 * c + x, fc_sums, 0.0).reshape(-1)
        small_terms = [
            grad_gain_one,
            grad_shift_one,
            at_rank(d_qkv_sums[: groups * head_width]),
            at_rank(d_qkv_sums[2 * groups * head_width :]),
            own_term(d_middle),
            grad_gain_two,
            grad_shift_two,
            own_term(d_top),
            fc_sums,
        ]
        small_terms = jnp.concatenate(
            [term.reshape(n_shard, -1) for term in small_terms], axis=1
        ).astype(BF16)
        small_terms = jnp.pad(
            small_terms.reshape(n_pos, 2, n_small),
            ((0, 0), (0, SMALL_ROWS - 2), (0, width - n_small)),
        )
        if head_a_shard:
            proj_terms = grad_w_proj.astype(BF16).reshape(n_pos // 2, own_rows, 2, 2, width // 4)
            proj_terms = proj_terms.transpose(0, 2, 3, 1, 4)
            proj_terms = jnp.where(x == 0, proj_terms, proj_terms[:, ::-1])
            proj_terms = proj_terms.reshape(n_pos, chip_rows, width // 4)
        else:
            proj_terms = jnp.zeros((n_pos, chip_rows, width // 4), BF16)
        first_terms = jnp.concatenate(
            [jnp.concatenate([grad_w_qkv, proj_terms], axis=2), small_terms], axis=1
        )
        own_first = ring_scatter(first_terms, place, origin)
        d_in_norm = jax.vjp(unit_norm, stream)[1](
            group_scatter(d_input_one.reshape(block_shape)) * gain_one
        )[0]
        grad_tokens = d_middle + d_in_norm

        def rows_of(chunk, core):
            return lax.dynamic_slice_in_dim(chunk, core * own_rows, own_rows, 0)

        def by_copy(mine, other):
            return jnp.where(x == 0, jnp.stack([mine, other]), jnp.stack([other, mine]))

        own_w_out = own_w_out.astype(BF16)
        grad_w_out = by_copy(own_w_out, to_copy(own_w_out)).reshape(own_hidden, width)

        own_w_fc = own_w_fc.astype(BF16)
        fc_rows = by_core(rows_of(own_w_fc, c), to_core(rows_of(own_w_fc, 1 - c)))
        fc_rows = by_copy(fc_rows, to_copy(fc_rows))
        fc_rows = fc_rows.reshape(2, 2, own_rows, n_pos, piece)
        grad_w_fc = fc_rows.transpose(2, 3, 1, 0, 4).reshape(own_rows, -1)

        own_first = own_first.astype(BF16)
        own_qkv = own_first[:chip_rows, :qkv_width]
        qkv_grad = by_core(rows_of(own_qkv, c), to_core(rows_of(own_qkv, 1 - c)))
        qkv_grad = by_copy(qkv_grad, to_copy(qkv_grad))
        qkv_grad = qkv_grad.reshape(2, 2, own_rows, 3, groups, head_width)
        grad_w_qkv = qkv_grad.transpose(2, 3, 4, 0, 1, 5).reshape(own_rows, -1)

        own_small = own_first[chip_rows:, :n_small]
        near_small = to_core(own_small)
        small_sum = jnp.where(
            c == 0,
            own_small[0].astype(F32) + near_small[0].astype(F32),
            own_small[1].astype(F32) + near_small[1].astype(F32),
        )
        small_send = jnp.pad(small_sum[None].astype(BF16), ((0, SMALL_ROWS - 1), (0, 0)))
        small_sum = small_sum + to_copy(small_send)[0].astype(F32)

        if head_a_shard:
            own_proj = own_first[:chip_rows, qkv_width:]
            given = lax.ppermute(own_proj, MESH_AXES, give_pairs)
            proj_rows = jnp.stack([own_proj, given]).reshape(2, 2, own_rows, width // 4)
            proj_rows = proj_rows.transpose(2, 0, 1, 3).reshape(own_rows, width)
            shared = lax.ppermute(proj_rows, MESH_AXES, share_pairs)
            grad_w_proj = jnp.where(p % 2 == x, proj_rows, shared)
        else:
            proj_rows = grad_w_proj.astype(BF16).reshape(groups, 1, head_width, width)
            mine = jnp.arange(RANKS)[None, :, None, None] == rank
            proj_rows = jnp.where(mine, proj_rows, 0).reshape(width, width)
            proj_rows = lax.psum_scatter(proj_rows, "shard", scatter_dimension=0, tiled=True)
            grad_w_proj = proj_rows.astype(F32) + to_copy(proj_rows).astype(F32)

        if n_pairs > 1:
            grad_w_out, grad_w_fc, grad_w_qkv, grad_w_proj, small_sum = lax.psum(
                tuple(
                    value.astype(BF16)
                    for value in (grad_w_out, grad_w_fc, grad_w_qkv, grad_w_proj, small_sum)
                ),
                "replica",
                axis_index_groups=pair_groups,
            )
        small_sum = small_sum.astype(F32)
        small_grads = [small_sum[starts[i] : starts[i + 1]] for i in range(len(vectors))]
        g_gain_one, g_shift_one, g_query, g_value, g_proj, g_gain_two, g_shift_two, g_out, g_fc = small_grads
        return (
            mixed,
            grad_tokens,
            g_gain_one,
            g_shift_one,
            grad_w_qkv.astype(F32),
            g_query,
            g_value,
            grad_w_proj.astype(F32),
            g_proj,
            g_gain_two,
            g_shift_two,
            grad_w_fc.astype(F32),
            g_fc,
            grad_w_out.astype(F32),
            g_out,
        )

    return local

LANES = 128
HALF = 64
VMEM_BYTES = 26 * 1024 * 1024
ORIGINS = 9
AT_X, AT_C, AT_Y, AT_COUNT = 9, 10, 11, 12
VMEM_SPEC = pl.BlockSpec(memory_space=pltpu.VMEM)
SMEM_SPEC = pl.BlockSpec(memory_space=pltpu.SMEM)
ANY_SPEC = pl.BlockSpec(memory_space=pl.ANY)
HBM_SPEC = pl.BlockSpec(memory_space=pltpu.HBM)


def kernel_call(body, in_specs, outs, scratch=(), micros=1):
    return pl.pallas_call(
        body,
        out_shape=tuple(jax.ShapeDtypeStruct(shape, dtype) for shape, dtype in outs),
        in_specs=list(in_specs),
        out_specs=tuple(VMEM_SPEC for _ in outs),
        scratch_shapes=list(scratch),
        compiler_params=pltpu.CompilerParams(vmem_limit_bytes=VMEM_BYTES),
        cost_estimate=pl.CostEstimate(
            flops=0, bytes_accessed=micros * 3_000_000, transcendentals=0
        ),
    )


def low_half(shape):
    return lax.broadcasted_iota(jnp.int32, shape, len(shape) - 1) < HALF


def turn(values):
    return jnp.concatenate([values[:, HALF:], values[:, :HALF]], axis=1)


def join(c, first, second, low):
    even = jnp.where(low, first, turn(second))
    odd = jnp.where(low, turn(first), second)
    return jnp.where(c == 0, even, odd)


def statistics(values):
    center = values - jnp.mean(values, axis=-1, keepdims=True)
    spread = jnp.mean(center * center, axis=-1, keepdims=True)
    return center, lax.rsqrt(spread + 1e-05)


def norm_back(unit, inverse, d_unit):
    along = jnp.mean(d_unit * unit, axis=-1, keepdims=True)
    return inverse * (d_unit - jnp.mean(d_unit, axis=-1, keepdims=True) - unit * along)


def used_rows(info, rows):
    return (lax.broadcasted_iota(jnp.int32, (rows, 1), 0) < info[AT_COUNT]).astype(F32)


def tokens_body(info, tokens, segments, cotangent, block, d_out):
    rows = tokens.shape[0]
    block[:rows, :] = tokens[...]
    down = lax.broadcasted_iota(jnp.int32, (SMALL_ROWS, rows), 0)
    across = lax.broadcasted_iota(jnp.int32, (SMALL_ROWS, rows), 1)
    used = jnp.where(across < info[AT_COUNT], 1.0, 0.0)
    notes = jnp.where(down == 0, segments[...].astype(F32), jnp.where(down == 1, used, 0.0))
    block[rows:, :rows] = notes.astype(BF16)
    d_out[...] = (used_rows(info, rows) * cotangent[...].astype(F32)).astype(BF16)


def own_part_body(info, w_qkv, w_proj, groups, half):
    x = info[AT_X]
    for z in range(w_qkv.shape[1] // (4 * HALF)):
        at = pl.ds(pl.multiple_of(z * 4 * HALF + x * LANES, LANES), LANES)
        groups[:, z * LANES : (z + 1) * LANES] = w_qkv[:, at]
    half[...] = w_proj[:, : half.shape[1]]


def first_chunk_body(info, groups, got_qkv, left, lent, vectors, got_vectors, first):
    own_rows = left.shape[0]
    width = 2 * left.shape[1]
    x, c, y = info[AT_X], info[AT_C], info[AT_Y]
    qkv = 3 * width // 4
    low = low_half((own_rows, LANES))
    for core in range(2):
        rows = slice(core * own_rows, (core + 1) * own_rows)
        for pair in range(groups.shape[1] // (2 * LANES)):
            both = []
            for z in (2 * pair, 2 * pair + 1):
                at = pl.ds(pl.multiple_of(z * 4 * HALF + x * LANES, LANES), LANES)
                mine = groups[:, z * LANES : (z + 1) * LANES]
                both.append(jnp.where(c == core, mine, got_qkv[:, at]).astype(F32))
            first[rows, pair * LANES : (pair + 1) * LANES] = join(c, *both, low).astype(BF16)
    half = jnp.where(x == y, left[...], lent[:, width // 2 :])
    first[:own_rows, qkv:] = half[:, : width // 4]
    first[own_rows : 2 * own_rows, qkv:] = half[:, width // 4 :]
    mine = vectors[0:8, :].astype(F32)
    other = got_vectors[0:8, :].astype(F32)
    shifts = vectors[8:16, :].astype(F32)
    blank = jnp.zeros(mine.shape, F32)
    lower = jnp.concatenate([jnp.where(c == 0, mine, other), blank], axis=1)
    upper = jnp.concatenate([blank, jnp.where(c == 0, other, mine)], axis=1)
    small = lower + upper
    wide = jnp.concatenate([mine, blank], axis=1)
    heads = jnp.where(low_half((1, LANES)), wide[6:7], turn(wide)[7:8])
    shifts = jnp.concatenate([shifts, blank], axis=1)
    shifts = jnp.where(x == 0, shifts, jnp.concatenate([shifts[2:], shifts[:2]], axis=0))
    shift = jnp.where(low_half((1, LANES)), shifts[0:1], turn(shifts)[1:2])
    row = lax.broadcasted_iota(jnp.int32, small.shape, 0)
    small = jnp.where(row == 6, shift, jnp.where(row == 7, heads, small))
    first[2 * own_rows :, :] = jnp.zeros((SMALL_ROWS, width), BF16)
    first[2 * own_rows : 2 * own_rows + 8, :LANES] = small.astype(BF16)


def second_chunk_body(info, w_fc, got_fc, w_out, chunk, sems):
    own_rows = w_fc.shape[0]
    piece = w_out.shape[0] // 2
    x, c = info[AT_X], info[AT_C]
    source = pl.ds(pl.multiple_of(x * piece, piece), piece)
    copies = [(w_out.at[source, :], chunk.at[pl.ds(2 * own_rows, piece), :])]
    for p in range(w_fc.shape[1] // (4 * LANES)):
        source = pl.ds(pl.multiple_of(p * 4 * LANES + (2 * c + x) * LANES, LANES), LANES)
        lanes = pl.ds(p * LANES, LANES)
        for weight, core in ((w_fc, c), (got_fc, 1 - c)):
            row = pl.multiple_of(core * own_rows, own_rows)
            copies.append((weight.at[:, source], chunk.at[pl.ds(row, own_rows), lanes]))
    for copy in run_copies(copies, sems):
        copy.wait()


def run_copies(copies, sems):
    started = []
    for i, (source, target) in enumerate(copies):
        copy = pltpu.make_async_copy(source, target, sems.at[i])
        copy.start()
        started.append(copy)
    return started


def blocks_body(*refs):
    blocks = refs[:RANKS]
    units, masks = refs[RANKS:]
    rows = units.shape[0] // RANKS
    down = lax.broadcasted_iota(jnp.int32, (rows, rows), 0)
    across = lax.broadcasted_iota(jnp.int32, (rows, rows), 1)
    for b, block in enumerate(blocks):
        center, inverse = statistics(block[:rows, :].astype(F32))
        units[b * rows : (b + 1) * rows, :] = center * inverse
        notes = block[rows : rows + SMALL_ROWS, : 2 * LANES].astype(F32)
        seg_row, use_row = notes[0:1, :rows], notes[1:2, :rows]
        seg_column = jnp.sum(jnp.where(down == across, seg_row, 0.0), axis=1, keepdims=True)
        visible = (seg_column == seg_row) & (across <= down) & (use_row > 0)
        masks[b] = jnp.where(visible, 1.0, 0.0)


def attention_body(info, *refs):
    units, masks, chunks = refs[0], refs[1], refs[2 : 2 + ORIGINS]
    normed, qkv, probs, context, send_own, send_away, keep_own, keep_away = refs[2 + ORIGINS : 10 + ORIGINS]
    qkv_weight, proj_weight, smalls, sems = refs[10 + ORIGINS :]
    x = info[AT_X]
    width = normed.shape[1]
    rows = normed.shape[0] // RANKS
    chip_rows = chunks[0].shape[0] - SMALL_ROWS
    own_rows = chip_rows // 2
    cols = 3 * width // 4
    copies = []
    for i, chunk in enumerate(chunks):
        at = info[i]
        start = chunks[i - 1].shape[0] if i == ORIGINS - 1 else 0
        stop = start + chunk.shape[0]
        for part in range(2):
            top = part * own_rows
            if start <= top and top + own_rows <= stop:
                source = pl.ds(top - start, own_rows)
                copies.append(
                    (
                        chunk.at[source, pl.ds(0, cols)],
                        qkv_weight.at[pl.ds(pl.multiple_of(at * chip_rows + top, own_rows), own_rows), :],
                    )
                )
                side = lax.rem(at + x, 2) * (width // 2) + part * (width // 4)
                copies.append(
                    (
                        chunk.at[source, pl.ds(cols, width // 4)],
                        proj_weight.at[
                            pl.ds(pl.multiple_of(lax.div(at, 2) * own_rows, own_rows), own_rows),
                            pl.ds(pl.multiple_of(side, LANES), width // 4),
                        ],
                    )
                )
        if stop > chip_rows:
            copies.append(
                (
                    chunk.at[pl.ds(chip_rows - start, SMALL_ROWS), pl.ds(0, LANES)],
                    smalls.at[:, pl.ds(pl.multiple_of(at * LANES, LANES), LANES)],
                )
            )
    started = run_copies(copies, sems)

    for copy in started:
        copy.wait()
    gain = smalls[0:1, :].astype(F32)
    shift = smalls[1:2, :].astype(F32)
    normed[...] = (units[...] * gain + shift).astype(BF16)

    low_row = low_half((8, LANES))
    biases = jnp.broadcast_to(smalls[7:8, :].astype(F32), (8, width))
    query_shift, value_shift = [], []
    for pair in range(2):
        first, second = (
            jnp.where(
                x == 0,
                biases[:, z * 2 * LANES : z * 2 * LANES + LANES],
                biases[:, z * 2 * LANES + LANES : (z + 1) * 2 * LANES],
            )
            for z in (2 * pair, 2 * pair + 1)
        )
        query_shift.append(jnp.where(low_row, first, turn(second))[0:1])
        value_shift.append(jnp.where(low_row, turn(first), second)[0:1])
    third = width // 4
    for n in range(3):
        product = dot(normed[...], qkv_weight[:, n * third : (n + 1) * third])
        if n != 1:
            product = product + jnp.concatenate(value_shift if n else query_shift, axis=1)
        qkv[:, n * third : (n + 1) * third] = product.astype(BF16)

    scale = HALF ** (-0.5)
    low = low_half((1, LANES))
    keep_low = jnp.where(low, 1.0, 0.0).astype(BF16)
    keep_high = jnp.where(low, 0.0, 1.0).astype(BF16)

    def attend(b, carry):
        at = pl.ds(pl.multiple_of(b * rows, rows), rows)
        mask = masks[b] > 0.5
        for pair in range(2):
            lanes = pair * LANES
            queries = qkv[at, lanes : lanes + LANES]
            keys = qkv[at, third + lanes : third + lanes + LANES]
            values = qkv[at, 2 * third + lanes : 2 * third + lanes + LANES]
            outs = []
            for side, keep in enumerate((keep_low, keep_high)):
                scores = jnp.where(mask, scale * dot_cols(queries * keep, keys), -1e30)
                expo = jnp.exp(scores - jnp.max(scores, axis=-1, keepdims=True))
                share = (expo / jnp.sum(expo, axis=-1, keepdims=True)).astype(BF16)
                probs[b * 4 + 2 * pair + side] = share
                outs.append(dot(share, values))
            context[at, lanes : lanes + LANES] = jnp.where(low, outs[0], outs[1]).astype(BF16)
        return carry

    lax.fori_loop(0, RANKS, attend, 0, unroll=True)
    for n in range(4):
        columns = slice(n * third, (n + 1) * third)
        store_parts(dot(context[...], proj_weight[:, columns]), columns, rows, send_own, send_away, keep_own, keep_away)


def store_parts(product, columns, rows, send_own, send_away, keep_own, keep_away):
    keep_own[:, columns] = product[:rows]
    send_own[:, columns] = product[rows : 2 * rows].astype(BF16)
    keep_away[:, columns] = product[2 * rows : 3 * rows]
    send_away[:, columns] = product[3 * rows :].astype(BF16)


def total(keep, near, far):
    return keep[...] + near[...].astype(F32) + far.astype(F32)


def add_body(left, right, result):
    result[...] = add(left[...], right[...])


def message_body(keep_own, keep_away, near_own, near_away, message):
    message[0] = (keep_own[...] + near_own[...].astype(F32)).astype(BF16)
    message[1] = (keep_away[...] + near_away[...].astype(F32)).astype(BF16)


def second_norm_body(
    block, block_other, keep_own, keep_away, near_own, near_away, got, smalls, middle, normed
):
    rows = keep_own.shape[0]
    gain, shift = smalls[3:4, :].astype(F32), smalls[4:5, :].astype(F32)
    both = ((block, keep_own, near_own), (block_other, keep_away, near_away))
    for i, (tokens, keep, near) in enumerate(both):
        values = tokens[:rows, :].astype(F32) + smalls[2:3, :].astype(F32)
        values = values + total(keep, near, got[1 - i])
        middle[i] = values
        center, inverse = statistics(values)
        normed[i] = (center * inverse * gain + shift).astype(BF16)


def feed_body(info, normed, beside, *refs):
    d_outs = refs[:RANKS]
    chunks, smalls = refs[RANKS : RANKS + ORIGINS], refs[RANKS + ORIGINS]
    given, d_out, hidden, d_pre, send_own, send_away, keep_own, keep_away = refs[
        RANKS + ORIGINS + 1 : RANKS + ORIGINS + 9
    ]
    sums, out_weight, fc_weight, sems = refs[RANKS + ORIGINS + 9 :]
    rows = normed.shape[1]
    width = given.shape[1]
    chip_rows = chunks[0].shape[0] // 2
    copies = []
    for i, chunk in enumerate(chunks):
        at = pl.ds(pl.multiple_of(info[i] * chip_rows, chip_rows), chip_rows)
        if i != ORIGINS - 1:
            copies.append((chunk.at[pl.ds(0, chip_rows), :], fc_weight.at[at, :]))
        if i != ORIGINS - 2:
            start = 0 if i == ORIGINS - 1 else chip_rows
            copies.append((chunk.at[pl.ds(start, chip_rows), :], out_weight.at[at, :]))
    started = run_copies(copies, sems)
    for b in range(RANKS):
        given[b * rows : (b + 1) * rows, :] = (beside if b % 2 else normed)[b // 2]
        d_out[b * rows : (b + 1) * rows, :] = d_outs[b][...]
    for copy in started:
        copy.wait()
    tile = 2 * LANES
    root = (2.0 / jnp.pi) ** 0.5
    sums[...] = jnp.zeros(sums.shape, F32)

    def units(n, carry):
        columns = pl.ds(pl.multiple_of(n * tile, tile), tile)
        pre = dot(given[...], fc_weight[:, columns]) + smalls[6:7, columns].astype(F32)
        d_hidden = dot_cols(d_out[...], out_weight[columns, :])
        square = pre * pre
        bend = jnp.tanh(root * pre * (1.0 + 0.044715 * square))
        hidden[:, columns] = (0.5 * pre * (1.0 + bend)).astype(BF16)
        slope = 0.5 * (1.0 + bend) + 0.5 * pre * (1.0 - bend * bend) * root * (
            1.0 + 3.0 * 0.044715 * square
        )
        low = (d_hidden * slope).astype(BF16)
        d_pre[:, columns] = low
        sums[6:7, columns] = jnp.sum(low.astype(F32), axis=0, keepdims=True)
        return carry

    lax.fori_loop(0, width // tile, units, 0, unroll=True)
    for n in range(width // tile):
        columns = slice(n * tile, (n + 1) * tile)
        product = dot_cols(d_pre[...], fc_weight[columns, :])
        store_parts(product, columns, rows, send_own, send_away, keep_own, keep_away)


def feed_out_body(hidden, out_weight, send_own, send_away, keep_own, keep_away):
    rows = keep_own.shape[0]
    tile = 2 * LANES
    for n in range(out_weight.shape[1] // tile):
        columns = slice(n * tile, (n + 1) * tile)
        store_parts(dot(hidden[...], out_weight[:, columns]), columns, rows, send_own, send_away, keep_own, keep_away)


def mixed_body(info, middle, keep_own, near, away, smalls, mixed):
    values = middle[0] + total(keep_own, near, away[...]) + smalls[5:6, :].astype(F32)
    mixed[...] = (used_rows(info, keep_own.shape[0]) * values).astype(BF16)


def second_back_body(
    middle, d_top, d_other, keep_own, keep_away, near_own, near_away, got, smalls, d_middle, branch_own, branch_away, sums
):
    gain = smalls[3:4, :].astype(F32)
    both = ((d_top, keep_own, near_own), (d_other, keep_away, near_away))
    for i, (d_out, keep, near) in enumerate(both):
        d_values = total(keep, near, got[1 - i])
        center, inverse = statistics(middle[i])
        unit = center * inverse
        result = d_out[...].astype(F32) + norm_back(unit, inverse, d_values * gain)
        low = result.astype(BF16)
        (branch_own if i == 0 else branch_away)[...] = low
        if i == 0:
            d_middle[...] = result
            sums[...] = jnp.zeros(sums.shape, F32)
            sums[2:3, :] = jnp.sum(low.astype(F32), axis=0, keepdims=True)
            sums[3:4, :] = jnp.sum(d_values * unit, axis=0, keepdims=True)
            sums[4:5, :] = jnp.sum(d_values, axis=0, keepdims=True)
            sums[5:6, :] = jnp.sum(d_out[...].astype(F32), axis=0, keepdims=True)


def attention_back_body(info, *refs):
    branches, units, refs = refs[:RANKS], refs[RANKS], refs[RANKS + 1 :]
    qkv, probs, qkv_weight, proj_weight, sums_two, sums_fc = refs[:6]
    d_branch, d_qkv, send_own, send_away, keep_own, keep_away, sums, d_context = refs[6:]
    rows = branches[0].shape[0]
    width = d_branch.shape[1]
    third = width // 4
    x = info[AT_X]
    for b in range(RANKS):
        d_branch[b * rows : (b + 1) * rows, :] = branches[b][...]
    d_context[...] = dot_cols(d_branch[...], proj_weight[...]).astype(BF16)
    scale = HALF ** (-0.5)
    low = low_half((1, LANES))
    keep_low = jnp.where(low, 1.0, 0.0).astype(BF16)
    keep_high = jnp.where(low, 0.0, 1.0).astype(BF16)

    def attend(b, carry):
        at = pl.ds(pl.multiple_of(b * rows, rows), rows)
        for pair in range(2):
            lanes = pair * LANES
            queries = qkv[at, lanes : lanes + LANES]
            keys = qkv[at, third + lanes : third + lanes + LANES]
            values = qkv[at, 2 * third + lanes : 2 * third + lanes + LANES]
            d_out = d_context[at, lanes : lanes + LANES]
            results = []
            for side, keep in enumerate((keep_low, keep_high)):
                share = probs[b * 4 + 2 * pair + side]
                wide = share.astype(F32)
                d_values = dot_rows(share, d_out)
                d_probs = dot_cols(d_out * keep, values)
                d_scores = wide * (d_probs - jnp.sum(wide * d_probs, axis=-1, keepdims=True))
                d_scores = d_scores.astype(BF16)
                results.append(
                    (scale * dot(d_scores, keys), scale * dot_rows(d_scores, queries), d_values)
                )
            for n in range(3):
                merged = jnp.where(low, results[0][n], results[1][n]).astype(BF16)
                d_qkv[at, n * third + lanes : n * third + lanes + LANES] = merged
        return carry

    lax.fori_loop(0, RANKS, attend, 0, unroll=True)
    sums[0:8, :] = sums_two[...] + sums_fc[...]
    sums[8:, :] = jnp.zeros((SMALL_ROWS - 8, width), F32)
    for n in range(4):
        columns = slice(n * third, (n + 1) * third)
        product = dot_cols(d_qkv[...], qkv_weight[columns, :])
        store_parts(product, columns, rows, send_own, send_away, keep_own, keep_away)
        sums[1:2, columns] = jnp.sum(product, axis=0, keepdims=True)
        sums[0:1, columns] = jnp.sum(product * units[:, columns], axis=0, keepdims=True)
    low_row = low_half((8, LANES))
    for pair in range(2):
        lanes = pair * LANES
        d_queries = jnp.sum(d_qkv[:, lanes : lanes + LANES].astype(F32), axis=0, keepdims=True)
        d_values = jnp.sum(
            d_qkv[:, 2 * third + lanes : 2 * third + lanes + LANES].astype(F32), axis=0, keepdims=True
        )
        d_queries = jnp.broadcast_to(d_queries, (8, LANES))
        d_values = jnp.broadcast_to(d_values, (8, LANES))
        even = jnp.where(low_row, d_queries, turn(d_values))[0:1]
        odd = jnp.where(low_row, turn(d_queries), d_values)[0:1]
        for z, group in ((2 * pair, even), (2 * pair + 1, odd)):
            for y in range(2):
                start = (2 * z + y) * LANES
                sums[7:8, start : start + LANES] = jnp.where(x == y, group, 0.0)


def first_back_body(tokens, d_middle, keep_own, near, away, smalls, result):
    center, inverse = statistics(tokens[...].astype(F32))
    d_unit = total(keep_own, near, away[...]) * smalls[0:1, :].astype(F32)
    result[...] = d_middle[...] + norm_back(center * inverse, inverse, d_unit)


def second_term(info, index, grad_fc, grad_out):
    at = info[index]
    results = []
    for grad in (grad_fc, grad_out):
        chip_rows = grad.shape[0] * 2 // HEADS
        results.append(grad[pl.ds(pl.multiple_of(at * chip_rows, chip_rows), chip_rows), :])
    return results


def add(left, right):
    return (left.astype(F32) + right.astype(F32)).astype(BF16)


def second_far_body(info, grad_fc, grad_out, forth, back):
    forth[...], back[...] = second_term(info, ORIGINS - 1, grad_fc, grad_out)


def second_hop_body(step, info, got_forth, got_back, grad_fc, grad_out, forth, back):
    rows = forth.shape[0] // 2
    for target, got, index, part in ((forth, got_forth, 2 * step, 0), (back, got_back, 2 * step - 1, 1)):
        terms = second_term(info, index, grad_fc, grad_out)
        for i in range(2):
            where = slice(i * rows, (i + 1) * rows)
            if got.shape[0] == rows:
                target[where, :] = add(terms[i], got[...]) if i == part else terms[i]
            else:
                target[where, :] = add(terms[i], got[where, :])


def second_last_body(info, got_forth, got_back, grad_fc, grad_out, own):
    terms = second_term(info, 0, grad_fc, grad_out)
    rows = own.shape[0] // 2
    for i in range(2):
        where = slice(i * rows, (i + 1) * rows)
        values = got_forth[where, :].astype(F32) + got_back[where, :].astype(F32)
        own[where, :] = add(values, terms[i])


def first_term(info, index, grad_qkv, grad_proj, sums):
    at = info[index]
    chip_rows = grad_qkv.shape[0] * 2 // HEADS
    own_rows = chip_rows // 2
    quarter = grad_proj.shape[1] // 4
    side = lax.rem(at + info[AT_X], 2) * 2 * quarter
    head = pl.ds(pl.multiple_of(lax.div(at, 2) * own_rows, own_rows), own_rows)
    results = []
    for part in range(2):
        rows = pl.ds(pl.multiple_of(at * chip_rows + part * own_rows, own_rows), own_rows)
        lanes = pl.ds(pl.multiple_of(side + part * quarter, LANES), quarter)
        results.append((grad_qkv[rows, :], grad_proj[head, lanes]))
    small = sums[:, pl.ds(pl.multiple_of(at * LANES, LANES), LANES)].astype(BF16)
    return results, small


def put_first(target, row, values, got, got_row):
    at = 0
    rows = values[0].shape[0]
    for value in values:
        lanes = slice(at, at + value.shape[1])
        if got is not None:
            value = add(value, got[got_row : got_row + rows, lanes])
        target[row : row + rows, lanes] = value
        at += value.shape[1]


def first_far_body(info, grad_qkv, grad_proj, sums, forth, back):
    (upper, lower), small = first_term(info, ORIGINS - 1, grad_qkv, grad_proj, sums)
    own_rows = forth.shape[0]
    put_first(forth, 0, upper, None, 0)
    put_first(back, 0, lower, None, 0)
    back[own_rows:, :] = jnp.zeros((SMALL_ROWS, back.shape[1]), BF16)
    put_first(back, own_rows, (small,), None, 0)


def first_hop_body(step, info, got_forth, got_back, grad_qkv, grad_proj, sums, forth, back):
    own_rows = (forth.shape[0] - SMALL_ROWS) // 2
    for target, got, index in ((forth, got_forth, 2 * step), (back, got_back, 2 * step - 1)):
        terms, small = first_term(info, index, grad_qkv, grad_proj, sums)
        shift = 0
        if got.shape[0] == own_rows:
            came = (got, None, None)
        elif got.shape[0] == own_rows + SMALL_ROWS:
            came, shift = (None, got, got), own_rows
        else:
            came = (got, got, got)
        target[2 * own_rows :, :] = jnp.zeros((SMALL_ROWS, target.shape[1]), BF16)
        for i, values in enumerate((*terms, (small,))):
            put_first(target, i * own_rows, values, came[i], i * own_rows - shift)


def first_last_body(info, got_forth, got_back, grad_qkv, grad_proj, sums, own):
    own_rows = (own.shape[0] - SMALL_ROWS) // 2
    terms, small = first_term(info, 0, grad_qkv, grad_proj, sums)
    own[2 * own_rows :, :] = jnp.zeros((SMALL_ROWS, own.shape[1]), BF16)
    for i, values in enumerate((*terms, (small,))):
        at = 0
        rows = slice(i * own_rows, i * own_rows + values[0].shape[0])
        for value in values:
            lanes = slice(at, at + value.shape[1])
            came = got_forth[rows, lanes].astype(F32) + got_back[rows, lanes].astype(F32)
            own[rows, lanes] = add(came, value)
            at += value.shape[1]


def four_parts(info, own, near, other, cross):
    x, c = info[AT_X], info[AT_C]

    def reader(copy, core):
        def read(rows, lanes):
            same = jnp.where(c == core, own[rows, lanes], near[rows, lanes])
            far = jnp.where(c == core, other[rows, lanes], cross[rows, lanes])
            return jnp.where(x == copy, same, far).astype(F32)

        return read

    return reader


def hidden_grads_body(info, own, near, other, cross, grad_fc, grad_out):
    x, c = info[AT_X], info[AT_C]
    own_rows = grad_fc.shape[0]
    width = own.shape[1]
    piece = grad_out.shape[0] // 2
    reader = four_parts(info, own, near, other, cross)
    rows = pl.ds(pl.multiple_of(c * own_rows, own_rows), own_rows)
    for copy in range(2):
        for core in range(2):
            read = reader(copy, core)
            for p in range(width // LANES):
                at = p * 4 * LANES + core * 2 * LANES + copy * LANES
                grad_fc[:, at : at + LANES] = read(rows, slice(p * LANES, (p + 1) * LANES))
        grad_out[copy * piece : (copy + 1) * piece, :] = jnp.where(
            x == copy, own[2 * own_rows :, :], other[2 * own_rows :, :]
        ).astype(F32)


def first_grads_body(info, own, near, other, cross, side, corner, grad_qkv, grad_proj, *small_outs):
    x, c, y = info[AT_X], info[AT_C], info[AT_Y]
    own_rows, width = grad_proj.shape
    qkv = 3 * width // 4
    quarter = width // 4
    low = low_half((own_rows, LANES))
    reader = four_parts(info, own, near, other, cross)
    rows = pl.ds(pl.multiple_of(c * own_rows, own_rows), own_rows)
    for copy in range(2):
        first, second = reader(copy, 0), reader(copy, 1)
        for pair in range(qkv // LANES):
            lanes = slice(pair * LANES, (pair + 1) * LANES)
            one, two = first(rows, lanes), second(rows, lanes)
            at = pair * 8 * HALF + copy * LANES
            grad_qkv[:, at : at + LANES] = jnp.where(low, one, turn(two))
            at += 4 * HALF
            grad_qkv[:, at : at + LANES] = jnp.where(low, turn(one), two)
    for part in range(2):
        block = slice(part * own_rows, (part + 1) * own_rows)
        left = jnp.where(x == y, own[block, qkv:], other[block, qkv:]).astype(F32)
        grad_proj[:, part * quarter : (part + 1) * quarter] = left
        right = jnp.where(x == y, side[block, :], corner[block, :]).astype(F32)
        grad_proj[:, 2 * quarter + part * quarter : 2 * quarter + (part + 1) * quarter] = right
    mine, beside, far, across = (
        ref[2 * own_rows :, :LANES].astype(F32) for ref in (own, near, other, cross)
    )
    summed = (mine + beside) + (far + across)
    summed = jnp.where(c == 0, summed, turn(summed))
    heads = jnp.where(x == y, mine, far)
    for i in range(6):
        small_outs[i][...] = summed[i : i + 1, :HALF]
    small_outs[6][0:1, :] = jnp.where(x == 0, mine, far)[6:7]
    small_outs[6][1:2, :] = jnp.where(x == 0, far, mine)[6:7]
    small_outs[7][...] = heads[7:8, :HALF]
    small_outs[8][...] = turn(heads)[7:8, :HALF]


def tie(*values):
    return lax.optimization_barrier(values)


def make_kernel_local(n_replica, n_shard):
    n_pos = n_shard // 2
    half = n_pos // 2

    def every(move):
        pairs = []
        for r in range(n_replica):
            for p in range(n_pos):
                for c in range(2):
                    to = move(r, p, c)
                    pairs.append((r * n_shard + p * 2 + c, to[0] * n_shard + to[1] * 2 + to[2]))
        return pairs

    ring = list(range(0, n_pos, 2)) + list(range(n_pos - 1, 0, -2))
    after = {p: ring[(i + 1) % n_pos] for i, p in enumerate(ring)}
    before = {p: ring[i - 1] for i, p in enumerate(ring)}

    def mover(move):
        pairs = every(move)
        return lambda v: lax.ppermute(v, MESH_AXES, pairs)

    to_core = mover(lambda r, p, c: (r, p, 1 - c))
    to_copy = mover(lambda r, p, c: (r ^ 1, p, c))
    to_next = mover(lambda r, p, c: (r, after[p], c))
    to_back = mover(lambda r, p, c: (r, before[p], c))
    to_side = mover(lambda r, p, c: (r, p ^ 1, c))
    to_corner = mover(lambda r, p, c: (r ^ 1, p ^ 1, c))

    def local(
        tokens,
        segments,
        counts,
        ln1_gain,
        ln1_bias,
        w_qkv,
        bias_query,
        bias_value,
        w_proj,
        bias_proj,
        ln2_gain,
        ln2_bias,
        w_fc,
        bias_fc,
        w_out,
        bias_out,
        cotangent,
    ):
        rows, width = tokens.shape
        own_rows = width // n_shard
        chip_rows = 2 * own_rows
        piece = w_out.shape[0] // 2
        units = n_pos * piece
        all_rows = RANKS * rows
        qkv_cols = 3 * width // 4
        first_shape = ((chip_rows + SMALL_ROWS, width), BF16)
        second_shape = ((chip_rows + piece, width), BF16)
        replica_at = lax.axis_index("replica")
        shard_at = lax.axis_index("shard")
        x, c, p = replica_at % 2, shard_at % 2, shard_at // 2
        place = jnp.where(p % 2 == 0, p // 2, n_pos - 1 - p // 2)

        def origin(index):
            index = index % n_pos
            return jnp.where(index < half, 2 * index, 2 * (n_pos - 1 - index) + 1)

        offsets = [0]
        for step in range(1, half):
            offsets += [-step, step]
        offsets += [half, half]
        info = jnp.stack(
            [origin(place + offset) for offset in offsets] + [x, c, p % 2, counts[0]]
        ).astype(jnp.int32)

        got_qkv, lent = to_core(w_qkv), to_side(w_proj)
        vectors = jnp.stack(
            [ln1_gain, ln1_bias, bias_proj, ln2_gain, ln2_bias, bias_out, bias_query, bias_value]
            + [bias_fc[i * own_rows : (i + 1) * own_rows] for i in range(4)]
            + [jnp.zeros((own_rows,), BF16)] * 4
        )
        got_vectors = to_core(vectors)
        groups, left = kernel_call(
            own_part_body,
            [SMEM_SPEC] + [VMEM_SPEC] * 2,
            [((own_rows, 3 * width // 2), BF16), ((own_rows, width // 2), BF16)],
        )(info, w_qkv, w_proj)
        block, d_top = kernel_call(
            tokens_body,
            [SMEM_SPEC] + [VMEM_SPEC] * 3,
            [((rows + SMALL_ROWS, width), BF16), ((rows, width), BF16)],
        )(info, tokens, segments.reshape(1, rows), cotangent)
        (first_chunk,) = kernel_call(
            first_chunk_body, [SMEM_SPEC] + [VMEM_SPEC] * 6, [first_shape], micros=2
        )(info, groups, got_qkv, left, lent, vectors, got_vectors)

        first_chunk, later_fc = tie(first_chunk, w_fc)
        forth, back = to_next(first_chunk), to_back(first_chunk)
        got_fc = to_core(later_fc)
        firsts = [first_chunk, forth, back]
        forth, back, block = tie(forth, back, block)
        block_other = to_copy(block)
        blocks = [block, to_core(block), block_other, to_core(block_other)]
        forth, back = to_next(forth), to_back(back)
        (second_chunk,) = kernel_call(
            second_chunk_body,
            [SMEM_SPEC] + [HBM_SPEC] * 3,
            [second_shape],
            [pltpu.SemaphoreType.DMA((1 + 2 * n_pos,))],
            micros=2,
        )(info, w_fc, got_fc, w_out)
        forth, back, second_chunk = tie(forth, back, second_chunk)
        seconds = [second_chunk]
        firsts += [forth, back]
        forth, back = to_next(forth), to_back(back)
        second_forth, second_back = to_next(second_chunk), to_back(second_chunk)
        firsts += [forth, back]
        unit, masks = kernel_call(
            blocks_body,
            [VMEM_SPEC] * RANKS,
            [((all_rows, width), F32), ((RANKS, rows, rows), F32)],
            micros=2,
        )(*blocks)
        unit, masks, forth, back = tie(unit, masks, forth, back)
        d_top, *firsts = tie(d_top, *firsts, to_next(forth[:own_rows]), to_back(back[own_rows:]))
        seconds += [second_forth, second_back]
        second_forth, second_back = to_next(second_forth), to_back(second_back)

        parts = [((rows, width), BF16)] * 2 + [((rows, width), F32)] * 2
        two_blocks = ((2, rows, width), BF16)
        d_other = to_copy(d_top)
        (
            normed, qkv, probs, context, send_own, send_away, keep_own, keep_away, qkv_weight, proj_weight, smalls
        ) = kernel_call(
            attention_body,
            [SMEM_SPEC] + [VMEM_SPEC] * 2 + [ANY_SPEC] * ORIGINS,
            [
                ((all_rows, width), BF16),
                ((all_rows, qkv_cols), BF16),
                ((4 * RANKS, rows, rows), BF16),
                ((all_rows, width // 4), BF16),
                *parts,
                ((width, qkv_cols), BF16),
                ((width // 4, width), BF16),
                ((SMALL_ROWS, width), BF16),
            ],
            [pltpu.SemaphoreType.DMA((5 * n_pos,))],
            micros=8,
        )(info, unit, masks, *firsts)
        send_own, send_away, d_top, d_other = tie(send_own, send_away, d_top, d_other)
        near_own, near_away = to_core(send_own), to_core(send_away)
        near_own, near_away, second_forth, second_back = tie(
            near_own, near_away, second_forth, second_back
        )

        def message(*parts):
            return kernel_call(message_body, [VMEM_SPEC] * 4, [two_blocks], micros=0)(*parts)[0]

        got = to_copy(message(keep_own, keep_away, near_own, near_away))
        seconds += [second_forth, second_back]
        second_forth, second_back = to_next(second_forth), to_back(second_back)
        d_outs = [d_top, to_core(d_top), d_other, to_core(d_other)]
        seconds += [second_forth, second_back]
        second_forth, second_back = second_forth[:chip_rows], second_back[chip_rows:]
        got, second_forth, second_back = tie(got, second_forth, second_back)
        seconds += [to_next(second_forth), to_back(second_back)]
        middle, normed_two = kernel_call(
            second_norm_body, [VMEM_SPEC] * 8, [((2, rows, width), F32), two_blocks], micros=2
        )(block, block_other, keep_own, keep_away, near_own, near_away, got, smalls)
        beside = to_core(normed_two)

        (
            given, d_out, hidden, d_pre, send_own, send_away, keep_own, keep_away, sums_fc, out_weight
        ) = kernel_call(
            feed_body,
            [SMEM_SPEC] + [VMEM_SPEC] * (2 + RANKS) + [ANY_SPEC] * ORIGINS + [VMEM_SPEC],
            [
                ((all_rows, width), BF16),
                ((all_rows, width), BF16),
                ((all_rows, units), BF16),
                ((all_rows, units), BF16),
                *parts,
                ((8, units), F32),
                ((units, width), BF16),
            ],
            [pltpu.VMEM((width, units), BF16), pltpu.SemaphoreType.DMA((2 * n_pos,))],
            micros=8,
        )(
            info, normed_two, beside, *d_outs, *seconds, smalls
        )

        near_own, near_away = to_core(send_own), to_core(send_away)
        mix_own, mix_away, mix_keep, mix_keep_away = kernel_call(
            feed_out_body, [VMEM_SPEC] * 2, parts, micros=2
        )(hidden, out_weight)
        near_own, near_away, given, d_out, hidden, d_pre, mix_own, mix_away = tie(
            near_own, near_away, given, d_out, hidden, d_pre, mix_own, mix_away
        )
        got = to_copy(message(keep_own, keep_away, near_own, near_away))
        grad_w_out = dot_rows(hidden, d_out).astype(BF16)
        grad_w_fc = dot_rows(given, d_pre).astype(BF16)
        far_forth, far_back = kernel_call(
            second_far_body,
            [SMEM_SPEC] + [VMEM_SPEC] * 2,
            [((chip_rows, width), BF16), ((piece, width), BF16)],
        )(info, grad_w_fc, grad_w_out)
        far_forth, far_back, mix_own, mix_away = tie(far_forth, far_back, mix_own, mix_away)
        far_forth, far_back = to_next(far_forth), to_back(far_back)
        mix_own, mix_away = to_core(mix_own), to_core(mix_away)

        def second_sums(step, got_forth, got_back):
            return kernel_call(
                functools.partial(second_hop_body, step),
                [SMEM_SPEC] + [VMEM_SPEC] * 4,
                [second_shape, second_shape],
            )(info, got_forth, got_back, grad_w_fc, grad_w_out)

        second_forth, second_back = second_sums(half - 1, far_forth, far_back)
        got, second_forth, second_back, mix_own, mix_away = tie(
            got, second_forth, second_back, mix_own, mix_away
        )
        second_forth, second_back = to_next(second_forth), to_back(second_back)
        d_middle, branch_own, branch_away, sums_two = kernel_call(
            second_back_body,
            [VMEM_SPEC] * 9,
            [((rows, width), F32), ((rows, width), BF16), ((rows, width), BF16), ((8, width), F32)],
            micros=1,
        )(middle, d_top, d_other, keep_own, keep_away, near_own, near_away, got, smalls)
        branches = [branch_own, to_core(branch_own), branch_away, to_core(branch_away)]
        mix_away = to_copy(add(mix_keep_away, mix_away))

        d_branch, d_qkv, send_own, send_away, keep_own, keep_away, sums = kernel_call(
            attention_back_body,
            [SMEM_SPEC] + [VMEM_SPEC] * 11,
            [
                ((all_rows, width), BF16),
                ((all_rows, qkv_cols), BF16),
                *parts,
                ((SMALL_ROWS, width), F32),
            ],
            [pltpu.VMEM((all_rows, width // 4), BF16)],
            micros=1,
        )(info, *branches, unit, qkv, probs, qkv_weight, proj_weight, sums_two, sums_fc)
        grad_w_proj = dot_rows(context, d_branch).astype(BF16)
        grad_w_qkv = dot_rows(normed, d_qkv).astype(BF16)
        firsts = (grad_w_qkv, grad_w_proj, sums)
        forth, back = kernel_call(
            first_far_body,
            [SMEM_SPEC] + [VMEM_SPEC] * 3,
            [((own_rows, width), BF16), ((own_rows + SMALL_ROWS, width), BF16)],
        )(info, *firsts)
        forth, back, second_forth, second_back, mix_away = tie(
            forth, back, second_forth, second_back, mix_away
        )
        forth, back = to_next(forth), to_back(back)
        second_forth, second_back = second_sums(half - 2, second_forth, second_back)

        def first_sums(step, forth, back):
            return kernel_call(
                functools.partial(first_hop_body, step),
                [SMEM_SPEC] + [VMEM_SPEC] * 5,
                [first_shape, first_shape],
            )(info, forth, back, *firsts)

        second_forth, second_back = to_next(second_forth), to_back(second_back)
        forth, back, send_own, send_away = tie(forth, back, send_own, send_away)
        near_away, near_own = to_core(send_away), to_core(send_own)
        near_away, near_own = tie(near_away, near_own)
        (away,) = kernel_call(
            add_body, [VMEM_SPEC] * 2, [((rows, width), BF16)], micros=1
        )(keep_away, near_away)
        forth, back = first_sums(3, forth, back)
        forth, back = to_next(forth), to_back(back)
        away = to_copy(away)
        second_forth, second_back, away = tie(second_forth, second_back, away)
        second_forth, second_back = second_sums(1, second_forth, second_back)
        second_forth, second_back = to_next(second_forth), to_back(second_back)
        (grad_tokens,) = kernel_call(first_back_body, [VMEM_SPEC] * 6, [((rows, width), F32)])(
            tokens, d_middle, keep_own, near_own, away, smalls
        )
        forth, back, grad_tokens = tie(forth, back, grad_tokens)
        forth, back = first_sums(2, forth, back)
        forth, back = to_next(forth), to_back(back)
        (mixed,) = kernel_call(mixed_body, [SMEM_SPEC] + [VMEM_SPEC] * 5, [((rows, width), BF16)])(
            info, middle, mix_keep, mix_own, mix_away, smalls
        )
        forth, back, second_forth, second_back, mixed = tie(
            forth, back, second_forth, second_back, mixed
        )
        (own_second,) = kernel_call(
            second_last_body, [SMEM_SPEC] + [VMEM_SPEC] * 4, [second_shape]
        )(info, second_forth, second_back, grad_w_fc, grad_w_out)
        near_second, other_second = to_core(own_second), to_copy(own_second)
        forth, back = first_sums(1, forth, back)
        forth, back = to_next(forth), to_back(back)
        forth, back, near_second, other_second = tie(forth, back, near_second, other_second)
        (own_first,) = kernel_call(
            first_last_body, [SMEM_SPEC] + [VMEM_SPEC] * 5, [first_shape]
        )(info, forth, back, *firsts)
        near_first, other_first = to_core(own_first), to_copy(own_first)
        own_proj = own_first[:chip_rows, qkv_cols:]
        given_side, given_far = to_side(own_proj), to_corner(own_proj)

        grad_w_fc, grad_w_out = kernel_call(
            hidden_grads_body,
            [SMEM_SPEC] + [VMEM_SPEC] * 4,
            [((own_rows, 4 * units), F32), ((2 * piece, width), F32)],
        )(info, own_second, near_second, other_second, to_core(other_second))

        other_first, given_side, given_far, grad_w_fc, grad_w_out = tie(
            other_first, given_side, given_far, grad_w_fc, grad_w_out
        )
        vector_shape = ((1, own_rows), F32)
        grad_w_qkv, grad_w_proj, *small = kernel_call(
            first_grads_body,
            [SMEM_SPEC] + [VMEM_SPEC] * 6,
            [((own_rows, 3 * width), F32), ((own_rows, width), F32)]
            + [vector_shape] * 6
            + [((2, piece), F32)]
            + [vector_shape] * 2,
        )(info, own_first, near_first, other_first, to_core(other_first), given_side, given_far)
        small = [value.reshape(-1) for value in small]
        return (
            mixed,
            grad_tokens,
            small[0],
            small[1],
            grad_w_qkv,
            small[7],
            small[8],
            grad_w_proj,
            small[2],
            small[3],
            small[4],
            grad_w_fc,
            small[6],
            grad_w_out,
            small[5],
        )

    return local


def solution(mesh):
    tokens_spec = P(MESH_AXES, None)
    slots_spec = P(MESH_AXES)
    rows_spec = P("shard", None)
    vector_spec = P("shard")
    in_specs = (
        tokens_spec,
        slots_spec,
        slots_spec,
        vector_spec,
        vector_spec,
        rows_spec,
        vector_spec,
        vector_spec,
        rows_spec,
        vector_spec,
        vector_spec,
        vector_spec,
        rows_spec,
        vector_spec,
        rows_spec,
        vector_spec,
        tokens_spec,
    )
    out_specs = (
        tokens_spec,
        tokens_spec,
        vector_spec,
        vector_spec,
        rows_spec,
        vector_spec,
        vector_spec,
        rows_spec,
        vector_spec,
        vector_spec,
        vector_spec,
        rows_spec,
        vector_spec,
        rows_spec,
        vector_spec,
    )
    n_replica, n_shard = mesh.shape["replica"], mesh.shape["shard"]
    make = make_kernel_local if (n_replica, n_shard) == (2, HEADS) else make_local
    local = make(n_replica, n_shard)
    return jax.shard_map(local, mesh=mesh, in_specs=in_specs, out_specs=out_specs, check_vma=False)
```

```python
import functools

import jax
import jax.numpy as jnp
from jax import lax
from jax.experimental import pallas as pl
from jax.experimental.pallas import tpu as pltpu
from jax.sharding import PartitionSpec as P

HEADS = 16
RANKS = 4
MESH_AXES = ("replica", "shard")
BF16 = jnp.bfloat16
F32 = jnp.float32
SMALL_ROWS = 16


def layer_norm(values, gain, shift):
    center = values - jnp.mean(values, axis=-1, keepdims=True)
    spread = jnp.mean(center * center, axis=-1, keepdims=True)
    return center * lax.rsqrt(spread + 1e-05) * gain + shift


def unit_norm(values):
    center = values - jnp.mean(values, axis=-1, keepdims=True)
    spread = jnp.mean(center * center, axis=-1, keepdims=True)
    return center * lax.rsqrt(spread + 1e-05)


def smooth_gate(values):
    return jax.nn.gelu(values, approximate=True)


def dot_rows(left, right):
    return lax.dot_general(left, right, (((0,), (0,)), ((), ())), preferred_element_type=F32)


def dot_cols(left, right):
    return lax.dot_general(left, right, (((1,), (1,)), ((), ())), preferred_element_type=F32)


def dot(left, right):
    return jnp.dot(left, right, preferred_element_type=F32)


def make_local(n_replica, n_shard):
    n_pos = n_shard // 2
    half = n_pos // 2
    head_a_shard = n_shard == HEADS
    n_pairs = n_replica // 2
    pair_groups = [[2 * i + j for i in range(n_pairs)] for j in range(2)]

    def every(move):
        pairs = []
        for r in range(n_replica):
            for p in range(n_pos):
                for c in range(2):
                    to = move(r, p, c)
                    if to is not None:
                        pairs.append((r * n_shard + p * 2 + c, to[0] * n_shard + to[1] * 2 + to[2]))
        return pairs

    ring = list(range(0, n_pos, 2)) + list(range(n_pos - 1, 0, -2))
    after = {p: ring[(i + 1) % n_pos] for i, p in enumerate(ring)}
    before = {p: ring[i - 1] for i, p in enumerate(ring)}
    core_pairs = every(lambda r, p, c: (r, p, 1 - c))
    copy_pairs = every(lambda r, p, c: (r ^ 1, p, c))
    next_pairs = every(lambda r, p, c: (r, after[p], c))
    back_pairs = every(lambda r, p, c: (r, before[p], c))
    lend_pairs = every(lambda r, p, c: (r, p ^ 1, c) if p % 2 == r % 2 else None)
    give_pairs = every(lambda r, p, c: (r, p ^ 1, c) if p % 2 != r % 2 else None)
    share_pairs = every(lambda r, p, c: (r ^ 1, p, c) if p % 2 == r % 2 else None)

    def to_core(v):
        return lax.ppermute(v, MESH_AXES, core_pairs)

    def to_copy(v):
        return lax.ppermute(v, MESH_AXES, copy_pairs)

    def to_next(v):
        return lax.ppermute(v, MESH_AXES, next_pairs)

    def to_back(v):
        return lax.ppermute(v, MESH_AXES, back_pairs)

    def cut(rows):
        return max(16, rows // 32 * 16)

    def ring_gather(chunk, place, origin):
        low = cut(chunk.shape[0])
        full = jnp.zeros((n_pos,) + chunk.shape, chunk.dtype)

        def put(full, value, offset, row=0):
            return lax.dynamic_update_slice(full, value[None], (origin(place + offset), row, 0))

        full = put(full, chunk, 0)
        forth = back = chunk
        for step in range(1, half):
            forth = to_next(forth)
            back = to_back(back)
            full = put(full, forth, -step)
            full = put(full, back, step)
        forth = to_next(forth[:low])
        back = to_back(back[low:])
        full = put(full, forth, half)
        full = put(full, back, half, low)
        return full

    def ring_scatter(full, place, origin):
        low = cut(full.shape[1])

        def term(offset):
            return lax.dynamic_index_in_dim(full, origin(place + offset), 0, keepdims=False)

        def add(left, right):
            return (left.astype(F32) + right.astype(F32)).astype(BF16)

        far = term(half)
        forth = to_next(far[:low])
        back = to_back(far[low:])
        ahead = term(half - 1)
        behind = term(1 - half)
        forth = to_next(jnp.concatenate([add(forth, ahead[:low]), ahead[low:]]))
        back = to_back(jnp.concatenate([behind[:low], add(back, behind[low:])]))
        for step in range(half - 2, 0, -1):
            forth = to_next(add(forth, term(step)))
            back = to_back(add(back, term(-step)))
        return term(0).astype(F32) + forth.astype(F32) + back.astype(F32)

    def group_gather(block):
        other = to_copy(block)
        return jnp.stack([block, to_core(block), other, to_core(other)])

    def group_scatter(parts):
        near = to_core(jnp.stack([parts[1], parts[3]]).astype(BF16)).astype(F32)
        away = to_copy((parts[2] + near[1]).astype(BF16)).astype(F32)
        return parts[0] + near[0] + away

    def local(
        tokens,
        segments,
        counts,
        ln1_gain,
        ln1_bias,
        w_qkv,
        bias_query,
        bias_value,
        w_proj,
        bias_proj,
        ln2_gain,
        ln2_bias,
        w_fc,
        bias_fc,
        w_out,
        bias_out,
        cotangent,
    ):
        row_count, width = tokens.shape
        head_width = width // HEADS
        own_rows = width // n_shard
        chip_rows = 2 * own_rows
        own_hidden = w_out.shape[0]
        piece = own_hidden // 2
        groups = HEADS // RANKS
        scale = head_width ** (-0.5)
        replica_at = lax.axis_index("replica")
        shard_at = lax.axis_index("shard")
        x = replica_at % 2
        c = shard_at % 2
        p = shard_at // 2
        rank = 2 * x + c
        place = jnp.where(p % 2 == 0, p // 2, n_pos - 1 - p // 2)

        def origin(index):
            index = index % n_pos
            return jnp.where(index < half, 2 * index, 2 * (n_pos - 1 - index) + 1)

        def by_core(mine, other):
            return jnp.where(c == 0, jnp.stack([mine, other]), jnp.stack([other, mine]))

        position = jnp.arange(row_count, dtype=jnp.int32)
        in_use = (position < counts[0]).astype(F32)
        notes = jnp.stack([segments.astype(BF16), in_use.astype(BF16)])
        notes = jnp.pad(notes, ((0, SMALL_ROWS - 2), (0, width - row_count)))
        seen = group_gather(jnp.concatenate([tokens, notes]))
        tokens_all = seen[:, :row_count].reshape(RANKS * row_count, width)
        seg_all = seen[:, row_count, :row_count]
        use_all = seen[:, row_count + 1, :row_count]

        def qkv_part(which):
            view = w_qkv.reshape(own_rows, 3, groups, RANKS, head_width)
            return lax.dynamic_index_in_dim(view, which, 3, keepdims=False).reshape(own_rows, -1)

        def fc_part(core):
            view = w_fc.reshape(own_rows, n_pos, 4, piece)
            part = lax.dynamic_index_in_dim(view, 2 * core + x, 2, keepdims=False)
            return part.reshape(own_rows, -1)

        vectors = [ln1_gain, ln1_bias, bias_query, bias_value, bias_proj, ln2_gain, ln2_bias, bias_out, bias_fc]
        starts = [0]
        for vector in vectors:
            starts.append(starts[-1] + vector.shape[0])
        n_small = starts[-1]
        qkv_width = 3 * groups * head_width
        small = jnp.concatenate(vectors)[None]
        small = jnp.pad(small, ((0, SMALL_ROWS - 1), (0, 0)))
        both_small = by_core(small[0], to_core(small)[0])
        qkv_chunk = by_core(qkv_part(rank), to_core(qkv_part(rank ^ 1))).reshape(chip_rows, qkv_width)
        if head_a_shard:
            lent = lax.ppermute(w_proj[:, width // 2 :], MESH_AXES, lend_pairs)
            proj_half = jnp.where(p % 2 == x, w_proj[:, : width // 2], lent)
            proj_chunk = jnp.concatenate([proj_half[:, : width // 4], proj_half[:, width // 4 :]])
        else:
            proj_chunk = jnp.zeros((chip_rows, width // 4), BF16)
        small_chunk = jnp.pad(both_small, ((0, SMALL_ROWS - 2), (0, width - n_small)))
        first_chunk = jnp.concatenate(
            [jnp.concatenate([qkv_chunk, proj_chunk], axis=1), small_chunk]
        )
        fc_chunk = by_core(fc_part(c), to_core(fc_part(1 - c))).reshape(chip_rows, n_pos * piece)
        out_chunk = lax.dynamic_slice_in_dim(w_out, x * piece, piece, 0)

        first_full = ring_gather(first_chunk, place, origin)
        fc_weight = ring_gather(fc_chunk, place, origin).reshape(width, n_pos * piece)
        out_weight = ring_gather(out_chunk, place, origin).reshape(n_pos * piece, width)

        qkv_weight = first_full[:, :chip_rows, :qkv_width].reshape(width, qkv_width)
        if head_a_shard:
            proj_full = first_full[:, :chip_rows, qkv_width:].reshape(
                n_pos // 2, 2, 2, own_rows, width // 4
            )
            proj_full = jnp.where(x == 0, proj_full, proj_full[:, ::-1])
            proj_weight = proj_full.transpose(0, 3, 1, 2, 4).reshape(groups * head_width, width)
        else:
            proj_full = lax.all_gather(w_proj, "shard", axis=0, tiled=True)
            proj_full = proj_full.reshape(groups, RANKS, head_width, width)
            proj_weight = lax.dynamic_index_in_dim(proj_full, rank, 1, keepdims=False)
            proj_weight = proj_weight.reshape(groups * head_width, width)
        smalls = first_full[:, chip_rows : chip_rows + 2, :n_small].reshape(n_shard, n_small)
        params = [
            smalls[:, starts[i] : starts[i + 1]].reshape(-1).astype(F32) for i in range(len(vectors))
        ]
        gain_one, shift_one, query_shift, value_shift, proj_shift, gain_two, shift_two, out_shift, fc_shift = params

        def rank_heads(vector):
            view = vector.reshape(groups, RANKS, head_width)
            return lax.dynamic_index_in_dim(view, rank, 1, keepdims=False).reshape(-1)

        fc_shift = lax.dynamic_index_in_dim(
            fc_shift.reshape(n_pos, 4, piece), 2 * c + x, 1, keepdims=False
        ).reshape(-1)
        qkv_shift = jnp.concatenate(
            [
                rank_heads(query_shift),
                jnp.zeros((groups * head_width,), F32),
                rank_heads(value_shift),
            ]
        )

        unit_one = unit_norm(tokens_all.astype(F32))
        input_one = (unit_one * gain_one + shift_one).astype(BF16)
        qkv_rows = (dot(input_one, qkv_weight) + qkv_shift).astype(BF16)
        qkv_view = qkv_rows.reshape(RANKS, row_count, 3, groups, head_width)
        queries, keys_rows, values_rows = qkv_view[:, :, 0], qkv_view[:, :, 1], qkv_view[:, :, 2]
        visible = (
            (seg_all[:, :, None] == seg_all[:, None, :])
            & (position[None, None, :] <= position[None, :, None])
            & (use_all[:, None, :] > 0)
        )[:, None]
        scores = scale * jnp.einsum("bqhd,bkhd->bhqk", queries, keys_rows, preferred_element_type=F32)
        scores = jnp.where(visible, scores, -1e30)
        top_score = jnp.max(scores, axis=-1, keepdims=True)
        expo = jnp.exp(scores - top_score)
        probs = expo / jnp.sum(expo, axis=-1, keepdims=True)
        probs_low = probs.astype(BF16)
        context = (
            jnp.einsum("bhqk,bkhd->bqhd", probs_low, values_rows, preferred_element_type=F32)
            .reshape(RANKS * row_count, groups * head_width)
            .astype(BF16)
        )
        block_shape = (RANKS, row_count, width)
        stream = tokens.astype(F32)
        middle = stream + proj_shift + group_scatter(dot(context, proj_weight).reshape(block_shape))

        normed_two, norm_two_back = jax.vjp(layer_norm, middle, gain_two, shift_two)
        input_two = group_gather(normed_two.astype(BF16)).reshape(RANKS * row_count, width)
        pre_act = dot(input_two, fc_weight) + fc_shift
        gate_value, gate_back = jax.vjp(smooth_gate, pre_act)
        hidden = gate_value.astype(BF16)
        branch_two = group_scatter(dot(hidden, out_weight).reshape(block_shape)) + out_shift
        mixed = (in_use[:, None] * (middle + branch_two)).astype(BF16)

        d_top = in_use[:, None] * cotangent.astype(F32)
        d_out = group_gather(d_top.astype(BF16)).reshape(RANKS * row_count, width)
        grad_w_out = dot_rows(hidden, d_out).astype(BF16).reshape(n_pos, piece, width)
        d_pre = gate_back(dot_cols(d_out, out_weight))[0].astype(BF16)
        grad_w_fc = dot_rows(input_two, d_pre).astype(BF16).reshape(n_pos, chip_rows, n_pos * piece)
        d_input_two = group_scatter(dot_cols(d_pre, fc_weight).reshape(block_shape))
        d_mid_norm, grad_gain_two, grad_shift_two = norm_two_back(d_input_two)
        d_middle = d_top + d_mid_norm
        own_w_out = ring_scatter(grad_w_out, place, origin)
        own_w_fc = ring_scatter(grad_w_fc, place, origin)

        d_branch = group_gather(d_middle.astype(BF16)).reshape(RANKS * row_count, width)
        grad_w_proj = dot_rows(context, d_branch)
        d_context = (
            dot_cols(d_branch, proj_weight)
            .astype(BF16)
            .reshape(RANKS, row_count, groups, head_width)
        )
        d_values = jnp.einsum("bhqk,bqhd->bkhd", probs_low, d_context, preferred_element_type=F32)
        d_probs = jnp.einsum("bqhd,bkhd->bhqk", d_context, values_rows, preferred_element_type=F32)
        d_scores = (
            probs * (d_probs - jnp.sum(probs * d_probs, axis=-1, keepdims=True))
        ).astype(BF16)
        d_queries = scale * jnp.einsum(
            "bhqk,bkhd->bqhd", d_scores, keys_rows, preferred_element_type=F32
        )
        d_keys = scale * jnp.einsum("bhqk,bqhd->bkhd", d_scores, queries, preferred_element_type=F32)
        d_qkv = (
            jnp.stack([d_queries, d_keys, d_values], axis=2)
            .reshape(RANKS * row_count, qkv_width)
            .astype(BF16)
        )
        grad_w_qkv = dot_rows(input_one, d_qkv).astype(BF16).reshape(n_pos, chip_rows, qkv_width)
        d_input_one = dot_cols(d_qkv, qkv_weight)
        grad_gain_one = jnp.sum(d_input_one * unit_one, axis=0)
        grad_shift_one = jnp.sum(d_input_one, axis=0)
        d_qkv_sums = jnp.sum(d_qkv.astype(F32), axis=0)

        def own_term(values):
            return jnp.sum(values.astype(BF16).astype(F32), axis=0)

        def at_rank(sums):
            view = sums.reshape(groups, 1, head_width)
            mine = jnp.arange(RANKS)[None, :, None] == rank
            return jnp.where(mine, view, 0.0).reshape(-1)

        fc_sums = jnp.sum(d_pre.astype(F32), axis=0).reshape(n_pos, 1, piece)
        fc_sums = jnp.where(jnp.arange(4)[None, :, None] == 2 * c + x, fc_sums, 0.0).reshape(-1)
        small_terms = [
            grad_gain_one,
            grad_shift_one,
            at_rank(d_qkv_sums[: groups * head_width]),
            at_rank(d_qkv_sums[2 * groups * head_width :]),
            own_term(d_middle),
            grad_gain_two,
            grad_shift_two,
            own_term(d_top),
            fc_sums,
        ]
        small_terms = jnp.concatenate(
            [term.reshape(n_shard, -1) for term in small_terms], axis=1
        ).astype(BF16)
        small_terms = jnp.pad(
            small_terms.reshape(n_pos, 2, n_small),
            ((0, 0), (0, SMALL_ROWS - 2), (0, width - n_small)),
        )
        if head_a_shard:
            proj_terms = grad_w_proj.astype(BF16).reshape(n_pos // 2, own_rows, 2, 2, width // 4)
            proj_terms = proj_terms.transpose(0, 2, 3, 1, 4)
            proj_terms = jnp.where(x == 0, proj_terms, proj_terms[:, ::-1])
            proj_terms = proj_terms.reshape(n_pos, chip_rows, width // 4)
        else:
            proj_terms = jnp.zeros((n_pos, chip_rows, width // 4), BF16)
        first_terms = jnp.concatenate(
            [jnp.concatenate([grad_w_qkv, proj_terms], axis=2), small_terms], axis=1
        )
        own_first = ring_scatter(first_terms, place, origin)
        d_in_norm = jax.vjp(unit_norm, stream)[1](
            group_scatter(d_input_one.reshape(block_shape)) * gain_one
        )[0]
        grad_tokens = d_middle + d_in_norm

        def rows_of(chunk, core):
            return lax.dynamic_slice_in_dim(chunk, core * own_rows, own_rows, 0)

        def by_copy(mine, other):
            return jnp.where(x == 0, jnp.stack([mine, other]), jnp.stack([other, mine]))

        own_w_out = own_w_out.astype(BF16)
        grad_w_out = by_copy(own_w_out, to_copy(own_w_out)).reshape(own_hidden, width)

        own_w_fc = own_w_fc.astype(BF16)
        fc_rows = by_core(rows_of(own_w_fc, c), to_core(rows_of(own_w_fc, 1 - c)))
        fc_rows = by_copy(fc_rows, to_copy(fc_rows))
        fc_rows = fc_rows.reshape(2, 2, own_rows, n_pos, piece)
        grad_w_fc = fc_rows.transpose(2, 3, 1, 0, 4).reshape(own_rows, -1)

        own_first = own_first.astype(BF16)
        own_qkv = own_first[:chip_rows, :qkv_width]
        qkv_grad = by_core(rows_of(own_qkv, c), to_core(rows_of(own_qkv, 1 - c)))
        qkv_grad = by_copy(qkv_grad, to_copy(qkv_grad))
        qkv_grad = qkv_grad.reshape(2, 2, own_rows, 3, groups, head_width)
        grad_w_qkv = qkv_grad.transpose(2, 3, 4, 0, 1, 5).reshape(own_rows, -1)

        own_small = own_first[chip_rows:, :n_small]
        near_small = to_core(own_small)
        small_sum = jnp.where(
            c == 0,
            own_small[0].astype(F32) + near_small[0].astype(F32),
            own_small[1].astype(F32) + near_small[1].astype(F32),
        )
        small_send = jnp.pad(small_sum[None].astype(BF16), ((0, SMALL_ROWS - 1), (0, 0)))
        small_sum = small_sum + to_copy(small_send)[0].astype(F32)

        if head_a_shard:
            own_proj = own_first[:chip_rows, qkv_width:]
            given = lax.ppermute(own_proj, MESH_AXES, give_pairs)
            proj_rows = jnp.stack([own_proj, given]).reshape(2, 2, own_rows, width // 4)
            proj_rows = proj_rows.transpose(2, 0, 1, 3).reshape(own_rows, width)
            shared = lax.ppermute(proj_rows, MESH_AXES, share_pairs)
            grad_w_proj = jnp.where(p % 2 == x, proj_rows, shared)
        else:
            proj_rows = grad_w_proj.astype(BF16).reshape(groups, 1, head_width, width)
            mine = jnp.arange(RANKS)[None, :, None, None] == rank
            proj_rows = jnp.where(mine, proj_rows, 0).reshape(width, width)
            proj_rows = lax.psum_scatter(proj_rows, "shard", scatter_dimension=0, tiled=True)
            grad_w_proj = proj_rows.astype(F32) + to_copy(proj_rows).astype(F32)

        if n_pairs > 1:
            grad_w_out, grad_w_fc, grad_w_qkv, grad_w_proj, small_sum = lax.psum(
                tuple(
                    value.astype(BF16)
                    for value in (grad_w_out, grad_w_fc, grad_w_qkv, grad_w_proj, small_sum)
                ),
                "replica",
                axis_index_groups=pair_groups,
            )
        small_sum = small_sum.astype(F32)
        small_grads = [small_sum[starts[i] : starts[i + 1]] for i in range(len(vectors))]
        g_gain_one, g_shift_one, g_query, g_value, g_proj, g_gain_two, g_shift_two, g_out, g_fc = small_grads
        return (
            mixed,
            grad_tokens,
            g_gain_one,
            g_shift_one,
            grad_w_qkv.astype(F32),
            g_query,
            g_value,
            grad_w_proj.astype(F32),
            g_proj,
            g_gain_two,
            g_shift_two,
            grad_w_fc.astype(F32),
            g_fc,
            grad_w_out.astype(F32),
            g_out,
        )

    return local

LANES = 128
HALF = 64
VMEM_BYTES = 26 * 1024 * 1024
ORIGINS = 9
AT_X, AT_C, AT_Y, AT_COUNT = 9, 10, 11, 12
VMEM_SPEC = pl.BlockSpec(memory_space=pltpu.VMEM)
SMEM_SPEC = pl.BlockSpec(memory_space=pltpu.SMEM)
ANY_SPEC = pl.BlockSpec(memory_space=pl.ANY)
HBM_SPEC = pl.BlockSpec(memory_space=pltpu.HBM)


def kernel_call(body, in_specs, outs, scratch=(), micros=1):
    return pl.pallas_call(
        body,
        out_shape=tuple(jax.ShapeDtypeStruct(shape, dtype) for shape, dtype in outs),
        in_specs=list(in_specs),
        out_specs=tuple(VMEM_SPEC for _ in outs),
        scratch_shapes=list(scratch),
        compiler_params=pltpu.CompilerParams(vmem_limit_bytes=VMEM_BYTES),
        cost_estimate=pl.CostEstimate(
            flops=0, bytes_accessed=micros * 3_000_000, transcendentals=0
        ),
    )


def low_half(shape):
    return lax.broadcasted_iota(jnp.int32, shape, len(shape) - 1) < HALF


def turn(values):
    return jnp.concatenate([values[:, HALF:], values[:, :HALF]], axis=1)


def join(c, first, second, low):
    even = jnp.where(low, first, turn(second))
    odd = jnp.where(low, turn(first), second)
    return jnp.where(c == 0, even, odd)


def statistics(values):
    center = values - jnp.mean(values, axis=-1, keepdims=True)
    spread = jnp.mean(center * center, axis=-1, keepdims=True)
    return center, lax.rsqrt(spread + 1e-05)


def norm_back(unit, inverse, d_unit):
    along = jnp.mean(d_unit * unit, axis=-1, keepdims=True)
    return inverse * (d_unit - jnp.mean(d_unit, axis=-1, keepdims=True) - unit * along)


def used_rows(info, rows):
    return (lax.broadcasted_iota(jnp.int32, (rows, 1), 0) < info[AT_COUNT]).astype(F32)


def tokens_body(info, tokens, segments, cotangent, block, d_out):
    rows = tokens.shape[0]
    block[:rows, :] = tokens[...]
    down = lax.broadcasted_iota(jnp.int32, (SMALL_ROWS, rows), 0)
    across = lax.broadcasted_iota(jnp.int32, (SMALL_ROWS, rows), 1)
    used = jnp.where(across < info[AT_COUNT], 1.0, 0.0)
    notes = jnp.where(down == 0, segments[...].astype(F32), jnp.where(down == 1, used, 0.0))
    block[rows:, :rows] = notes.astype(BF16)
    d_out[...] = (used_rows(info, rows) * cotangent[...].astype(F32)).astype(BF16)


def own_part_body(info, w_qkv, w_proj, groups, half):
    x = info[AT_X]
    for z in range(w_qkv.shape[1] // (4 * HALF)):
        at = pl.ds(pl.multiple_of(z * 4 * HALF + x * LANES, LANES), LANES)
        groups[:, z * LANES : (z + 1) * LANES] = w_qkv[:, at]
    half[...] = w_proj[:, : half.shape[1]]


def first_chunk_body(info, groups, got_qkv, left, lent, vectors, got_vectors, first):
    own_rows = left.shape[0]
    width = 2 * left.shape[1]
    x, c, y = info[AT_X], info[AT_C], info[AT_Y]
    qkv = 3 * width // 4
    low = low_half((own_rows, LANES))
    for core in range(2):
        rows = slice(core * own_rows, (core + 1) * own_rows)
        for pair in range(groups.shape[1] // (2 * LANES)):
            both = []
            for z in (2 * pair, 2 * pair + 1):
                at = pl.ds(pl.multiple_of(z * 4 * HALF + x * LANES, LANES), LANES)
                mine = groups[:, z * LANES : (z + 1) * LANES]
                both.append(jnp.where(c == core, mine, got_qkv[:, at]).astype(F32))
            first[rows, pair * LANES : (pair + 1) * LANES] = join(c, *both, low).astype(BF16)
    half = jnp.where(x == y, left[...], lent[:, width // 2 :])
    first[:own_rows, qkv:] = half[:, : width // 4]
    first[own_rows : 2 * own_rows, qkv:] = half[:, width // 4 :]
    mine = vectors[0:8, :].astype(F32)
    other = got_vectors[0:8, :].astype(F32)
    shifts = vectors[8:16, :].astype(F32)
    blank = jnp.zeros(mine.shape, F32)
    lower = jnp.concatenate([jnp.where(c == 0, mine, other), blank], axis=1)
    upper = jnp.concatenate([blank, jnp.where(c == 0, other, mine)], axis=1)
    small = lower + upper
    wide = jnp.concatenate([mine, blank], axis=1)
    heads = jnp.where(low_half((1, LANES)), wide[6:7], turn(wide)[7:8])
    shifts = jnp.concatenate([shifts, blank], axis=1)
    shifts = jnp.where(x == 0, shifts, jnp.concatenate([shifts[2:], shifts[:2]], axis=0))
    shift = jnp.where(low_half((1, LANES)), shifts[0:1], turn(shifts)[1:2])
    row = lax.broadcasted_iota(jnp.int32, small.shape, 0)
    small = jnp.where(row == 6, shift, jnp.where(row == 7, heads, small))
    first[2 * own_rows :, :] = jnp.zeros((SMALL_ROWS, width), BF16)
    first[2 * own_rows : 2 * own_rows + 8, :LANES] = small.astype(BF16)


def second_chunk_body(info, w_fc, got_fc, w_out, chunk, sems):
    own_rows = w_fc.shape[0]
    piece = w_out.shape[0] // 2
    x, c = info[AT_X], info[AT_C]
    source = pl.ds(pl.multiple_of(x * piece, piece), piece)
    copies = [(w_out.at[source, :], chunk.at[pl.ds(2 * own_rows, piece), :])]
    for p in range(w_fc.shape[1] // (4 * LANES)):
        source = pl.ds(pl.multiple_of(p * 4 * LANES + (2 * c + x) * LANES, LANES), LANES)
        lanes = pl.ds(p * LANES, LANES)
        for weight, core in ((w_fc, c), (got_fc, 1 - c)):
            row = pl.multiple_of(core * own_rows, own_rows)
            copies.append((weight.at[:, source], chunk.at[pl.ds(row, own_rows), lanes]))
    for copy in run_copies(copies, sems):
        copy.wait()


def run_copies(copies, sems):
    started = []
    for i, (source, target) in enumerate(copies):
        copy = pltpu.make_async_copy(source, target, sems.at[i])
        copy.start()
        started.append(copy)
    return started


def blocks_body(*refs):
    blocks = refs[:RANKS]
    units, masks = refs[RANKS:]
    rows = units.shape[0] // RANKS
    down = lax.broadcasted_iota(jnp.int32, (rows, rows), 0)
    across = lax.broadcasted_iota(jnp.int32, (rows, rows), 1)
    for b, block in enumerate(blocks):
        center, inverse = statistics(block[:rows, :].astype(F32))
        units[b * rows : (b + 1) * rows, :] = center * inverse
        notes = block[rows : rows + SMALL_ROWS, : 2 * LANES].astype(F32)
        seg_row, use_row = notes[0:1, :rows], notes[1:2, :rows]
        seg_column = jnp.sum(jnp.where(down == across, seg_row, 0.0), axis=1, keepdims=True)
        visible = (seg_column == seg_row) & (across <= down) & (use_row > 0)
        masks[b] = jnp.where(visible, 1.0, 0.0)


def attention_body(info, *refs):
    units, masks, chunks = refs[0], refs[1], refs[2 : 2 + ORIGINS]
    normed, qkv, probs, context, send_own, send_away, keep_own, keep_away = refs[2 + ORIGINS : 10 + ORIGINS]
    qkv_weight, proj_weight, smalls, sems = refs[10 + ORIGINS :]
    x = info[AT_X]
    width = normed.shape[1]
    rows = normed.shape[0] // RANKS
    chip_rows = chunks[0].shape[0] - SMALL_ROWS
    own_rows = chip_rows // 2
    cols = 3 * width // 4
    copies = []
    for i, chunk in enumerate(chunks):
        at = info[i]
        start = chunks[i - 1].shape[0] if i == ORIGINS - 1 else 0
        stop = start + chunk.shape[0]
        for part in range(2):
            top = part * own_rows
            if start <= top and top + own_rows <= stop:
                source = pl.ds(top - start, own_rows)
                copies.append(
                    (
                        chunk.at[source, pl.ds(0, cols)],
                        qkv_weight.at[pl.ds(pl.multiple_of(at * chip_rows + top, own_rows), own_rows), :],
                    )
                )
                side = lax.rem(at + x, 2) * (width // 2) + part * (width // 4)
                copies.append(
                    (
                        chunk.at[source, pl.ds(cols, width // 4)],
                        proj_weight.at[
                            pl.ds(pl.multiple_of(lax.div(at, 2) * own_rows, own_rows), own_rows),
                            pl.ds(pl.multiple_of(side, LANES), width // 4),
                        ],
                    )
                )
        if stop > chip_rows:
            copies.append(
                (
                    chunk.at[pl.ds(chip_rows - start, SMALL_ROWS), pl.ds(0, LANES)],
                    smalls.at[:, pl.ds(pl.multiple_of(at * LANES, LANES), LANES)],
                )
            )
    started = run_copies(copies, sems)

    for copy in started:
        copy.wait()
    gain = smalls[0:1, :].astype(F32)
    shift = smalls[1:2, :].astype(F32)
    normed[...] = (units[...] * gain + shift).astype(BF16)

    low_row = low_half((8, LANES))
    biases = jnp.broadcast_to(smalls[7:8, :].astype(F32), (8, width))
    query_shift, value_shift = [], []
    for pair in range(2):
        first, second = (
            jnp.where(
                x == 0,
                biases[:, z * 2 * LANES : z * 2 * LANES + LANES],
                biases[:, z * 2 * LANES + LANES : (z + 1) * 2 * LANES],
            )
            for z in (2 * pair, 2 * pair + 1)
        )
        query_shift.append(jnp.where(low_row, first, turn(second))[0:1])
        value_shift.append(jnp.where(low_row, turn(first), second)[0:1])
    third = width // 4
    for n in range(3):
        product = dot(normed[...], qkv_weight[:, n * third : (n + 1) * third])
        if n != 1:
            product = product + jnp.concatenate(value_shift if n else query_shift, axis=1)
        qkv[:, n * third : (n + 1) * third] = product.astype(BF16)

    scale = HALF ** (-0.5)
    low = low_half((1, LANES))
    keep_low = jnp.where(low, 1.0, 0.0).astype(BF16)
    keep_high = jnp.where(low, 0.0, 1.0).astype(BF16)

    def attend(b, carry):
        at = pl.ds(pl.multiple_of(b * rows, rows), rows)
        mask = masks[b] > 0.5
        for pair in range(2):
            lanes = pair * LANES
            queries = qkv[at, lanes : lanes + LANES]
            keys = qkv[at, third + lanes : third + lanes + LANES]
            values = qkv[at, 2 * third + lanes : 2 * third + lanes + LANES]
            outs = []
            for side, keep in enumerate((keep_low, keep_high)):
                scores = jnp.where(mask, scale * dot_cols(queries * keep, keys), -1e30)
                expo = jnp.exp(scores - jnp.max(scores, axis=-1, keepdims=True))
                share = (expo / jnp.sum(expo, axis=-1, keepdims=True)).astype(BF16)
                probs[b * 4 + 2 * pair + side] = share
                outs.append(dot(share, values))
            context[at, lanes : lanes + LANES] = jnp.where(low, outs[0], outs[1]).astype(BF16)
        return carry

    lax.fori_loop(0, RANKS, attend, 0, unroll=True)
    for n in range(4):
        columns = slice(n * third, (n + 1) * third)
        store_parts(dot(context[...], proj_weight[:, columns]), columns, rows, send_own, send_away, keep_own, keep_away)


def store_parts(product, columns, rows, send_own, send_away, keep_own, keep_away):
    keep_own[:, columns] = product[:rows]
    send_own[:, columns] = product[rows : 2 * rows].astype(BF16)
    keep_away[:, columns] = product[2 * rows : 3 * rows]
    send_away[:, columns] = product[3 * rows :].astype(BF16)


def total(keep, near, far):
    return keep[...] + near[...].astype(F32) + far.astype(F32)


def add_body(left, right, result):
    result[...] = add(left[...], right[...])


def message_body(keep_own, keep_away, near_own, near_away, message):
    message[0] = (keep_own[...] + near_own[...].astype(F32)).astype(BF16)
    message[1] = (keep_away[...] + near_away[...].astype(F32)).astype(BF16)


def second_norm_body(
    block, block_other, keep_own, keep_away, near_own, near_away, got, smalls, middle, normed
):
    rows = keep_own.shape[0]
    gain, shift = smalls[3:4, :].astype(F32), smalls[4:5, :].astype(F32)
    both = ((block, keep_own, near_own), (block_other, keep_away, near_away))
    for i, (tokens, keep, near) in enumerate(both):
        values = tokens[:rows, :].astype(F32) + smalls[2:3, :].astype(F32)
        values = values + total(keep, near, got[1 - i])
        middle[i] = values
        center, inverse = statistics(values)
        normed[i] = (center * inverse * gain + shift).astype(BF16)


def feed_body(info, normed, beside, *refs):
    d_outs = refs[:RANKS]
    chunks, smalls = refs[RANKS : RANKS + ORIGINS], refs[RANKS + ORIGINS]
    given, d_out, hidden, d_pre, send_own, send_away, keep_own, keep_away = refs[
        RANKS + ORIGINS + 1 : RANKS + ORIGINS + 9
    ]
    sums, out_weight, fc_weight, sems = refs[RANKS + ORIGINS + 9 :]
    rows = normed.shape[1]
    width = given.shape[1]
    chip_rows = chunks[0].shape[0] // 2
    copies = []
    for i, chunk in enumerate(chunks):
        at = pl.ds(pl.multiple_of(info[i] * chip_rows, chip_rows), chip_rows)
        if i != ORIGINS - 1:
            copies.append((chunk.at[pl.ds(0, chip_rows), :], fc_weight.at[at, :]))
        if i != ORIGINS - 2:
            start = 0 if i == ORIGINS - 1 else chip_rows
            copies.append((chunk.at[pl.ds(start, chip_rows), :], out_weight.at[at, :]))
    started = run_copies(copies, sems)
    for b in range(RANKS):
        given[b * rows : (b + 1) * rows, :] = (beside if b % 2 else normed)[b // 2]
        d_out[b * rows : (b + 1) * rows, :] = d_outs[b][...]
    for copy in started:
        copy.wait()
    tile = 2 * LANES
    root = (2.0 / jnp.pi) ** 0.5
    sums[...] = jnp.zeros(sums.shape, F32)

    def units(n, carry):
        columns = pl.ds(pl.multiple_of(n * tile, tile), tile)
        pre = dot(given[...], fc_weight[:, columns]) + smalls[6:7, columns].astype(F32)
        d_hidden = dot_cols(d_out[...], out_weight[columns, :])
        square = pre * pre
        bend = jnp.tanh(root * pre * (1.0 + 0.044715 * square))
        hidden[:, columns] = (0.5 * pre * (1.0 + bend)).astype(BF16)
        slope = 0.5 * (1.0 + bend) + 0.5 * pre * (1.0 - bend * bend) * root * (
            1.0 + 3.0 * 0.044715 * square
        )
        low = (d_hidden * slope).astype(BF16)
        d_pre[:, columns] = low
        sums[6:7, columns] = jnp.sum(low.astype(F32), axis=0, keepdims=True)
        return carry

    lax.fori_loop(0, width // tile, units, 0, unroll=True)
    for n in range(width // tile):
        columns = slice(n * tile, (n + 1) * tile)
        product = dot_cols(d_pre[...], fc_weight[columns, :])
        store_parts(product, columns, rows, send_own, send_away, keep_own, keep_away)


def feed_out_body(hidden, out_weight, send_own, send_away, keep_own, keep_away):
    rows = keep_own.shape[0]
    tile = 2 * LANES
    for n in range(out_weight.shape[1] // tile):
        columns = slice(n * tile, (n + 1) * tile)
        store_parts(dot(hidden[...], out_weight[:, columns]), columns, rows, send_own, send_away, keep_own, keep_away)


def mixed_body(info, middle, keep_own, near, away, smalls, mixed):
    values = middle[0] + total(keep_own, near, away[...]) + smalls[5:6, :].astype(F32)
    mixed[...] = (used_rows(info, keep_own.shape[0]) * values).astype(BF16)


def second_back_body(
    middle, d_top, d_other, keep_own, keep_away, near_own, near_away, got, smalls, d_middle, branch_own, branch_away, sums
):
    gain = smalls[3:4, :].astype(F32)
    both = ((d_top, keep_own, near_own), (d_other, keep_away, near_away))
    for i, (d_out, keep, near) in enumerate(both):
        d_values = total(keep, near, got[1 - i])
        center, inverse = statistics(middle[i])
        unit = center * inverse
        result = d_out[...].astype(F32) + norm_back(unit, inverse, d_values * gain)
        low = result.astype(BF16)
        (branch_own if i == 0 else branch_away)[...] = low
        if i == 0:
            d_middle[...] = result
            sums[...] = jnp.zeros(sums.shape, F32)
            sums[2:3, :] = jnp.sum(low.astype(F32), axis=0, keepdims=True)
            sums[3:4, :] = jnp.sum(d_values * unit, axis=0, keepdims=True)
            sums[4:5, :] = jnp.sum(d_values, axis=0, keepdims=True)
            sums[5:6, :] = jnp.sum(d_out[...].astype(F32), axis=0, keepdims=True)


def attention_back_body(info, *refs):
    branches, units, refs = refs[:RANKS], refs[RANKS], refs[RANKS + 1 :]
    qkv, probs, qkv_weight, proj_weight, sums_two, sums_fc = refs[:6]
    d_branch, d_qkv, send_own, send_away, keep_own, keep_away, sums, d_context = refs[6:]
    rows = branches[0].shape[0]
    width = d_branch.shape[1]
    third = width // 4
    x = info[AT_X]
    for b in range(RANKS):
        d_branch[b * rows : (b + 1) * rows, :] = branches[b][...]
    d_context[...] = dot_cols(d_branch[...], proj_weight[...]).astype(BF16)
    scale = HALF ** (-0.5)
    low = low_half((1, LANES))
    keep_low = jnp.where(low, 1.0, 0.0).astype(BF16)
    keep_high = jnp.where(low, 0.0, 1.0).astype(BF16)

    def attend(b, carry):
        at = pl.ds(pl.multiple_of(b * rows, rows), rows)
        for pair in range(2):
            lanes = pair * LANES
            queries = qkv[at, lanes : lanes + LANES]
            keys = qkv[at, third + lanes : third + lanes + LANES]
            values = qkv[at, 2 * third + lanes : 2 * third + lanes + LANES]
            d_out = d_context[at, lanes : lanes + LANES]
            results = []
            for side, keep in enumerate((keep_low, keep_high)):
                share = probs[b * 4 + 2 * pair + side]
                wide = share.astype(F32)
                d_values = dot_rows(share, d_out)
                d_probs = dot_cols(d_out * keep, values)
                d_scores = wide * (d_probs - jnp.sum(wide * d_probs, axis=-1, keepdims=True))
                d_scores = d_scores.astype(BF16)
                results.append(
                    (scale * dot(d_scores, keys), scale * dot_rows(d_scores, queries), d_values)
                )
            for n in range(3):
                merged = jnp.where(low, results[0][n], results[1][n]).astype(BF16)
                d_qkv[at, n * third + lanes : n * third + lanes + LANES] = merged
        return carry

    lax.fori_loop(0, RANKS, attend, 0, unroll=True)
    sums[0:8, :] = sums_two[...] + sums_fc[...]
    sums[8:, :] = jnp.zeros((SMALL_ROWS - 8, width), F32)
    for n in range(4):
        columns = slice(n * third, (n + 1) * third)
        product = dot_cols(d_qkv[...], qkv_weight[columns, :])
        store_parts(product, columns, rows, send_own, send_away, keep_own, keep_away)
        sums[1:2, columns] = jnp.sum(product, axis=0, keepdims=True)
        sums[0:1, columns] = jnp.sum(product * units[:, columns], axis=0, keepdims=True)
    low_row = low_half((8, LANES))
    for pair in range(2):
        lanes = pair * LANES
        d_queries = jnp.sum(d_qkv[:, lanes : lanes + LANES].astype(F32), axis=0, keepdims=True)
        d_values = jnp.sum(
            d_qkv[:, 2 * third + lanes : 2 * third + lanes + LANES].astype(F32), axis=0, keepdims=True
        )
        d_queries = jnp.broadcast_to(d_queries, (8, LANES))
        d_values = jnp.broadcast_to(d_values, (8, LANES))
        even = jnp.where(low_row, d_queries, turn(d_values))[0:1]
        odd = jnp.where(low_row, turn(d_queries), d_values)[0:1]
        for z, group in ((2 * pair, even), (2 * pair + 1, odd)):
            for y in range(2):
                start = (2 * z + y) * LANES
                sums[7:8, start : start + LANES] = jnp.where(x == y, group, 0.0)


def first_back_body(tokens, d_middle, keep_own, near, away, smalls, result):
    center, inverse = statistics(tokens[...].astype(F32))
    d_unit = total(keep_own, near, away[...]) * smalls[0:1, :].astype(F32)
    result[...] = d_middle[...] + norm_back(center * inverse, inverse, d_unit)


def second_term(info, index, grad_fc, grad_out):
    at = info[index]
    results = []
    for grad in (grad_fc, grad_out):
        chip_rows = grad.shape[0] * 2 // HEADS
        results.append(grad[pl.ds(pl.multiple_of(at * chip_rows, chip_rows), chip_rows), :])
    return results


def add(left, right):
    return (left.astype(F32) + right.astype(F32)).astype(BF16)


def second_far_body(info, grad_fc, grad_out, forth, back):
    forth[...], back[...] = second_term(info, ORIGINS - 1, grad_fc, grad_out)


def second_hop_body(step, info, got_forth, got_back, grad_fc, grad_out, forth, back):
    rows = forth.shape[0] // 2
    for target, got, index, part in ((forth, got_forth, 2 * step, 0), (back, got_back, 2 * step - 1, 1)):
        terms = second_term(info, index, grad_fc, grad_out)
        for i in range(2):
            where = slice(i * rows, (i + 1) * rows)
            if got.shape[0] == rows:
                target[where, :] = add(terms[i], got[...]) if i == part else terms[i]
            else:
                target[where, :] = add(terms[i], got[where, :])


def second_last_body(info, got_forth, got_back, grad_fc, grad_out, own):
    terms = second_term(info, 0, grad_fc, grad_out)
    rows = own.shape[0] // 2
    for i in range(2):
        where = slice(i * rows, (i + 1) * rows)
        values = got_forth[where, :].astype(F32) + got_back[where, :].astype(F32)
        own[where, :] = add(values, terms[i])


def first_term(info, index, grad_qkv, grad_proj, sums):
    at = info[index]
    chip_rows = grad_qkv.shape[0] * 2 // HEADS
    own_rows = chip_rows // 2
    quarter = grad_proj.shape[1] // 4
    side = lax.rem(at + info[AT_X], 2) * 2 * quarter
    head = pl.ds(pl.multiple_of(lax.div(at, 2) * own_rows, own_rows), own_rows)
    results = []
    for part in range(2):
        rows = pl.ds(pl.multiple_of(at * chip_rows + part * own_rows, own_rows), own_rows)
        lanes = pl.ds(pl.multiple_of(side + part * quarter, LANES), quarter)
        results.append((grad_qkv[rows, :], grad_proj[head, lanes]))
    small = sums[:, pl.ds(pl.multiple_of(at * LANES, LANES), LANES)].astype(BF16)
    return results, small


def put_first(target, row, values, got, got_row):
    at = 0
    rows = values[0].shape[0]
    for value in values:
        lanes = slice(at, at + value.shape[1])
        if got is not None:
            value = add(value, got[got_row : got_row + rows, lanes])
        target[row : row + rows, lanes] = value
        at += value.shape[1]


def first_far_body(info, grad_qkv, grad_proj, sums, forth, back):
    (upper, lower), small = first_term(info, ORIGINS - 1, grad_qkv, grad_proj, sums)
    own_rows = forth.shape[0]
    put_first(forth, 0, upper, None, 0)
    put_first(back, 0, lower, None, 0)
    back[own_rows:, :] = jnp.zeros((SMALL_ROWS, back.shape[1]), BF16)
    put_first(back, own_rows, (small,), None, 0)


def first_hop_body(step, info, got_forth, got_back, grad_qkv, grad_proj, sums, forth, back):
    own_rows = (forth.shape[0] - SMALL_ROWS) // 2
    for target, got, index in ((forth, got_forth, 2 * step), (back, got_back, 2 * step - 1)):
        terms, small = first_term(info, index, grad_qkv, grad_proj, sums)
        shift = 0
        if got.shape[0] == own_rows:
            came = (got, None, None)
        elif got.shape[0] == own_rows + SMALL_ROWS:
            came, shift = (None, got, got), own_rows
        else:
            came = (got, got, got)
        target[2 * own_rows :, :] = jnp.zeros((SMALL_ROWS, target.shape[1]), BF16)
        for i, values in enumerate((*terms, (small,))):
            put_first(target, i * own_rows, values, came[i], i * own_rows - shift)


def first_last_body(info, got_forth, got_back, grad_qkv, grad_proj, sums, own):
    own_rows = (own.shape[0] - SMALL_ROWS) // 2
    terms, small = first_term(info, 0, grad_qkv, grad_proj, sums)
    own[2 * own_rows :, :] = jnp.zeros((SMALL_ROWS, own.shape[1]), BF16)
    for i, values in enumerate((*terms, (small,))):
        at = 0
        rows = slice(i * own_rows, i * own_rows + values[0].shape[0])
        for value in values:
            lanes = slice(at, at + value.shape[1])
            came = got_forth[rows, lanes].astype(F32) + got_back[rows, lanes].astype(F32)
            own[rows, lanes] = add(came, value)
            at += value.shape[1]


def at_each_place(info, body):
    for x in range(2):
        for c in range(2):
            pl.when((info[AT_X] == x) & (info[AT_C] == c))(functools.partial(body, x, c))


def part_of(x, c, copy, core, own, near, other, cross):
    if copy == x:
        return own if core == c else near
    return other if core == c else cross


def hidden_grads_body(info, own, near, other, cross, grad_fc, grad_out):
    own_rows = grad_fc.shape[0]
    width = own.shape[1]
    piece = grad_out.shape[0] // 2

    def gather(x, c):
        rows = slice(c * own_rows, (c + 1) * own_rows)
        for copy in range(2):
            for core in range(2):
                part = part_of(x, c, copy, core, own, near, other, cross)
                for p in range(width // LANES):
                    at = p * 4 * LANES + core * 2 * LANES + copy * LANES
                    lanes = slice(p * LANES, (p + 1) * LANES)
                    grad_fc[:, at : at + LANES] = part[rows, lanes].astype(F32)
            half = own if x == copy else other
            grad_out[copy * piece : (copy + 1) * piece, :] = half[2 * own_rows :, :].astype(F32)

    at_each_place(info, gather)


def first_grads_body(info, own, near, other, cross, side, corner, grad_qkv, grad_proj, *small_outs):
    x, c, y = info[AT_X], info[AT_C], info[AT_Y]
    own_rows, width = grad_proj.shape
    qkv = 3 * width // 4
    quarter = width // 4
    low = low_half((own_rows, LANES))

    def gather(x, c):
        rows = slice(c * own_rows, (c + 1) * own_rows)
        for copy in range(2):
            first = part_of(x, c, copy, 0, own, near, other, cross)
            second = part_of(x, c, copy, 1, own, near, other, cross)
            for pair in range(qkv // LANES):
                lanes = slice(pair * LANES, (pair + 1) * LANES)
                one, two = first[rows, lanes].astype(F32), second[rows, lanes].astype(F32)
                at = pair * 8 * HALF + copy * LANES
                grad_qkv[:, at : at + LANES] = jnp.where(low, one, turn(two))
                at += 4 * HALF
                grad_qkv[:, at : at + LANES] = jnp.where(low, turn(one), two)

    at_each_place(info, gather)
    for part in range(2):
        block = slice(part * own_rows, (part + 1) * own_rows)
        left = jnp.where(x == y, own[block, qkv:], other[block, qkv:]).astype(F32)
        grad_proj[:, part * quarter : (part + 1) * quarter] = left
        right = jnp.where(x == y, side[block, :], corner[block, :]).astype(F32)
        grad_proj[:, 2 * quarter + part * quarter : 2 * quarter + (part + 1) * quarter] = right
    mine, beside, far, across = (
        ref[2 * own_rows :, :LANES].astype(F32) for ref in (own, near, other, cross)
    )
    summed = (mine + beside) + (far + across)
    summed = jnp.where(c == 0, summed, turn(summed))
    heads = jnp.where(x == y, mine, far)
    for i in range(6):
        small_outs[i][...] = summed[i : i + 1, :HALF]
    small_outs[6][0:1, :] = jnp.where(x == 0, mine, far)[6:7]
    small_outs[6][1:2, :] = jnp.where(x == 0, far, mine)[6:7]
    small_outs[7][...] = heads[7:8, :HALF]
    small_outs[8][...] = turn(heads)[7:8, :HALF]


def tie(*values):
    return lax.optimization_barrier(values)


def make_kernel_local(n_replica, n_shard):
    n_pos = n_shard // 2
    half = n_pos // 2

    def every(move):
        pairs = []
        for r in range(n_replica):
            for p in range(n_pos):
                for c in range(2):
                    to = move(r, p, c)
                    pairs.append((r * n_shard + p * 2 + c, to[0] * n_shard + to[1] * 2 + to[2]))
        return pairs

    ring = list(range(0, n_pos, 2)) + list(range(n_pos - 1, 0, -2))
    after = {p: ring[(i + 1) % n_pos] for i, p in enumerate(ring)}
    before = {p: ring[i - 1] for i, p in enumerate(ring)}

    def mover(move):
        pairs = every(move)
        return lambda v: lax.ppermute(v, MESH_AXES, pairs)

    to_core = mover(lambda r, p, c: (r, p, 1 - c))
    to_copy = mover(lambda r, p, c: (r ^ 1, p, c))
    to_next = mover(lambda r, p, c: (r, after[p], c))
    to_back = mover(lambda r, p, c: (r, before[p], c))
    to_side = mover(lambda r, p, c: (r, p ^ 1, c))
    to_corner = mover(lambda r, p, c: (r ^ 1, p ^ 1, c))

    def local(
        tokens,
        segments,
        counts,
        ln1_gain,
        ln1_bias,
        w_qkv,
        bias_query,
        bias_value,
        w_proj,
        bias_proj,
        ln2_gain,
        ln2_bias,
        w_fc,
        bias_fc,
        w_out,
        bias_out,
        cotangent,
    ):
        rows, width = tokens.shape
        own_rows = width // n_shard
        chip_rows = 2 * own_rows
        piece = w_out.shape[0] // 2
        units = n_pos * piece
        all_rows = RANKS * rows
        qkv_cols = 3 * width // 4
        first_shape = ((chip_rows + SMALL_ROWS, width), BF16)
        second_shape = ((chip_rows + piece, width), BF16)
        replica_at = lax.axis_index("replica")
        shard_at = lax.axis_index("shard")
        x, c, p = replica_at % 2, shard_at % 2, shard_at // 2
        place = jnp.where(p % 2 == 0, p // 2, n_pos - 1 - p // 2)

        def origin(index):
            index = index % n_pos
            return jnp.where(index < half, 2 * index, 2 * (n_pos - 1 - index) + 1)

        offsets = [0]
        for step in range(1, half):
            offsets += [-step, step]
        offsets += [half, half]
        info = jnp.stack(
            [origin(place + offset) for offset in offsets] + [x, c, p % 2, counts[0]]
        ).astype(jnp.int32)

        got_qkv, lent = to_core(w_qkv), to_side(w_proj)
        vectors = jnp.stack(
            [ln1_gain, ln1_bias, bias_proj, ln2_gain, ln2_bias, bias_out, bias_query, bias_value]
            + [bias_fc[i * own_rows : (i + 1) * own_rows] for i in range(4)]
            + [jnp.zeros((own_rows,), BF16)] * 4
        )
        got_vectors = to_core(vectors)
        groups, left = kernel_call(
            own_part_body,
            [SMEM_SPEC] + [VMEM_SPEC] * 2,
            [((own_rows, 3 * width // 2), BF16), ((own_rows, width // 2), BF16)],
        )(info, w_qkv, w_proj)
        block, d_top = kernel_call(
            tokens_body,
            [SMEM_SPEC] + [VMEM_SPEC] * 3,
            [((rows + SMALL_ROWS, width), BF16), ((rows, width), BF16)],
        )(info, tokens, segments.reshape(1, rows), cotangent)
        (first_chunk,) = kernel_call(
            first_chunk_body, [SMEM_SPEC] + [VMEM_SPEC] * 6, [first_shape], micros=2
        )(info, groups, got_qkv, left, lent, vectors, got_vectors)

        first_chunk, later_fc = tie(first_chunk, w_fc)
        forth, back = to_next(first_chunk), to_back(first_chunk)
        got_fc = to_core(later_fc)
        firsts = [first_chunk, forth, back]
        forth, back, block = tie(forth, back, block)
        block_other = to_copy(block)
        blocks = [block, to_core(block), block_other, to_core(block_other)]
        forth, back = to_next(forth), to_back(back)
        (second_chunk,) = kernel_call(
            second_chunk_body,
            [SMEM_SPEC] + [HBM_SPEC] * 3,
            [second_shape],
            [pltpu.SemaphoreType.DMA((1 + 2 * n_pos,))],
            micros=2,
        )(info, w_fc, got_fc, w_out)
        forth, back, second_chunk = tie(forth, back, second_chunk)
        seconds = [second_chunk]
        firsts += [forth, back]
        forth, back = to_next(forth), to_back(back)
        second_forth, second_back = to_next(second_chunk), to_back(second_chunk)
        firsts += [forth, back]
        unit, masks = kernel_call(
            blocks_body,
            [VMEM_SPEC] * RANKS,
            [((all_rows, width), F32), ((RANKS, rows, rows), F32)],
            micros=2,
        )(*blocks)
        unit, masks, forth, back = tie(unit, masks, forth, back)
        d_top, *firsts = tie(d_top, *firsts, to_next(forth[:own_rows]), to_back(back[own_rows:]))
        seconds += [second_forth, second_back]
        second_forth, second_back = to_next(second_forth), to_back(second_back)

        parts = [((rows, width), BF16)] * 2 + [((rows, width), F32)] * 2
        two_blocks = ((2, rows, width), BF16)
        d_other = to_copy(d_top)
        (
            normed, qkv, probs, context, send_own, send_away, keep_own, keep_away, qkv_weight, proj_weight, smalls
        ) = kernel_call(
            attention_body,
            [SMEM_SPEC] + [VMEM_SPEC] * 2 + [ANY_SPEC] * ORIGINS,
            [
                ((all_rows, width), BF16),
                ((all_rows, qkv_cols), BF16),
                ((4 * RANKS, rows, rows), BF16),
                ((all_rows, width // 4), BF16),
                *parts,
                ((width, qkv_cols), BF16),
                ((width // 4, width), BF16),
                ((SMALL_ROWS, width), BF16),
            ],
            [pltpu.SemaphoreType.DMA((5 * n_pos,))],
            micros=8,
        )(info, unit, masks, *firsts)
        send_own, send_away, d_top, d_other = tie(send_own, send_away, d_top, d_other)
        near_own, near_away = to_core(send_own), to_core(send_away)
        near_own, near_away, second_forth, second_back = tie(
            near_own, near_away, second_forth, second_back
        )

        def message(*parts):
            return kernel_call(message_body, [VMEM_SPEC] * 4, [two_blocks], micros=0)(*parts)[0]

        got = to_copy(message(keep_own, keep_away, near_own, near_away))
        seconds += [second_forth, second_back]
        second_forth, second_back = to_next(second_forth), to_back(second_back)
        d_outs = [d_top, to_core(d_top), d_other, to_core(d_other)]
        seconds += [second_forth, second_back]
        second_forth, second_back = second_forth[:chip_rows], second_back[chip_rows:]
        got, second_forth, second_back = tie(got, second_forth, second_back)
        seconds += [to_next(second_forth), to_back(second_back)]
        middle, normed_two = kernel_call(
            second_norm_body, [VMEM_SPEC] * 8, [((2, rows, width), F32), two_blocks], micros=2
        )(block, block_other, keep_own, keep_away, near_own, near_away, got, smalls)
        beside = to_core(normed_two)

        (
            given, d_out, hidden, d_pre, send_own, send_away, keep_own, keep_away, sums_fc, out_weight
        ) = kernel_call(
            feed_body,
            [SMEM_SPEC] + [VMEM_SPEC] * (2 + RANKS) + [ANY_SPEC] * ORIGINS + [VMEM_SPEC],
            [
                ((all_rows, width), BF16),
                ((all_rows, width), BF16),
                ((all_rows, units), BF16),
                ((all_rows, units), BF16),
                *parts,
                ((8, units), F32),
                ((units, width), BF16),
            ],
            [pltpu.VMEM((width, units), BF16), pltpu.SemaphoreType.DMA((2 * n_pos,))],
            micros=8,
        )(
            info, normed_two, beside, *d_outs, *seconds, smalls
        )

        near_own, near_away = to_core(send_own), to_core(send_away)
        mix_own, mix_away, mix_keep, mix_keep_away = kernel_call(
            feed_out_body, [VMEM_SPEC] * 2, parts, micros=2
        )(hidden, out_weight)
        near_own, near_away, given, d_out, hidden, d_pre, mix_own, mix_away = tie(
            near_own, near_away, given, d_out, hidden, d_pre, mix_own, mix_away
        )
        got = to_copy(message(keep_own, keep_away, near_own, near_away))
        grad_w_out = dot_rows(hidden, d_out).astype(BF16)
        grad_w_fc = dot_rows(given, d_pre).astype(BF16)
        far_forth, far_back = kernel_call(
            second_far_body,
            [SMEM_SPEC] + [VMEM_SPEC] * 2,
            [((chip_rows, width), BF16), ((piece, width), BF16)],
        )(info, grad_w_fc, grad_w_out)
        far_forth, far_back, mix_own, mix_away = tie(far_forth, far_back, mix_own, mix_away)
        far_forth, far_back = to_next(far_forth), to_back(far_back)
        mix_own, mix_away = to_core(mix_own), to_core(mix_away)

        def second_sums(step, got_forth, got_back):
            return kernel_call(
                functools.partial(second_hop_body, step),
                [SMEM_SPEC] + [VMEM_SPEC] * 4,
                [second_shape, second_shape],
                micros=3,
            )(info, got_forth, got_back, grad_w_fc, grad_w_out)

        second_forth, second_back = second_sums(half - 1, far_forth, far_back)
        got, second_forth, second_back, mix_own, mix_away = tie(
            got, second_forth, second_back, mix_own, mix_away
        )
        second_forth, second_back = to_next(second_forth), to_back(second_back)
        d_middle, branch_own, branch_away, sums_two = kernel_call(
            second_back_body,
            [VMEM_SPEC] * 9,
            [((rows, width), F32), ((rows, width), BF16), ((rows, width), BF16), ((8, width), F32)],
            micros=1,
        )(middle, d_top, d_other, keep_own, keep_away, near_own, near_away, got, smalls)
        branches = [branch_own, to_core(branch_own), branch_away, to_core(branch_away)]
        mix_away = to_copy(add(mix_keep_away, mix_away))

        d_branch, d_qkv, send_own, send_away, keep_own, keep_away, sums = kernel_call(
            attention_back_body,
            [SMEM_SPEC] + [VMEM_SPEC] * 11,
            [
                ((all_rows, width), BF16),
                ((all_rows, qkv_cols), BF16),
                *parts,
                ((SMALL_ROWS, width), F32),
            ],
            [pltpu.VMEM((all_rows, width // 4), BF16)],
            micros=1,
        )(info, *branches, unit, qkv, probs, qkv_weight, proj_weight, sums_two, sums_fc)
        grad_w_proj = dot_rows(context, d_branch).astype(BF16)
        grad_w_qkv = dot_rows(normed, d_qkv).astype(BF16)
        firsts = (grad_w_qkv, grad_w_proj, sums)
        forth, back = kernel_call(
            first_far_body,
            [SMEM_SPEC] + [VMEM_SPEC] * 3,
            [((own_rows, width), BF16), ((own_rows + SMALL_ROWS, width), BF16)],
        )(info, *firsts)
        forth, back, second_forth, second_back, mix_away = tie(
            forth, back, second_forth, second_back, mix_away
        )
        forth, back = to_next(forth), to_back(back)
        second_forth, second_back = second_sums(half - 2, second_forth, second_back)

        def first_sums(step, forth, back):
            return kernel_call(
                functools.partial(first_hop_body, step),
                [SMEM_SPEC] + [VMEM_SPEC] * 5,
                [first_shape, first_shape],
                micros=4,
            )(info, forth, back, *firsts)

        second_forth, second_back = to_next(second_forth), to_back(second_back)
        forth, back, send_own, send_away = tie(forth, back, send_own, send_away)
        near_away, near_own = to_core(send_away), to_core(send_own)
        near_away, near_own = tie(near_away, near_own)
        (away,) = kernel_call(
            add_body, [VMEM_SPEC] * 2, [((rows, width), BF16)], micros=1
        )(keep_away, near_away)
        forth, back = first_sums(3, forth, back)
        forth, back = to_next(forth), to_back(back)
        away = to_copy(away)
        second_forth, second_back, away = tie(second_forth, second_back, away)
        second_forth, second_back = second_sums(1, second_forth, second_back)
        second_forth, second_back = to_next(second_forth), to_back(second_back)
        (grad_tokens,) = kernel_call(first_back_body, [VMEM_SPEC] * 6, [((rows, width), F32)])(
            tokens, d_middle, keep_own, near_own, away, smalls
        )
        forth, back, grad_tokens = tie(forth, back, grad_tokens)
        forth, back = first_sums(2, forth, back)
        forth, back = to_next(forth), to_back(back)
        (mixed,) = kernel_call(mixed_body, [SMEM_SPEC] + [VMEM_SPEC] * 5, [((rows, width), BF16)])(
            info, middle, mix_keep, mix_own, mix_away, smalls
        )
        forth, back, second_forth, second_back, mixed = tie(
            forth, back, second_forth, second_back, mixed
        )
        (own_second,) = kernel_call(
            second_last_body, [SMEM_SPEC] + [VMEM_SPEC] * 4, [second_shape]
        )(info, second_forth, second_back, grad_w_fc, grad_w_out)
        near_second, other_second = to_core(own_second), to_copy(own_second)
        forth, back = first_sums(1, forth, back)
        forth, back = to_next(forth), to_back(back)
        forth, back, near_second, other_second = tie(forth, back, near_second, other_second)
        (own_first,) = kernel_call(
            first_last_body, [SMEM_SPEC] + [VMEM_SPEC] * 5, [first_shape]
        )(info, forth, back, *firsts)
        near_first, other_first = to_core(own_first), to_copy(own_first)
        own_proj = own_first[:chip_rows, qkv_cols:]
        given_side, given_far = to_side(own_proj), to_corner(own_proj)

        grad_w_fc, grad_w_out = kernel_call(
            hidden_grads_body,
            [SMEM_SPEC] + [VMEM_SPEC] * 4,
            [((own_rows, 4 * units), F32), ((2 * piece, width), F32)],
        )(info, own_second, near_second, other_second, to_core(other_second))

        other_first, given_side, given_far, grad_w_fc, grad_w_out = tie(
            other_first, given_side, given_far, grad_w_fc, grad_w_out
        )
        vector_shape = ((1, own_rows), F32)
        grad_w_qkv, grad_w_proj, *small = kernel_call(
            first_grads_body,
            [SMEM_SPEC] + [VMEM_SPEC] * 6,
            [((own_rows, 3 * width), F32), ((own_rows, width), F32)]
            + [vector_shape] * 6
            + [((2, piece), F32)]
            + [vector_shape] * 2,
        )(info, own_first, near_first, other_first, to_core(other_first), given_side, given_far)
        small = [value.reshape(-1) for value in small]
        return (
            mixed,
            grad_tokens,
            small[0],
            small[1],
            grad_w_qkv,
            small[7],
            small[8],
            grad_w_proj,
            small[2],
            small[3],
            small[4],
            grad_w_fc,
            small[6],
            grad_w_out,
            small[5],
        )

    return local


def solution(mesh):
    tokens_spec = P(MESH_AXES, None)
    slots_spec = P(MESH_AXES)
    rows_spec = P("shard", None)
    vector_spec = P("shard")
    in_specs = (
        tokens_spec,
        slots_spec,
        slots_spec,
        vector_spec,
        vector_spec,
        rows_spec,
        vector_spec,
        vector_spec,
        rows_spec,
        vector_spec,
        vector_spec,
        vector_spec,
        rows_spec,
        vector_spec,
        rows_spec,
        vector_spec,
        tokens_spec,
    )
    out_specs = (
        tokens_spec,
        tokens_spec,
        vector_spec,
        vector_spec,
        rows_spec,
        vector_spec,
        vector_spec,
        rows_spec,
        vector_spec,
        vector_spec,
        vector_spec,
        rows_spec,
        vector_spec,
        rows_spec,
        vector_spec,
    )
    n_replica, n_shard = mesh.shape["replica"], mesh.shape["shard"]
    make = make_kernel_local if (n_replica, n_shard) == (2, HEADS) else make_local
    local = make(n_replica, n_shard)
    return jax.shard_map(local, mesh=mesh, in_specs=in_specs, out_specs=out_specs, check_vma=False)
```
